32 devices in a mesh: ens: 2 (over x), gx: 16 (over z, y, core).
Axes of the slice: x: 2, y: 2, z: 4, core: 2. Of those that a mesh axis runs over, the one named last changes fastest.
Arguments:
- rhs_pressure: float32 [256, 128, 128], P(('ens', 'gx')), parts along dimension 0, may hold values from -6 to 6
- rhs_saturation: float32 [256, 128, 128], P(('ens', 'gx')), parts along dimension 0, may hold values from -6 to 6
- trans_x: float32 [256, 128, 128], P(('ens', 'gx')), parts along dimension 0, may hold values from 0.05 to 2
- trans_y: float32 [256, 128, 128], P(('ens', 'gx')), parts along dimension 0, may hold values from 0.05 to 2
- trans_z: float32 [256, 128, 128], P(('ens', 'gx')), parts along dimension 0, may hold values from 0.05 to 2
- coupling: float32 [256, 128, 128], P(('ens', 'gx')), parts along dimension 0, may hold values from -4 to 4
- upwind: float32 [256, 128, 128], P(('ens', 'gx')), parts along dimension 0, may hold values from -5 to 5
- storage: float32 [256, 128, 128], P(('ens', 'gx')), parts along dimension 0, may hold values from 0.3 to 3
- cross: float32 [256, 128, 128], P(('ens', 'gx')), parts along dimension 0, may hold values from -4 to 4
- accel: float32 [256, 128, 128], P(('ens', 'gx')), parts along dimension 0, may hold values from 1.15 to 3
- perf_cell: int32 [8192], P(('ens', 'gx')), parts along dimension 0, may hold values from 0 to 131071, as said below
- perf_well: int32 [8192], P(('ens', 'gx')), parts along dimension 0, may hold values from 0 to 511, as said below
- perf_index: float32 [8192], P(('ens', 'gx')), parts along dimension 0, may hold values from 0.1 to 2
- well_rhs: float32 [1024], P('ens'), parts along dimension 0, may hold values from -6 to 6
- well_slot: int32 [1024], P('ens'), parts along dimension 0, may hold values from 0 to 511, each once
Outputs:
- adj_pressure: float32 [256, 128, 128], P(('ens', 'gx')), parts along dimension 0
- adj_saturation: float32 [256, 128, 128], P(('ens', 'gx')), parts along dimension 0
- control_grad: float32 [1024], P(('ens', 'gx')), parts along dimension 0
The draws below stay inside these ranges and needn't reach their ends.
There are 2 independent parts, one for each index of `ens`. The reference program is written for one: setup_inputs(seed, part) draws one part's arguments, and reference() takes and returns one part's arrays. A program takes and returns all parts, laid end to end along the dimension named above; each array names one. Nothing has to cross between parts.
Inputs may be any that keep to these rules, and one draw needn't show every extreme that they name: `perf_cell`: flat index within the brick: x within the brick times 128 * 128, plus y * 128, plus z. Each device's perforations come in 32 groups of 8 consecutive entries, one well's path each: consecutive cells along z at one (x, y), or cells along x through the brick's planes. `perf_well`: group g of device j belongs to well j * 32 + g, or, for wells that run along x across a brick face, to well (j - 1) * 32 + g; a well has perforations on at most two neighbouring devices, and some wells have none. `well_slot`: each slot once; slots j * 32 to (j + 1) * 32 - 1 belong to device j of gx.
All inputs are finite; a program needn't handle non-finite values.
Results may differ from the reference program's by a relative error of at most 0.00002.
Values sent between devices are 32-bit elements; how exact they have to be, the bound alone decides.
No kernel may reach another device: no remote copies, remote signals or barrier semaphores. Data moves between devices by JAX's collectives and lax.ppermute only.
A program may use at most 64 MiB of HBM per device.

```python
import math
import jax
import jax.numpy as jnp
from jax import lax

CX = 8
NY = 128
NZ = 128
PERF_DEV = 256
WELL_DEV = 32
SWEEPS = 6
NX = 128
CELLS_DEV = 131072
PERFS = 4096
WELLS = 512


def well_layout(key):
    devices_all = PERFS // PERF_DEV
    run_len = PERF_DEV // WELL_DEV
    key_flag, key_x, key_y, key_z = jax.random.split(key, 4)
    flag = jax.random.randint(key_flag, (devices_all, WELL_DEV), 0, 4) == 0
    group = jnp.arange(WELL_DEV, dtype=jnp.int32)[None, :]
    device = jnp.arange(devices_all, dtype=jnp.int32)[:, None]
    edge_group = jnp.logical_or(group == 0, group == WELL_DEV - 1)
    flag = jnp.logical_and(flag, jnp.logical_not(edge_group))
    flag = jnp.logical_and(flag, device > 0)
    before = jnp.concatenate([jnp.zeros((1, WELL_DEV), bool), flag[:-1]], axis=0)
    carried = jnp.logical_and(flag, jnp.logical_not(before))
    after = jnp.concatenate([carried[1:], jnp.zeros((1, WELL_DEV), bool)], axis=0)
    along_x = jnp.logical_or(carried, after)
    x_base = jax.random.randint(key_x, (devices_all, WELL_DEV), 0, CX)
    y_base = jax.random.randint(key_y, (devices_all, WELL_DEV), 0, NY)
    z_base = jax.random.randint(key_z, (devices_all, WELL_DEV), 0, NZ - run_len + 1)
    step = jnp.arange(run_len, dtype=jnp.int32)[None, None, :]
    horiz = along_x[:, :, None]
    x_cell = jnp.where(horiz, step % CX, x_base[:, :, None])
    z_cell = jnp.where(horiz, z_base[:, :, None] + step // CX, z_base[:, :, None] + step)
    cell = (x_cell * (NY * NZ) + y_base[:, :, None] * NZ + z_cell).astype(jnp.int32)
    well = ((device - carried.astype(jnp.int32)) * WELL_DEV + group).astype(jnp.int32)
    well = jnp.broadcast_to(well[:, :, None], cell.shape)
    return (cell.reshape(-1), well.reshape(-1))


def draw_perf_cell(key, part):
    cell, well = well_layout(key)
    return cell


def draw_perf_well(key, part):
    cell, well = well_layout(key)
    return well


def level_of(stream_key, extent, cuts, low, top_value):
    factor_of, own = 1.0, jax.random.fold_in(stream_key, 6)
    for position, blocks in cuts:
        draws = jnp.exp(jax.random.uniform(jax.random.fold_in(own, position), (blocks,), jnp.float32, low / len(cuts), top_value / len(cuts)))
        factor_of = factor_of * jnp.repeat(draws, extent[position] // blocks).reshape([-1 if axis == position else 1 for axis in range(len(extent))])
    return factor_of


def noise(rng, extent, width, most, shards=(), held_as=jnp.bfloat16):
    values = jax.random.normal(rng, extent, jnp.float32) * width
    if len(shards) > 0:
        values = level_of(rng, extent, shards, -0.22, 0.18) * values
    return jnp.clip(values, min=-most, max=most).astype(held_as)


def setup_inputs(seed: int = 0, part: int = 0) -> dict:
    splits = jax.random.split(jax.random.key(seed), 16)
    own_keys = jax.random.split(jax.random.fold_in(splits[15], part), 16)
    return {
        "rhs_pressure": noise(own_keys[0], (NX, NY, NZ), 1.0, 6.0, ((0, 16),), jnp.float32),
        "rhs_saturation": noise(own_keys[1], (NX, NY, NZ), 1.0, 6.0, ((0, 16),), jnp.float32),
        "trans_x": jnp.clip(jnp.exp(math.log(2.0) - 3.6888794 * jax.random.uniform(own_keys[2], (NX, NY, NZ), jnp.float32) ** level_of(own_keys[2], (NX, NY, NZ), ((0, 16),), -0.2, 0.2)), 0.05, 2.0),
        "trans_y": jnp.clip(jnp.exp(math.log(2.0) - 3.6888794 * jax.random.uniform(own_keys[3], (NX, NY, NZ), jnp.float32) ** level_of(own_keys[3], (NX, NY, NZ), ((0, 16),), -0.2, 0.2)), 0.05, 2.0),
        "trans_z": jnp.clip(jnp.exp(math.log(2.0) - 3.6888794 * jax.random.uniform(own_keys[4], (NX, NY, NZ), jnp.float32) ** level_of(own_keys[4], (NX, NY, NZ), ((0, 16),), -0.2, 0.2)), 0.05, 2.0),
        "coupling": noise(own_keys[5], (NX, NY, NZ), 0.7, 4.0, ((0, 16),), jnp.float32),
        "upwind": noise(own_keys[6], (NX, NY, NZ), 1.0, 5.0, ((0, 16),), jnp.float32),
        "storage": jnp.clip(jnp.exp(math.log(3.0) - 2.3025851 * jax.random.uniform(own_keys[7], (NX, NY, NZ), jnp.float32) ** level_of(own_keys[7], (NX, NY, NZ), ((0, 16),), -0.2, 0.2)), 0.3, 3.0),
        "cross": noise(own_keys[8], (NX, NY, NZ), 0.7, 4.0, ((0, 16),), jnp.float32),
        "accel": jnp.clip(jnp.exp(math.log(3.0) - 0.9588504 * jax.random.uniform(own_keys[9], (NX, NY, NZ), jnp.float32) ** level_of(own_keys[9], (NX, NY, NZ), ((0, 16),), -0.2, 0.2)), 1.15, 3.0),
        "perf_cell": draw_perf_cell(jax.random.fold_in(jax.random.fold_in(splits[15], part), 71), part),
        "perf_well": draw_perf_well(jax.random.fold_in(jax.random.fold_in(splits[15], part), 71), part),
        "perf_index": jnp.clip(jnp.exp(math.log(2.0) - 2.9957323 * jax.random.uniform(own_keys[12], (PERFS,), jnp.float32) ** level_of(own_keys[12], (PERFS,), ((0, 16),), -0.2, 0.2)), 0.1, 2.0),
        "well_rhs": noise(own_keys[13], (WELLS,), 1.0, 6.0, (), jnp.float32),
        "well_slot": jax.random.permutation(own_keys[14], WELLS).astype(jnp.int32),
    }


def next_cell(field, axis):
    size = field.shape[axis]
    body_part = lax.slice_in_dim(field, 1, size, axis=axis)
    edge = jnp.zeros_like(lax.slice_in_dim(field, 0, 1, axis=axis))
    return jnp.concatenate([body_part, edge], axis=axis)


def prev_cell(field, axis):
    size = field.shape[axis]
    body_part = lax.slice_in_dim(field, 0, size - 1, axis=axis)
    edge = jnp.zeros_like(lax.slice_in_dim(field, 0, 1, axis=axis))
    return jnp.concatenate([edge, body_part], axis=axis)


def reference(rhs_pressure, rhs_saturation, trans_x, trans_y, trans_z, coupling, upwind, storage, cross, accel, perf_cell, perf_well, perf_index, well_rhs, well_slot):
    zero = jnp.float32(0.0)
    xpos = lax.broadcasted_iota(jnp.int32, trans_x.shape, 0)
    ypos = lax.broadcasted_iota(jnp.int32, trans_x.shape, 1)
    zpos = lax.broadcasted_iota(jnp.int32, trans_x.shape, 2)
    tx = jnp.where(xpos == NX - 1, zero, trans_x)
    ty = jnp.where(ypos == NY - 1, zero, trans_y)
    tz = jnp.where(zpos == NZ - 1, zero, trans_z)
    txl = prev_cell(tx, 0)
    tyl = prev_cell(ty, 1)
    tzl = prev_cell(tz, 2)
    tsum = tx + txl + ty + tyl + tz + tzl

    def nsum(field):
        total = tx * next_cell(field, 0) + txl * prev_cell(field, 0)
        total = total + ty * next_cell(field, 1) + tyl * prev_cell(field, 1)
        return total + tz * next_cell(field, 2) + tzl * prev_cell(field, 2)

    owner = (jnp.arange(PERFS, dtype=jnp.int32) // PERF_DEV).astype(jnp.int32)
    flat_cell = (owner * CELLS_DEV + perf_cell).astype(jnp.int32)
    ncell = NX * NY * NZ
    cwi = jnp.zeros((ncell,), jnp.float32).at[flat_cell].add(perf_index).reshape(trans_x.shape)
    wsum = jnp.zeros((WELLS,), jnp.float32).at[perf_well].add(perf_index)
    dp = accel * (tsum * (1.0 + jnp.abs(coupling)) + cwi)
    ds = accel * (jnp.abs(upwind) * tsum) + storage
    dw = 1.5 * wsum + 0.5

    def well_total(pressure):
        values = perf_index * pressure.reshape(-1)[flat_cell]
        return jnp.zeros((WELLS,), jnp.float32).at[perf_well].add(values)

    adj_p = jnp.zeros(trans_x.shape, jnp.float32)
    adj_s = jnp.zeros(trans_x.shape, jnp.float32)
    mu = jnp.zeros((WELLS,), jnp.float32)
    for sweep in range(SWEEPS):
        mu = (well_rhs + well_total(adj_p)) / dw
        inflow = jnp.zeros((ncell,), jnp.float32).at[flat_cell].add(perf_index * mu[perf_well]).reshape(trans_x.shape)
        sp = nsum(adj_p)
        ss = nsum(adj_s)
        adj_p = (rhs_pressure + sp + coupling * ss + inflow) / dp
        adj_s = (rhs_saturation + upwind * ss - cross * adj_p) / ds
    grad = mu * wsum - well_total(adj_p)
    control_grad = jnp.zeros((WELLS,), jnp.float32).at[well_slot].set(grad)
    return adj_p, adj_s, control_grad
```

```python
import functools

import jax
import jax.numpy as jnp
from jax import lax
from jax.experimental import pallas as pl
from jax.experimental.pallas import tpu as pltpu
from jax.sharding import PartitionSpec as P

SWEEPS = 6
SUB = 8
LANES = 128
F32 = jnp.float32


def vmem(rows):
    return pltpu.VMEM((rows, LANES), F32)


def placed(array, space):
    return array if space is pltpu.SMEM else pltpu.with_memory_space_constraint(array, space)


def spec(space):
    return pl.BlockSpec(memory_space=space)


def iota(shape, dim):
    return lax.broadcasted_iota(jnp.int32, shape, dim)


def lane_sum(block):
    return jnp.sum(block, axis=1, keepdims=True)


def spread(column, groups):
    return jnp.broadcast_to(column, (groups, LANES))


def row_of(column, groups):
    mine = iota((groups, LANES), 0) == iota((groups, LANES), 1)
    return jnp.sum(jnp.where(mine, column, 0.0), axis=0, keepdims=True)


def column_of(row, groups):
    mine = iota((groups, LANES), 0) == iota((groups, LANES), 1)
    return spread(lane_sum(jnp.where(mine, jnp.broadcast_to(row, (groups, LANES)), 0.0)), groups)


def well_block(part_own, part_before, groups):
    sub = iota((SUB, LANES), 0)
    own = jnp.broadcast_to(row_of(part_own, groups), (SUB, LANES))
    before = jnp.broadcast_to(row_of(part_before, groups), (SUB, LANES))
    return jnp.where(sub == 0, own, jnp.where(sub == 1, before, 0.0))


def group_rows(ref, groups, run):
    per_row = LANES // run
    return jnp.concatenate(
        [jnp.broadcast_to(ref[i : i + 1, :], (per_row, LANES)) for i in range(groups // per_row)], axis=0
    )


def first_kernel(sizes, tx_hbm, well_ref, index_ref, send_ref, wells_ref, sem):
    ny, groups, run = sizes.ny, sizes.groups, sizes.run
    copy = pltpu.make_async_copy(
        tx_hbm.at[pl.ds((sizes.planes - 1) * ny, ny)], send_ref.at[pl.ds(0, ny)], sem
    )
    copy.start()
    place = lax.axis_index("gx")
    shape = (groups, LANES)
    per_row = LANES // run
    local = iota(shape, 0) % per_row
    lane = iota(shape, 1)
    weights = jnp.where(lane // run == local, group_rows(index_ref, groups, run), 0.0)
    total = lane_sum(weights)
    first = jnp.where(lane == local * run, group_rows(well_ref, groups, run).astype(F32), 0.0)
    well = lane_sum(first)
    before = well < (place * groups).astype(F32)
    before = spread(jnp.where(before, 1.0, 0.0), groups)
    total = spread(total, groups)
    wells_ref[0:groups, :] = before
    wells_ref[groups : 2 * groups, :] = total
    send_ref[ny : ny + SUB, :] = well_block(total * (1.0 - before), total * before, groups)
    copy.wait()


def setup_kernel(
    sizes,
    cell_ref,
    index_ref,
    tx_hbm,
    ty_hbm,
    tz_hbm,
    accel_hbm,
    coupling_hbm,
    upwind_hbm,
    storage_hbm,
    rhs_p_hbm,
    rhs_s_hbm,
    cross_hbm,
    tx_ref,
    ty_ref,
    tyl_ref,
    tz_ref,
    tzl_ref,
    rp_ref,
    ip_ref,
    cc_ref,
    rs_ref,
    uu_ref,
    xx_ref,
    extra_ref,
    weight_ref,
    raw_ty,
    raw_storage,
    cwi_ref,
    sems,
):
    ny, planes, groups, run = sizes.ny, sizes.planes, sizes.groups, sizes.run
    rows = planes * ny
    moves = [
        (tx_hbm, tx_ref),
        (ty_hbm, raw_ty.at[pl.ds(SUB, rows)]),
        (tz_hbm, tz_ref),
        (accel_hbm, ip_ref),
        (coupling_hbm, cc_ref),
        (upwind_hbm, uu_ref),
        (storage_hbm, raw_storage),
        (rhs_p_hbm, rp_ref),
        (rhs_s_hbm, rs_ref),
        (cross_hbm, xx_ref),
    ]
    copies = [pltpu.make_async_copy(src, dst, sems.at[i]) for i, (src, dst) in enumerate(moves)]
    for copy in copies:
        copy.start()

    last = lax.axis_index("gx") == lax.axis_size("gx") - 1
    keep_last = jnp.where(last, 0.0, 1.0)
    zero = jnp.zeros((SUB, LANES), F32)

    @pl.loop(0, rows // SUB, unroll=8)
    def _(i):
        cwi_ref[pl.ds(pl.multiple_of(i * SUB, SUB), SUB), :] = zero

    spot = iota((SUB, LANES), 0) * LANES + iota((SUB, LANES), 1)
    for g in range(groups):
        weight = zero
        for k in range(g * run, (g + 1) * run):
            cell = cell_ref[k]
            at = (cell // (ny * LANES)) * LANES + cell % LANES
            weight = weight + jnp.where(spot == at, index_ref[k], 0.0)
        weight_ref[g * SUB : (g + 1) * SUB, :] = weight
        slab = pl.ds((cell_ref[g * run] // LANES) % ny, planes, ny)
        cwi_ref[slab, :] = cwi_ref[slab, :] + weight

    for copy in copies:
        copy.wait()

    lane = iota((SUB, LANES), 1)
    sub = iota((SUB, LANES), 0)

    @pl.loop(0, ny // SUB)
    def _(r):
        y0 = pl.multiple_of(r * SUB, SUB)
        ypos = sub + y0
        txl = None
        for x in range(planes):
            at = pl.ds(y0 + x * ny, SUB)
            tx = tx_ref[at, :]
            if x == planes - 1:
                tx = tx * keep_last
                tx_ref[at, :] = tx
            ty = jnp.where(ypos == ny - 1, 0.0, raw_ty[pl.ds(y0 + (x * ny + SUB), SUB), :])
            tyl = jnp.where(ypos == 0, 0.0, raw_ty[pl.ds(y0 + (x * ny + SUB - 1), SUB), :])
            tz = jnp.where(lane == LANES - 1, 0.0, tz_ref[at, :])
            tzl = pltpu.roll(tz, 1, 1)
            ty_ref[at, :] = ty
            tyl_ref[at, :] = tyl
            tz_ref[at, :] = tz
            tzl_ref[at, :] = tzl
            tsum = tx + ty + tyl + tz + tzl
            if x > 0:
                tsum = tsum + txl
            accel = ip_ref[at, :]
            coupling = cc_ref[at, :]
            upwind = uu_ref[at, :]
            to_p = accel * (1.0 + jnp.abs(coupling))
            to_s = accel * jnp.abs(upwind)
            dp = to_p * tsum + accel * cwi_ref[at, :]
            ds = to_s * tsum + raw_storage[at, :]
            if x == 0:
                here = pl.ds(y0, SUB)
                extra_ref[here, :] = to_p
                extra_ref[pl.ds(y0 + ny, SUB), :] = to_s
                extra_ref[pl.ds(y0 + 2 * ny, SUB), :] = ds
                ip_ref[at, :] = dp
            else:
                ip = 1.0 / dp
                is_ = 1.0 / ds
                ip_ref[at, :] = ip
                cc_ref[at, :] = coupling * ip
                rp_ref[at, :] = rp_ref[at, :] * ip
                rs_ref[at, :] = rs_ref[at, :] * is_
                uu_ref[at, :] = upwind * is_
                xx_ref[at, :] = xx_ref[at, :] * is_
            txl = tx


def add_wells(sizes, cell_ref, mu_ref, wp_ref, ws_ref, p_ref, s_ref):
    for g in range(sizes.groups):
        slab = pl.ds((cell_ref[g * sizes.run] // LANES) % sizes.ny + SUB, sizes.planes, sizes.ny)
        at = pl.ds(g * SUB, SUB)
        mu = mu_ref[g : g + 1, :]
        p_ref[slab, :] = p_ref[slab, :] + mu * wp_ref[at, :]
        s_ref[slab, :] = s_ref[slab, :] - mu * ws_ref[at, :]


def path_sums(sizes, cell_ref, weight_ref, p_ref, parts_ref):
    for g in range(sizes.groups):
        slab = pl.ds((cell_ref[g * sizes.run] // LANES) % sizes.ny + SUB, sizes.planes, sizes.ny)
        parts_ref[g : g + 1, :] = jnp.sum(
            p_ref[slab, :] * weight_ref[g * SUB : (g + 1) * SUB, :], axis=0, keepdims=True
        )
    return spread(lane_sum(parts_ref[...]), sizes.groups)


def pack(sizes, even, p_ref, s_ref, send_e, send_o, wells):
    ny = sizes.ny
    top = (sizes.planes - 1) * ny
    from_e = pl.multiple_of(jnp.where(even, top, 0) + SUB, SUB)
    from_o = pl.multiple_of(jnp.where(even, 0, top) + SUB, SUB)
    for r in range(0, ny, SUB):
        for send, start in ((send_e, from_e), (send_o, from_o)):
            send[r : r + SUB, :] = p_ref[pl.ds(start + r, SUB), :]
            send[ny + r : ny + r + SUB, :] = s_ref[pl.ds(start + r, SUB), :]
    send_e[2 * ny : 2 * ny + SUB, :] = wells
    send_o[2 * ny : 2 * ny + SUB, :] = wells


def own_lanes(ref, place, groups):
    shape = (groups, LANES)
    start = place * groups
    row = jnp.broadcast_to(ref[pl.ds(start // LANES, 1), :].astype(F32), shape)
    mine = iota(shape, 1) == iota(shape, 0) + start % LANES
    return spread(lane_sum(jnp.where(mine, row, 0.0)), groups)


BEFORE, RHS_OWN, INV_OWN, SUM_OWN, RHS, INV, SLOT_OWN, SLOT_BEFORE, TABLE = range(9)


def start_kernel(
    sizes,
    cell_ref,
    from_e,
    from_o,
    wells_ref,
    rhs_ref,
    slot_ref,
    rp_ref,
    ip_ref,
    cc_ref,
    rs_ref,
    uu_ref,
    xx_ref,
    extra_ref,
    weight_ref,
    p_ref,
    s_ref,
    edge_ref,
    wp_ref,
    ws_ref,
    table_ref,
    parts_out,
    send_e,
    send_o,
    mu_ref,
    parts_ref,
):
    ny, planes, groups = sizes.ny, sizes.planes, sizes.groups
    rows = planes * ny
    place = lax.axis_index("gx")
    even = place % 2 == 0

    tile_e, tile_o = from_e[ny : ny + SUB, :], from_o[ny : ny + SUB, :]
    low = jnp.where(even, tile_o, tile_e)
    high = jnp.where(even, tile_e, tile_o)
    before = wells_ref[0:groups, :]
    mine = wells_ref[groups : 2 * groups, :]
    is_before = before > 0.5
    sum_own = mine * (1.0 - before) + column_of(high[1:2, :], groups)
    sum_before = mine * before + column_of(low[0:1, :], groups)
    rhs_own = own_lanes(rhs_ref, place, groups)
    rhs_before = own_lanes(rhs_ref, jnp.maximum(place - 1, 0), groups)
    inv_own = 1.0 / (1.5 * sum_own + 0.5)
    inv_before = 1.0 / (1.5 * sum_before + 0.5)
    rhs = jnp.where(is_before, rhs_before, rhs_own)
    inv = jnp.where(is_before, inv_before, inv_own)
    entries = {
        BEFORE: before,
        RHS_OWN: rhs_own,
        INV_OWN: inv_own,
        SUM_OWN: sum_own,
        RHS: rhs,
        INV: inv,
        SLOT_OWN: own_lanes(slot_ref, place, groups),
        SLOT_BEFORE: own_lanes(slot_ref, jnp.maximum(place - 1, 0), groups),
    }
    for i, entry in entries.items():
        table_ref[i * groups : (i + 1) * groups, :] = entry
    mu_ref[...] = rhs * inv

    @pl.loop(0, ny // SUB)
    def _(r):
        y0 = pl.multiple_of(r * SUB, SUB)
        at = pl.ds(y0, SUB)
        txl = jnp.where(even, from_o[at, :], from_e[at, :])
        ip = 1.0 / (ip_ref[at, :] + extra_ref[at, :] * txl)
        is_ = 1.0 / (extra_ref[pl.ds(y0 + 2 * ny, SUB), :] + extra_ref[pl.ds(y0 + ny, SUB), :] * txl)
        rp, rs, xx = rp_ref[at, :] * ip, rs_ref[at, :] * is_, xx_ref[at, :] * is_
        plane = [txl, ip, cc_ref[at, :] * ip, rp, rs, uu_ref[at, :] * is_, xx]
        for i, value in enumerate(plane):
            edge_ref[pl.ds(y0 + i * ny, SUB), :] = value
        p_ref[pl.ds(y0 + SUB, SUB), :] = rp
        s_ref[pl.ds(y0 + SUB, SUB), :] = rs - xx * rp
        for x in range(1, planes):
            at = pl.ds(y0 + x * ny, SUB)
            to = pl.ds(y0 + (x * ny + SUB), SUB)
            rp = rp_ref[at, :]
            p_ref[to, :] = rp
            s_ref[to, :] = rs_ref[at, :] - xx_ref[at, :] * rp

    clear_ends(rows, p_ref, s_ref)
    sub = iota((SUB, LANES), 0)
    for g in range(groups):
        y = (cell_ref[g * sizes.run] // LANES) % ny
        at = pl.ds(g * SUB, SUB)
        slab = pl.ds(y, planes, ny)
        ip = jnp.where(sub == 0, edge_ref[pl.ds(y + ny, 1), :], ip_ref[slab, :])
        xx = jnp.where(sub == 0, edge_ref[pl.ds(y + 6 * ny, 1), :], xx_ref[slab, :])
        wp = weight_ref[at, :] * ip
        wp_ref[at, :] = wp
        ws_ref[at, :] = wp * xx
    add_wells(sizes, cell_ref, mu_ref, wp_ref, ws_ref, p_ref, s_ref)
    total = path_sums(sizes, cell_ref, weight_ref, p_ref, parts_ref)
    part_own, part_before = total * (1.0 - before), total * before
    parts_out[0:groups, :] = part_own
    parts_out[groups : 2 * groups, :] = part_before
    pack(sizes, even, p_ref, s_ref, send_e, send_o, well_block(part_own, part_before, groups))


def clear_ends(rows, *refs):
    zero = jnp.zeros((SUB, LANES), F32)
    for ref in refs:
        ref[0:SUB, :] = zero
        ref[rows + SUB : rows + 2 * SUB, :] = zero


def sweep_kernel(
    sizes,
    final,
    cell_ref,
    from_e,
    from_o,
    p_old,
    s_old,
    parts_in,
    tx_ref,
    ty_ref,
    tyl_ref,
    tz_ref,
    tzl_ref,
    rp_ref,
    ip_ref,
    cc_ref,
    rs_ref,
    uu_ref,
    xx_ref,
    edge_ref,
    weight_ref,
    wp_ref,
    ws_ref,
    table_ref,
    p_ref,
    s_ref,
    *rest,
):
    ny, planes, groups = sizes.ny, sizes.planes, sizes.groups
    rows = planes * ny
    if final:
        grads_ref, mu_ref, parts_ref = rest
    else:
        parts_out, send_e, send_o, mu_ref, parts_ref = rest
    place = lax.axis_index("gx")
    even = place % 2 == 0

    def table(i):
        return table_ref[i * groups : (i + 1) * groups, :]

    tile_e, tile_o = from_e[2 * ny : 2 * ny + SUB, :], from_o[2 * ny : 2 * ny + SUB, :]
    low = jnp.where(even, tile_o, tile_e)
    high = jnp.where(even, tile_e, tile_o)
    before = table(BEFORE)
    total_own = parts_in[0:groups, :] + column_of(high[1:2, :], groups)
    total_before = parts_in[groups : 2 * groups, :] + column_of(low[0:1, :], groups)
    mu_ref[...] = (table(RHS) + jnp.where(before > 0.5, total_before, total_own)) * table(INV)

    @pl.loop(0, ny // SUB)
    def _(r):
        y0 = pl.multiple_of(r * SUB, SUB)
        at = pl.ds(y0, SUB)
        at_s = pl.ds(y0 + ny, SUB)
        p_e, p_o, s_e, s_o = from_e[at, :], from_o[at, :], from_e[at_s, :], from_o[at_s, :]
        ps = [jnp.where(even, p_o, p_e)]
        ss = [jnp.where(even, s_o, s_e)]
        for x in range(planes):
            here = pl.ds(y0 + (x * ny + SUB), SUB)
            ps.append(p_old[here, :])
            ss.append(s_old[here, :])
        ps.append(jnp.where(even, p_e, p_o))
        ss.append(jnp.where(even, s_e, s_o))

        def edge(i):
            return edge_ref[pl.ds(y0 + i * ny, SUB), :]

        txl = edge(0)
        for x in range(planes):
            at = pl.ds(y0 + x * ny, SUB)
            up = pl.ds(y0 + (x * ny + SUB + 1), SUB)
            down = pl.ds(y0 + (x * ny + SUB - 1), SUB)
            tx, ty, tyl, tz, tzl = tx_ref[at, :], ty_ref[at, :], tyl_ref[at, :], tz_ref[at, :], tzl_ref[at, :]

            def neighbours(fields, old):
                mid = fields[x + 1]
                total = tx * fields[x + 2] + txl * fields[x]
                total = total + (ty * old[up, :] + tyl * old[down, :])
                return total + (tz * pltpu.roll(mid, LANES - 1, 1) + tzl * pltpu.roll(mid, 1, 1))

            sum_p = neighbours(ps, p_old)
            sum_s = neighbours(ss, s_old)
            if x == 0:
                ip, cc, rp, rs, uu, xx = [edge(i) for i in range(1, 7)]
            else:
                ip, cc, rp, rs, uu, xx = [ref[at, :] for ref in (ip_ref, cc_ref, rp_ref, rs_ref, uu_ref, xx_ref)]
            p = rp + ip * sum_p + cc * sum_s
            to = pl.ds(y0 + (x * ny + SUB), SUB)
            p_ref[to, :] = p
            s_ref[to, :] = rs + uu * sum_s - xx * p
            txl = tx

    add_wells(sizes, cell_ref, mu_ref, wp_ref, ws_ref, p_ref, s_ref)
    total = path_sums(sizes, cell_ref, weight_ref, p_ref, parts_ref)
    part_own, part_before = total * (1.0 - before), total * before
    clear_ends(rows, p_ref, s_ref)
    if not final:
        parts_out[0:groups, :] = part_own
        parts_out[groups : 2 * groups, :] = part_before
        pack(sizes, even, p_ref, s_ref, send_e, send_o, well_block(part_own, part_before, groups))
        return
    mu_own = (table(RHS_OWN) + total_own) * table(INV_OWN)
    grad_own = mu_own * table(SUM_OWN) - part_own
    grad_before = -part_before
    lane = iota((groups, LANES), 1)
    slot_own, slot_before = table(SLOT_OWN), table(SLOT_BEFORE)
    inside = lane < groups
    for d in range(sizes.devices):
        want = (lane + d * groups).astype(F32)
        own = jnp.where(inside & (slot_own == want), grad_own, 0.0)
        other = jnp.where(inside & (slot_before == want), grad_before, 0.0)
        row = jnp.sum(own + other, axis=0, keepdims=True)
        grads_ref[d * SUB : (d + 1) * SUB, :] = jnp.where(
            iota((SUB, LANES), 0) == 0, jnp.broadcast_to(row, (SUB, LANES)), 0.0
        )


class Sizes:
    def __init__(self, planes, ny, groups, run, devices):
        self.planes, self.ny, self.groups, self.run, self.devices = planes, ny, groups, run, devices


def body(
    rhs_pressure,
    rhs_saturation,
    trans_x,
    trans_y,
    trans_z,
    coupling,
    upwind,
    storage,
    cross,
    accel,
    perf_cell,
    perf_well,
    perf_index,
    well_rhs,
    well_slot,
):
    planes, ny, nz = trans_x.shape
    devices = lax.axis_size("gx")
    groups = well_rhs.shape[0] // devices
    run = perf_cell.shape[0] // groups
    sizes = Sizes(planes, ny, groups, run, devices)
    rows = planes * ny
    padded = rows + 2 * SUB
    SMEM, VMEM, HBM = pltpu.SMEM, pltpu.VMEM, pltpu.HBM

    def flat(array):
        return array.reshape(rows, nz)

    def lines(array):
        return array.reshape(-1, LANES)

    def call(kernel, args, spaces, outs, scratch, name, micros):
        return pl.pallas_call(
            functools.partial(kernel),
            in_specs=[spec(space) for space in spaces],
            out_specs=[spec(VMEM)] * len(outs),
            out_shape=outs,
            scratch_shapes=scratch,
            compiler_params=pltpu.CompilerParams(vmem_limit_bytes=16 * 1024 * 1024),
            cost_estimate=pl.CostEstimate(flops=int(micros * 4e6), bytes_accessed=int(micros * 3e6), transcendentals=0),
            name=name,
        )(*[placed(a, space) for a, space in zip(args, spaces)])

    pairs_e = [(i, i ^ 1) for i in range(devices) if i ^ 1 < devices]
    pairs_o = []
    for i in range(1, devices - 1, 2):
        pairs_o += [(i, i + 1), (i + 1, i)]

    def exchange(send_e, send_o):
        return lax.ppermute(send_e, "gx", pairs_e), lax.ppermute(send_o, "gx", pairs_o)

    tx = flat(trans_x)
    send, wells = call(
        functools.partial(first_kernel, sizes),
        [tx, lines(perf_well), lines(perf_index)],
        [HBM, VMEM, VMEM],
        [vmem(ny + SUB), vmem(2 * groups)],
        [pltpu.SemaphoreType.DMA],
        "first",
        1,
    )
    from_e, from_o = exchange(send, send)
    big = [tx] + [
        flat(a)
        for a in (trans_y, trans_z, accel, coupling, upwind, storage, rhs_pressure, rhs_saturation, cross)
    ]
    made = call(
        functools.partial(setup_kernel, sizes),
        [perf_cell, perf_index] + big,
        [SMEM, SMEM] + [HBM] * len(big),
        [vmem(rows)] * 11 + [vmem(3 * ny), vmem(groups * SUB)],
        [VMEM((padded, LANES), F32), VMEM((rows, LANES), F32), VMEM((rows, LANES), F32), pltpu.SemaphoreType.DMA((10,))],
        "setup",
        4,
    )
    coefficients, (extra, weight) = list(made[:11]), made[11:]
    scratch = [VMEM((groups, LANES), F32), VMEM((groups, LANES), F32)]
    fields = [vmem(padded), vmem(padded)]
    sends = [vmem(2 * groups), vmem(2 * ny + SUB), vmem(2 * ny + SUB)]
    p, s, edge, wp, ws, table, parts, send_e, send_o = call(
        functools.partial(start_kernel, sizes),
        [perf_cell, from_e, from_o, wells, lines(well_rhs), lines(well_slot)] + coefficients[5:] + [extra, weight],
        [SMEM] + [VMEM] * 13,
        fields + [vmem(7 * ny), vmem(groups * SUB), vmem(groups * SUB), vmem(TABLE * groups)] + sends,
        scratch,
        "start",
        1,
    )
    for sweep in range(1, SWEEPS):
        final = sweep == SWEEPS - 1
        from_e, from_o = exchange(send_e, send_o)
        args = [perf_cell, from_e, from_o, p, s, parts] + coefficients + [edge, weight, wp, ws, table]
        p, s, *rest = call(
            functools.partial(sweep_kernel, sizes, final),
            args,
            [SMEM] + [VMEM] * (len(args) - 1),
            fields + ([vmem(devices * SUB)] if final else sends),
            scratch,
            "sweep",
            1,
        )
        if not final:
            parts, send_e, send_o = rest
    grads = lax.all_to_all(rest[0].reshape(devices, SUB, LANES), "gx", 0, 0)
    control = jnp.sum(grads, axis=(0, 1))[:groups]
    shape = trans_x.shape
    return p[SUB : SUB + rows].reshape(shape), s[SUB : SUB + rows].reshape(shape), control


def solution(mesh):
    grid = P(("ens", "gx"), None, None)
    line = P(("ens", "gx"))
    return jax.shard_map(
        body,
        mesh=mesh,
        in_specs=(grid,) * 10 + (line,) * 3 + (P("ens"), P("ens")),
        out_specs=(grid, grid, line),
        check_vma=False,
    )
```

```python
import functools

import jax
import jax.numpy as jnp
from jax import lax
from jax.experimental import pallas as pl
from jax.experimental.pallas import tpu as pltpu
from jax.sharding import PartitionSpec as P

SWEEPS = 6
SUB = 8
LANES = 128
F32 = jnp.float32


def vmem(rows):
    return pltpu.VMEM((rows, LANES), F32)


def placed(array, space):
    return array if space is pltpu.SMEM else pltpu.with_memory_space_constraint(array, space)


def spec(space):
    return pl.BlockSpec(memory_space=space)


def iota(shape, dim):
    return lax.broadcasted_iota(jnp.int32, shape, dim)


def lane_sum(block):
    return jnp.sum(block, axis=1, keepdims=True)


def spread(column, groups):
    return jnp.broadcast_to(column, (groups, LANES))


def row_of(column, groups):
    mine = iota((groups, LANES), 0) == iota((groups, LANES), 1)
    return jnp.sum(jnp.where(mine, column, 0.0), axis=0, keepdims=True)


def column_of(row, groups):
    mine = iota((groups, LANES), 0) == iota((groups, LANES), 1)
    return spread(lane_sum(jnp.where(mine, jnp.broadcast_to(row, (groups, LANES)), 0.0)), groups)


def well_block(part_own, part_before, groups):
    sub = iota((SUB, LANES), 0)
    own = jnp.broadcast_to(row_of(part_own, groups), (SUB, LANES))
    before = jnp.broadcast_to(row_of(part_before, groups), (SUB, LANES))
    return jnp.where(sub == 0, own, jnp.where(sub == 1, before, 0.0))


def group_rows(ref, groups, run):
    per_row = LANES // run
    return jnp.concatenate(
        [jnp.broadcast_to(ref[i : i + 1, :], (per_row, LANES)) for i in range(groups // per_row)], axis=0
    )


def first_kernel(sizes, tx_hbm, well_hbm, index_hbm, send_ref, wells_ref, well_ref, index_ref, sems):
    ny, groups, run = sizes.ny, sizes.groups, sizes.run
    plane = pltpu.make_async_copy(
        tx_hbm.at[pl.ds((sizes.planes - 1) * ny, ny)], send_ref.at[pl.ds(0, ny)], sems.at[0]
    )
    get_well = pltpu.make_async_copy(well_hbm, well_ref, sems.at[1])
    get_index = pltpu.make_async_copy(index_hbm, index_ref, sems.at[2])
    for copy in (get_well, get_index, plane):
        copy.start()
    place = lax.axis_index("gx")
    shape = (groups, LANES)
    per_row = LANES // run
    local = iota(shape, 0) % per_row
    lane = iota(shape, 1)
    get_well.wait()
    get_index.wait()
    weights = jnp.where(lane // run == local, group_rows(index_ref, groups, run), 0.0)
    total = lane_sum(weights)
    first = jnp.where(lane == local * run, group_rows(well_ref, groups, run).astype(F32), 0.0)
    well = lane_sum(first)
    before = well < (place * groups).astype(F32)
    before = spread(jnp.where(before, 1.0, 0.0), groups)
    total = spread(total, groups)
    wells_ref[0:groups, :] = before
    wells_ref[groups : 2 * groups, :] = total
    send_ref[ny : ny + SUB, :] = well_block(total * (1.0 - before), total * before, groups)
    plane.wait()


def setup_kernel(
    sizes,
    cell_ref,
    index_hbm,
    tx_hbm,
    ty_hbm,
    tz_hbm,
    accel_hbm,
    coupling_hbm,
    upwind_hbm,
    storage_hbm,
    rhs_p_hbm,
    rhs_s_hbm,
    cross_hbm,
    tx_ref,
    ty_ref,
    tyl_ref,
    tz_ref,
    tzl_ref,
    rp_ref,
    ip_ref,
    cc_ref,
    rs_ref,
    uu_ref,
    xx_ref,
    extra_ref,
    weight_ref,
    raw_ty,
    raw_storage,
    cwi_ref,
    index_ref,
    sems,
    index_sem,
):
    ny, planes, groups, run = sizes.ny, sizes.planes, sizes.groups, sizes.run
    rows = planes * ny
    moves = [
        (tx_hbm, tx_ref),
        (ty_hbm, raw_ty.at[pl.ds(SUB, rows)]),
        (tz_hbm, tz_ref),
        (accel_hbm, ip_ref),
        (coupling_hbm, cc_ref),
        (upwind_hbm, uu_ref),
        (storage_hbm, raw_storage),
        (rhs_p_hbm, rp_ref),
        (rhs_s_hbm, rs_ref),
        (cross_hbm, xx_ref),
    ]
    copies = [pltpu.make_async_copy(src, dst, sems.at[i]) for i, (src, dst) in enumerate(moves)]
    fetch = pltpu.make_async_copy(index_hbm, index_ref, index_sem)
    fetch.start()
    for copy in copies:
        copy.start()

    last = lax.axis_index("gx") == lax.axis_size("gx") - 1
    keep_last = jnp.where(last, 0.0, 1.0)
    zero = jnp.zeros((SUB, LANES), F32)

    @pl.loop(0, rows // SUB, unroll=8)
    def _(i):
        cwi_ref[pl.ds(pl.multiple_of(i * SUB, SUB), SUB), :] = zero

    fetch.wait()
    spot = iota((SUB, LANES), 0) * LANES + iota((SUB, LANES), 1)
    for g in range(groups):
        weight = zero
        for k in range(g * run, (g + 1) * run):
            cell = cell_ref[k]
            at = (cell // (ny * LANES)) * LANES + cell % LANES
            weight = weight + jnp.where(spot == at, index_ref[k], 0.0)
        weight_ref[g * SUB : (g + 1) * SUB, :] = weight
        slab = pl.ds((cell_ref[g * run] // LANES) % ny, planes, ny)
        cwi_ref[slab, :] = cwi_ref[slab, :] + weight

    for copy in copies:
        copy.wait()

    lane = iota((SUB, LANES), 1)
    sub = iota((SUB, LANES), 0)

    @pl.loop(0, ny // SUB)
    def _(r):
        y0 = pl.multiple_of(r * SUB, SUB)
        ypos = sub + y0
        txl = None
        for x in range(planes):
            at = pl.ds(y0 + x * ny, SUB)
            tx = tx_ref[at, :]
            if x == planes - 1:
                tx = tx * keep_last
                tx_ref[at, :] = tx
            ty = jnp.where(ypos == ny - 1, 0.0, raw_ty[pl.ds(y0 + (x * ny + SUB), SUB), :])
            tyl = jnp.where(ypos == 0, 0.0, raw_ty[pl.ds(y0 + (x * ny + SUB - 1), SUB), :])
            tz = jnp.where(lane == LANES - 1, 0.0, tz_ref[at, :])
            tzl = pltpu.roll(tz, 1, 1)
            ty_ref[at, :] = ty
            tyl_ref[at, :] = tyl
            tz_ref[at, :] = tz
            tzl_ref[at, :] = tzl
            tsum = tx + ty + tyl + tz + tzl
            if x > 0:
                tsum = tsum + txl
            accel = ip_ref[at, :]
            coupling = cc_ref[at, :]
            upwind = uu_ref[at, :]
            to_p = accel * (1.0 + jnp.abs(coupling))
            to_s = accel * jnp.abs(upwind)
            dp = to_p * tsum + accel * cwi_ref[at, :]
            ds = to_s * tsum + raw_storage[at, :]
            if x == 0:
                here = pl.ds(y0, SUB)
                extra_ref[here, :] = to_p
                extra_ref[pl.ds(y0 + ny, SUB), :] = to_s
                extra_ref[pl.ds(y0 + 2 * ny, SUB), :] = ds
                ip_ref[at, :] = dp
            else:
                ip = 1.0 / dp
                is_ = 1.0 / ds
                ip_ref[at, :] = ip
                cc_ref[at, :] = coupling * ip
                rp_ref[at, :] = rp_ref[at, :] * ip
                rs_ref[at, :] = rs_ref[at, :] * is_
                uu_ref[at, :] = upwind * is_
                xx_ref[at, :] = xx_ref[at, :] * is_
            txl = tx


def own_lanes(ref, place, groups):
    shape = (groups, LANES)
    start = place * groups
    row = jnp.broadcast_to(ref[pl.ds(start // LANES, 1), :].astype(F32), shape)
    mine = iota(shape, 1) == iota(shape, 0) + start % LANES
    return spread(lane_sum(jnp.where(mine, row, 0.0)), groups)


def clear_ends(rows, *refs):
    zero = jnp.zeros((SUB, LANES), F32)
    for ref in refs:
        ref[0:SUB, :] = zero
        ref[rows + SUB : rows + 2 * SUB, :] = zero


def path_y(sizes, cell_ref, g):
    return (cell_ref[g * sizes.run] // LANES) % sizes.ny


def slab_of(sizes, cell_ref, g, pad):
    return pl.ds(path_y(sizes, cell_ref, g) + pad, sizes.planes, sizes.ny)


def add_wells(sizes, cell_ref, mu_ref, wp_ref, ws_ref, p_ref, s_ref, pad):
    for g in range(sizes.groups):
        slab = slab_of(sizes, cell_ref, g, pad)
        at = pl.ds(g * SUB, SUB)
        mu = mu_ref[g : g + 1, :]
        p_ref[slab, :] = p_ref[slab, :] + mu * wp_ref[at, :]
        s_ref[slab, :] = s_ref[slab, :] - mu * ws_ref[at, :]


def add_wells_to_plane(sizes, cell_ref, mu_ref, wp_ref, ws_ref, x, send_ref):
    for g in range(sizes.groups):
        y = path_y(sizes, cell_ref, g)
        in_p, in_s, at = pl.ds(y, 1), pl.ds(y + sizes.ny, 1), pl.ds(x + g * SUB, 1)
        mu = mu_ref[g : g + 1, :]
        send_ref[in_p, :] = send_ref[in_p, :] + mu * wp_ref[at, :]
        send_ref[in_s, :] = send_ref[in_s, :] - mu * ws_ref[at, :]


def path_rows(sizes, cell_ref, weight_ref, p_ref, rows_ref):
    for g in range(sizes.groups):
        slab = slab_of(sizes, cell_ref, g, SUB)
        at = pl.ds(g * SUB, SUB)
        rows_ref[g : g + 1, :] = jnp.sum(p_ref[slab, :] * weight_ref[at, :], axis=0, keepdims=True)


def facing(sizes, even):
    last = sizes.planes - 1
    return jnp.where(even, 0, last), jnp.where(even, last, 0)


def finish_plane(sizes, x, p_ref, s_ref, halo_ref, plane_ref, send_ref):
    ny = sizes.ny
    start = pl.multiple_of(x * ny + SUB, SUB)
    for r in range(0, ny, SUB):
        at = slice(r, r + SUB)
        at_s = slice(ny + r, ny + r + SUB)
        p, s = p_ref[pl.ds(start + r, SUB), :], s_ref[pl.ds(start + r, SUB), :]
        if halo_ref is not None:
            hp, hs = halo_ref[at, :], halo_ref[at_s, :]
            a, b, c, xx = [plane_ref[i * ny + r : i * ny + r + SUB, :] for i in range(4)]
            change = a * hp + b * hs
            p = p + change
            s = s + c * hs - xx * change
        send_ref[at, :] = p
        send_ref[at_s, :] = s


BEFORE, RHS_OWN, INV_OWN, SUM_OWN, RHS, INV, SLOT_OWN, SLOT_BEFORE, TABLE = range(9)


def shared_cells(sizes, cell_ref, weight_ref, wp_ref, out_ref):
    groups = sizes.groups
    shape = (groups, LANES)
    sub, lane = iota(shape, 0), iota(shape, 1)
    y_row = jnp.full(shape, -1, jnp.int32)
    y_col = y_row
    for g in range(groups):
        y = path_y(sizes, cell_ref, g)
        y_row = jnp.where(lane == g, y, y_row)
        y_col = jnp.where(sub == g, y, y_col)
    total = jnp.zeros(shape, F32)
    empty = jnp.zeros((LANES - groups, LANES), F32)
    for x in range(sizes.planes):
        at = pl.ds(x, groups, SUB)
        other = jnp.concatenate([wp_ref[at, :], empty], axis=0)
        total = total + lax.dot_general(
            weight_ref[at, :], other, (((1,), (1,)), ((), ())),
            precision=lax.Precision.HIGHEST, preferred_element_type=F32,
        )
    out_ref[...] = jnp.where(y_row == y_col, total, 0.0)


def start_kernel(
    sizes,
    cell_ref,
    from_o,
    from_e,
    wells_ref,
    rhs_hbm,
    slot_hbm,
    tx_ref,
    rp_ref,
    ip_ref,
    cc_ref,
    rs_ref,
    uu_ref,
    xx_ref,
    extra_ref,
    weight_ref,
    p_ref,
    s_ref,
    edge_ref,
    plane_e,
    plane_o,
    wp_ref,
    ws_ref,
    shared_ref,
    table_ref,
    mu_ref,
    parts_out,
    send_o,
    rows_ref,
    rhs_ref,
    slot_ref,
    sems,
):
    ny, planes, groups = sizes.ny, sizes.planes, sizes.groups
    rows = planes * ny
    place = lax.axis_index("gx")
    even = place % 2 == 0
    x_o, _ = facing(sizes, even)
    fetches = [
        pltpu.make_async_copy(rhs_hbm, rhs_ref, sems.at[0]),
        pltpu.make_async_copy(slot_hbm, slot_ref, sems.at[1]),
    ]
    for fetch in fetches:
        fetch.start()

    @pl.loop(0, ny // SUB)
    def _(r):
        y0 = pl.multiple_of(r * SUB, SUB)
        at = pl.ds(y0, SUB)
        txl = jnp.where(even, from_o[at, :], from_e[at, :])
        ip = 1.0 / (ip_ref[at, :] + extra_ref[at, :] * txl)
        is_ = 1.0 / (extra_ref[pl.ds(y0 + 2 * ny, SUB), :] + extra_ref[pl.ds(y0 + ny, SUB), :] * txl)
        cc, uu = cc_ref[at, :] * ip, uu_ref[at, :] * is_
        rp, rs, xx = rp_ref[at, :] * ip, rs_ref[at, :] * is_, xx_ref[at, :] * is_
        for i, value in enumerate([ip, cc, rp, rs, uu, xx]):
            edge_ref[pl.ds(y0 + i * ny, SUB), :] = value
        end = pl.ds(y0 + (planes - 1) * ny, SUB)
        tx = tx_ref[end, :]
        low = [ip * txl, cc * txl, uu * txl, xx]
        high = [ip_ref[end, :] * tx, cc_ref[end, :] * tx, uu_ref[end, :] * tx, xx_ref[end, :]]
        for i in range(4):
            to = pl.ds(y0 + i * ny, SUB)
            plane_o[to, :] = jnp.where(even, low[i], high[i])
            plane_e[to, :] = jnp.where(even, high[i], low[i])
        p_ref[pl.ds(y0 + SUB, SUB), :] = rp
        s_ref[pl.ds(y0 + SUB, SUB), :] = rs - xx * rp
        for x in range(1, planes):
            at = pl.ds(y0 + x * ny, SUB)
            to = pl.ds(y0 + (x * ny + SUB), SUB)
            rp = rp_ref[at, :]
            p_ref[to, :] = rp
            s_ref[to, :] = rs_ref[at, :] - xx_ref[at, :] * rp

    clear_ends(rows, p_ref, s_ref)
    sub = iota((SUB, LANES), 0)
    for g in range(groups):
        y = path_y(sizes, cell_ref, g)
        at = pl.ds(g * SUB, SUB)
        slab = pl.ds(y, planes, ny)
        ip = jnp.where(sub == 0, edge_ref[pl.ds(y, 1), :], ip_ref[slab, :])
        xx = jnp.where(sub == 0, edge_ref[pl.ds(y + 5 * ny, 1), :], xx_ref[slab, :])
        wp = weight_ref[at, :] * ip
        wp_ref[at, :] = wp
        ws_ref[at, :] = wp * xx
    shared_cells(sizes, cell_ref, weight_ref, wp_ref, shared_ref)

    tile_e, tile_o = from_e[ny : ny + SUB, :], from_o[ny : ny + SUB, :]
    low = jnp.where(even, tile_o, tile_e)
    high = jnp.where(even, tile_e, tile_o)
    before = wells_ref[0:groups, :]
    mine = wells_ref[groups : 2 * groups, :]
    is_before = before > 0.5
    sum_own = mine * (1.0 - before) + column_of(high[1:2, :], groups)
    sum_before = mine * before + column_of(low[0:1, :], groups)
    for fetch in fetches:
        fetch.wait()
    rhs_own = own_lanes(rhs_ref, place, groups)
    rhs_before = own_lanes(rhs_ref, jnp.maximum(place - 1, 0), groups)
    inv_own = 1.0 / (1.5 * sum_own + 0.5)
    inv_before = 1.0 / (1.5 * sum_before + 0.5)
    rhs = jnp.where(is_before, rhs_before, rhs_own)
    inv = jnp.where(is_before, inv_before, inv_own)
    entries = {
        BEFORE: before,
        RHS_OWN: rhs_own,
        INV_OWN: inv_own,
        SUM_OWN: sum_own,
        RHS: rhs,
        INV: inv,
        SLOT_OWN: own_lanes(slot_ref, place, groups),
        SLOT_BEFORE: own_lanes(slot_ref, jnp.maximum(place - 1, 0), groups),
    }
    for i, entry in entries.items():
        table_ref[i * groups : (i + 1) * groups, :] = entry
    mu = rhs * inv
    mu_ref[...] = mu

    finish_plane(sizes, x_o, p_ref, s_ref, None, None, send_o)
    add_wells_to_plane(sizes, cell_ref, mu_ref, wp_ref, ws_ref, x_o, send_o)
    path_rows(sizes, cell_ref, weight_ref, p_ref, rows_ref)
    put_sums(sizes, before, rows_ref[...] + shared_ref[...] * row_of(mu, groups), parts_out, send_o)


def put_sums(sizes, before, by_lane, parts_out, send_o):
    ny, groups = sizes.ny, sizes.groups
    total = spread(lane_sum(by_lane), groups)
    part_own, part_before = total * (1.0 - before), total * before
    parts_out[0:groups, :] = part_own
    parts_out[groups : 2 * groups, :] = part_before
    send_o[2 * ny : 2 * ny + SUB, :] = well_block(part_own, part_before, groups)
    return part_own, part_before


def finish_core_plane(sizes, cell_ref, p_ref, s_ref, mu_ref, wp_ref, ws_ref, send_o, halo, plane_e, send_e):
    even = lax.axis_index("gx") % 2 == 0
    _, x_e = facing(sizes, even)
    finish_plane(sizes, x_e, p_ref, s_ref, halo, plane_e, send_e)
    add_wells_to_plane(sizes, cell_ref, mu_ref, wp_ref, ws_ref, x_e, send_e)
    tail = slice(2 * sizes.ny, 2 * sizes.ny + SUB)
    send_e[tail, :] = send_o[tail, :]


def near_weights(sizes, cell_ref, weight_ref, plane_e, plane_o, near_ref):
    ny, groups = sizes.ny, sizes.groups
    even = lax.axis_index("gx") % 2 == 0
    x_o, x_e = facing(sizes, even)
    for g in range(groups):
        y = path_y(sizes, cell_ref, g)
        for i, (x, plane) in enumerate(((x_o, plane_o), (x_e, plane_e))):
            weight = weight_ref[pl.ds(x + g * SUB, 1), :]
            for j in range(2):
                to = (2 * i + j) * groups + g
                near_ref[to : to + 1, :] = weight * plane[pl.ds(y + j * ny, 1), :]


def put_planes(sizes, even, send_e, send_o, p_ref, s_ref, pad):
    ny = sizes.ny
    x_o, x_e = facing(sizes, even)
    for send, x in ((send_o, x_o), (send_e, x_e)):
        start = pl.multiple_of(x * ny + pad, SUB)
        for r in range(0, ny, SUB):
            p_ref[pl.ds(start + r, SUB), :] = send[r : r + SUB, :]
            s_ref[pl.ds(start + r, SUB), :] = send[ny + r : ny + r + SUB, :]


def inner_kernel(
    sizes,
    first,
    cell_ref,
    p_in,
    s_in,
    mu_ref,
    wp_ref,
    ws_ref,
    weight_ref,
    send_o,
    tx_ref,
    ty_ref,
    tyl_ref,
    tz_ref,
    tzl_ref,
    rp_ref,
    ip_ref,
    cc_ref,
    rs_ref,
    uu_ref,
    xx_ref,
    edge_ref,
    plane_e,
    *refs,
):
    ny, planes = sizes.ny, sizes.planes
    rows = planes * ny
    even = lax.axis_index("gx") % 2 == 0
    if first:
        plane_o, p_old, s_old, p_ref, s_ref, rows_ref, send_e, near_ref = refs
        halo = None
        near_weights(sizes, cell_ref, weight_ref, plane_e, plane_o, near_ref)
    else:
        halo, p_old, s_old, p_ref, s_ref, rows_ref, send_e = refs
    finish_core_plane(sizes, cell_ref, p_old, s_old, mu_ref, wp_ref, ws_ref, send_o, halo, plane_e, send_e)
    add_wells(sizes, cell_ref, mu_ref, wp_ref, ws_ref, p_old, s_old, SUB)
    put_planes(sizes, even, send_e, send_o, p_old, s_old, SUB)

    @pl.loop(0, ny // SUB)
    def _(r):
        y0 = pl.multiple_of(r * SUB, SUB)
        here = [pl.ds(y0 + (x * ny + SUB), SUB) for x in range(planes)]
        ps = [p_old[at, :] for at in here]
        ss = [s_old[at, :] for at in here]
        tx = None
        for x in range(planes):
            at = pl.ds(y0 + x * ny, SUB)
            up = pl.ds(y0 + (x * ny + SUB + 1), SUB)
            down = pl.ds(y0 + (x * ny + SUB - 1), SUB)
            txl = tx
            tx = tx_ref[at, :] if x < planes - 1 else None
            ty, tyl, tz, tzl = ty_ref[at, :], tyl_ref[at, :], tz_ref[at, :], tzl_ref[at, :]

            def neighbours(fields, old):
                mid = fields[x]
                total = tz * pltpu.roll(mid, LANES - 1, 1) + tzl * pltpu.roll(mid, 1, 1)
                total = total + (ty * old[up, :] + tyl * old[down, :])
                if x < planes - 1:
                    total = total + tx * fields[x + 1]
                if x > 0:
                    total = total + txl * fields[x - 1]
                return total

            sum_p = neighbours(ps, p_old)
            sum_s = neighbours(ss, s_old)
            if x == 0:
                ip, cc, rp, rs, uu, xx = [edge_ref[pl.ds(y0 + i * ny, SUB), :] for i in range(6)]
            else:
                ip, cc, rp, rs, uu, xx = [ref[at, :] for ref in (ip_ref, cc_ref, rp_ref, rs_ref, uu_ref, xx_ref)]
            p = rp + ip * sum_p + cc * sum_s
            p_ref[here[x], :] = p
            s_ref[here[x], :] = rs + uu * sum_s - xx * p

    clear_ends(rows, p_ref, s_ref)
    path_rows(sizes, cell_ref, weight_ref, p_ref, rows_ref)


def facing_kernel(sizes, cell_ref, from_o, p_ref, s_ref, plane_o, near_ref, send_o, sums_ref):
    even = lax.axis_index("gx") % 2 == 0
    x_o, _ = facing(sizes, even)
    finish_plane(sizes, x_o, p_ref, s_ref, from_o, plane_o, send_o)
    send_o[2 * sizes.ny :, :] = from_o[2 * sizes.ny :, :]
    near_sums(sizes, cell_ref, from_o, near_ref, 0, sums_ref)


def near_sums(sizes, cell_ref, halo, near_ref, side, sums_ref):
    groups = sizes.groups
    for g in range(groups):
        y = path_y(sizes, cell_ref, g)
        row = jnp.zeros((1, LANES), F32)
        for j in range(2):
            at = (2 * side + j) * groups + g
            row = row + near_ref[at : at + 1, :] * halo[pl.ds(y + j * sizes.ny, 1), :]
        sums_ref[g : g + 1, :] = row


def outer_kernel(
    sizes,
    final,
    cell_ref,
    send_in,
    from_e,
    rows_ref,
    sums_ref,
    parts_in,
    table_ref,
    wp_ref,
    ws_ref,
    shared_ref,
    near_ref,
    send_o,
    mu_ref,
    parts_out,
    *rest,
):
    ny, groups = sizes.ny, sizes.groups
    near_rows = rest[-1]
    even = lax.axis_index("gx") % 2 == 0
    x_o, _ = facing(sizes, even)

    def table(i):
        return table_ref[i * groups : (i + 1) * groups, :]

    tile_e, tile_o = from_e[2 * ny : 2 * ny + SUB, :], send_o[2 * ny : 2 * ny + SUB, :]
    low = jnp.where(even, tile_o, tile_e)
    high = jnp.where(even, tile_e, tile_o)
    before = table(BEFORE)
    total_own = parts_in[0:groups, :] + column_of(high[1:2, :], groups)
    total_before = parts_in[groups : 2 * groups, :] + column_of(low[0:1, :], groups)
    mu = (table(RHS) + jnp.where(before > 0.5, total_before, total_own)) * table(INV)
    mu_ref[...] = mu
    near_sums(sizes, cell_ref, from_e, near_ref, 1, near_rows)
    by_lane = rows_ref[...] + sums_ref[...] + near_rows[...] + shared_ref[...] * row_of(mu, groups)
    add_wells_to_plane(sizes, cell_ref, mu_ref, wp_ref, ws_ref, x_o, send_o)
    part_own, part_before = put_sums(sizes, before, by_lane, parts_out, send_o)
    if not final:
        return
    grads_ref = rest[0]
    mu_own = (table(RHS_OWN) + total_own) * table(INV_OWN)
    grad_own = mu_own * table(SUM_OWN) - part_own
    grad_before = -part_before
    lane = iota((groups, LANES), 1)
    slot_own, slot_before = table(SLOT_OWN), table(SLOT_BEFORE)
    inside = lane < groups
    for d in range(sizes.devices):
        want = (lane + d * groups).astype(F32)
        own = jnp.where(inside & (slot_own == want), grad_own, 0.0)
        other = jnp.where(inside & (slot_before == want), grad_before, 0.0)
        row = jnp.sum(own + other, axis=0, keepdims=True)
        grads_ref[d * SUB : (d + 1) * SUB, :] = jnp.where(
            iota((SUB, LANES), 0) == 0, jnp.broadcast_to(row, (SUB, LANES)), 0.0
        )


def final_kernel(
    sizes, cell_ref, p_in, s_in, mu_ref, wp_ref, ws_ref, plane_e, send_o, from_e, p_ref, s_ref, send_e
):
    rows = sizes.planes * sizes.ny
    even = lax.axis_index("gx") % 2 == 0

    @pl.loop(0, rows // SUB, unroll=8)
    def _(i):
        at = pl.ds(pl.multiple_of(i * SUB, SUB), SUB)
        come = pl.ds(pl.multiple_of(i * SUB + SUB, SUB), SUB)
        p_ref[at, :] = p_in[come, :]
        s_ref[at, :] = s_in[come, :]

    add_wells(sizes, cell_ref, mu_ref, wp_ref, ws_ref, p_ref, s_ref, 0)
    finish_core_plane(sizes, cell_ref, p_in, s_in, mu_ref, wp_ref, ws_ref, send_o, from_e, plane_e, send_e)
    put_planes(sizes, even, send_e, send_o, p_ref, s_ref, 0)


class Sizes:
    def __init__(self, planes, ny, groups, run, devices):
        self.planes, self.ny, self.groups, self.run, self.devices = planes, ny, groups, run, devices


def body(
    rhs_pressure,
    rhs_saturation,
    trans_x,
    trans_y,
    trans_z,
    coupling,
    upwind,
    storage,
    cross,
    accel,
    perf_cell,
    perf_well,
    perf_index,
    well_rhs,
    well_slot,
):
    planes, ny, nz = trans_x.shape
    devices = lax.axis_size("gx")
    groups = well_rhs.shape[0] // devices
    run = perf_cell.shape[0] // groups
    sizes = Sizes(planes, ny, groups, run, devices)
    rows = planes * ny
    padded = rows + 2 * SUB
    SMEM, VMEM, HBM, DMA = pltpu.SMEM, pltpu.VMEM, pltpu.HBM, pltpu.SemaphoreType.DMA

    def flat(array):
        return array.reshape(rows, nz)

    def lines(array):
        return array.reshape(-1, LANES)

    def call(kernel, args, spaces, outs, scratch, name, micros, aliases=None):
        return pl.pallas_call(
            kernel,
            in_specs=[spec(space) for space in spaces],
            out_specs=[spec(VMEM)] * len(outs),
            out_shape=outs,
            scratch_shapes=scratch,
            input_output_aliases=aliases or {},
            compiler_params=pltpu.CompilerParams(vmem_limit_bytes=16 * 1024 * 1024),
            cost_estimate=pl.CostEstimate(flops=int(micros * 4e6), bytes_accessed=int(micros * 3e6), transcendentals=0),
            name=name,
        )(*[placed(a, space) for a, space in zip(args, spaces)])

    def call_vmem(kernel, args, outs, scratch, name, micros, aliases=None):
        return call(
            functools.partial(kernel, sizes), [perf_cell] + args, [SMEM] + [VMEM] * len(args), outs, scratch,
            name, micros, aliases,
        )

    pairs_e = [(i, i ^ 1) for i in range(devices) if i ^ 1 < devices]
    pairs_o = []
    for i in range(1, devices - 1, 2):
        pairs_o += [(i, i + 1), (i + 1, i)]

    def to_core(block):
        return lax.ppermute(block, "gx", pairs_e)

    def to_chip(block):
        return lax.ppermute(block, "gx", pairs_o)

    tx = flat(trans_x)
    index = lines(perf_index)
    send, wells = call(
        functools.partial(first_kernel, sizes),
        [tx, lines(perf_well), index],
        [HBM, HBM, HBM],
        [vmem(ny + SUB), vmem(2 * groups)],
        [VMEM(index.shape, jnp.int32), VMEM(index.shape, F32), DMA((3,))],
        "first",
        1,
    )
    from_o = to_chip(send)
    from_e = to_core(send)
    big = [tx] + [
        flat(a)
        for a in (trans_y, trans_z, accel, coupling, upwind, storage, rhs_pressure, rhs_saturation, cross)
    ]
    made = call(
        functools.partial(setup_kernel, sizes),
        [perf_cell, perf_index] + big,
        [SMEM] + [HBM] * (1 + len(big)),
        [vmem(rows)] * 11 + [vmem(3 * ny), vmem(groups * SUB)],
        [
            VMEM((padded, LANES), F32),
            VMEM((rows, LANES), F32),
            VMEM((rows, LANES), F32),
            SMEM(perf_index.shape, F32),
            DMA((10,)),
            DMA,
        ],
        "setup",
        4,
    )
    coefficients, (extra, weight) = list(made[:11]), made[11:]
    group_row = VMEM((groups, LANES), F32)
    fields = [vmem(padded), vmem(padded)]
    block = vmem(2 * ny + SUB)
    slabs = vmem(groups * SUB)
    p, s, edge, plane_e, plane_o, wp, ws, shared, table, mu, parts, send_o = call(
        functools.partial(start_kernel, sizes),
        [perf_cell, from_o, from_e, wells, lines(well_rhs), lines(well_slot), coefficients[0]]
        + coefficients[5:]
        + [extra, weight],
        [SMEM] + [VMEM] * 3 + [HBM] * 2 + [VMEM] * 9,
        fields
        + [vmem(6 * ny), vmem(4 * ny), vmem(4 * ny), slabs, slabs, vmem(groups), vmem(TABLE * groups)]
        + [vmem(groups), vmem(2 * groups), block],
        [
            group_row,
            VMEM(lines(well_rhs).shape, F32),
            VMEM(lines(well_slot).shape, jnp.int32),
            DMA((2,)),
        ],
        "start",
        2,
    )
    near = None
    for sweep in range(1, SWEEPS):
        final = sweep == SWEEPS - 1
        next_o = to_chip(send_o)
        first = sweep == 1
        _, _, p, s, by_lane, send_e, *rest = call_vmem(
            lambda sz, *refs: inner_kernel(sz, first, *refs),
            [p, s, mu, wp, ws, weight, send_o] + coefficients + [edge, plane_e, plane_o if first else from_e],
            fields + fields + [vmem(groups), block] + ([vmem(4 * groups)] if first else []),
            [],
            "inner",
            2,
            {1: 0, 2: 1},
        )
        if first:
            near = rest[0]
        next_e = to_core(send_e)
        from_e, from_o = next_e, next_o
        half_o, sums = call_vmem(
            facing_kernel, [from_o, p, s, plane_o, near], [block, vmem(groups)], [], "facing", 0.5
        )
        send_o, mu, parts, *rest = call_vmem(
            lambda sz, *refs: outer_kernel(sz, final, *refs),
            [half_o, from_e, by_lane, sums, parts, table, wp, ws, shared, near],
            [block, vmem(groups), vmem(2 * groups)] + ([vmem(devices * SUB)] if final else []),
            [group_row],
            "outer",
            1,
            {1: 0},
        )
    grads = lax.all_to_all(rest[0].reshape(devices, SUB, LANES), "gx", 0, 0)
    p, s = call_vmem(
        final_kernel,
        [p, s, mu, wp, ws, plane_e, send_o, from_e],
        [vmem(rows), vmem(rows)],
        [VMEM((2 * ny + SUB, LANES), F32)],
        "final",
        2,
    )
    control = jnp.sum(grads, axis=(0, 1))[:groups]
    shape = trans_x.shape
    return p.reshape(shape), s.reshape(shape), control


def solution(mesh):
    grid = P(("ens", "gx"), None, None)
    line = P(("ens", "gx"))
    return jax.shard_map(
        body,
        mesh=mesh,
        in_specs=(grid,) * 10 + (line,) * 3 + (P("ens"), P("ens")),
        out_specs=(grid, grid, line),
        check_vma=False,
    )
```

```python
import functools

import jax
import jax.numpy as jnp
from jax import lax
from jax.experimental import pallas as pl
from jax.experimental.pallas import tpu as pltpu
from jax.sharding import PartitionSpec as P

SWEEPS = 6
SUB = 8
LANES = 128
F32 = jnp.float32


def vmem(rows):
    return pltpu.VMEM((rows, LANES), F32)


def placed(array, space):
    return array if space is pltpu.SMEM else pltpu.with_memory_space_constraint(array, space)


def spec(space):
    return pl.BlockSpec(memory_space=space)


def iota(shape, dim):
    return lax.broadcasted_iota(jnp.int32, shape, dim)


def lane_sum(block):
    return jnp.sum(block, axis=1, keepdims=True)


def spread(column, groups):
    return jnp.broadcast_to(column, (groups, LANES))


def row_of(column, groups):
    mine = iota((groups, LANES), 0) == iota((groups, LANES), 1)
    return jnp.sum(jnp.where(mine, column, 0.0), axis=0, keepdims=True)


def column_of(row, groups):
    mine = iota((groups, LANES), 0) == iota((groups, LANES), 1)
    return spread(lane_sum(jnp.where(mine, jnp.broadcast_to(row, (groups, LANES)), 0.0)), groups)


def well_block(part_own, part_before, groups):
    sub = iota((SUB, LANES), 0)
    own = jnp.broadcast_to(row_of(part_own, groups), (SUB, LANES))
    before = jnp.broadcast_to(row_of(part_before, groups), (SUB, LANES))
    return jnp.where(sub == 0, own, jnp.where(sub == 1, before, 0.0))


def group_rows(ref, groups, run):
    per_row = LANES // run
    return jnp.concatenate(
        [jnp.broadcast_to(ref[i : i + 1, :], (per_row, LANES)) for i in range(groups // per_row)], axis=0
    )


def first_kernel(sizes, tx_hbm, well_hbm, index_hbm, send_ref, wells_ref, well_ref, index_ref, sems):
    ny, groups, run = sizes.ny, sizes.groups, sizes.run
    plane = pltpu.make_async_copy(
        tx_hbm.at[pl.ds((sizes.planes - 1) * ny, ny)], send_ref.at[pl.ds(0, ny)], sems.at[0]
    )
    get_well = pltpu.make_async_copy(well_hbm, well_ref, sems.at[1])
    get_index = pltpu.make_async_copy(index_hbm, index_ref, sems.at[2])
    for copy in (get_well, get_index, plane):
        copy.start()
    place = lax.axis_index("gx")
    shape = (groups, LANES)
    per_row = LANES // run
    local = iota(shape, 0) % per_row
    lane = iota(shape, 1)
    get_well.wait()
    get_index.wait()
    weights = jnp.where(lane // run == local, group_rows(index_ref, groups, run), 0.0)
    total = lane_sum(weights)
    first = jnp.where(lane == local * run, group_rows(well_ref, groups, run).astype(F32), 0.0)
    well = lane_sum(first)
    before = well < (place * groups).astype(F32)
    before = spread(jnp.where(before, 1.0, 0.0), groups)
    total = spread(total, groups)
    wells_ref[0:groups, :] = before
    wells_ref[groups : 2 * groups, :] = total
    send_ref[ny : ny + SUB, :] = well_block(total * (1.0 - before), total * before, groups)
    plane.wait()


def setup_kernel(
    sizes,
    cell_hbm,
    index_hbm,
    tx_hbm,
    ty_hbm,
    tz_hbm,
    accel_hbm,
    coupling_hbm,
    upwind_hbm,
    storage_hbm,
    rhs_p_hbm,
    rhs_s_hbm,
    cross_hbm,
    tx_ref,
    ty_ref,
    tyl_ref,
    tz_ref,
    tzl_ref,
    rp_ref,
    ip_ref,
    cc_ref,
    rs_ref,
    uu_ref,
    xx_ref,
    extra_ref,
    weight_ref,
    y_ref,
    raw_ty,
    raw_storage,
    cwi_ref,
    cell_ref,
    index_ref,
    sems,
    fetch_sems,
):
    ny, planes, groups, run = sizes.ny, sizes.planes, sizes.groups, sizes.run
    rows = planes * ny
    moves = [
        (tx_hbm, tx_ref),
        (ty_hbm, raw_ty),
        (tz_hbm, tz_ref),
        (accel_hbm, ip_ref),
        (coupling_hbm, cc_ref),
        (upwind_hbm, uu_ref),
        (storage_hbm, raw_storage),
        (rhs_p_hbm, rp_ref),
        (rhs_s_hbm, rs_ref),
        (cross_hbm, xx_ref),
    ]
    fetches = [
        pltpu.make_async_copy(src, dst, fetch_sems.at[i])
        for i, (src, dst) in enumerate(((cell_hbm, cell_ref), (index_hbm, index_ref)))
    ]
    for fetch in fetches:
        fetch.start()
    copies = []
    for x in range(planes):
        for i, (src, dst) in enumerate(moves):
            to = x * ny + SUB if dst is raw_ty else x * ny
            copies.append(
                pltpu.make_async_copy(src.at[pl.ds(x * ny, ny)], dst.at[pl.ds(to, ny)], sems.at[x, i])
            )
    for copy in copies:
        copy.start()

    last = lax.axis_index("gx") == lax.axis_size("gx") - 1
    keep_last = jnp.where(last, 0.0, 1.0)
    zero = jnp.zeros((SUB, LANES), F32)

    @pl.loop(0, rows // SUB, unroll=8)
    def _(i):
        cwi_ref[pl.ds(pl.multiple_of(i * SUB, SUB), SUB), :] = zero

    for fetch in fetches:
        fetch.wait()
    spot = iota((SUB, LANES), 0) * LANES + iota((SUB, LANES), 1)
    for g in range(groups):
        y_ref[g] = (cell_ref[g * run] // LANES) % ny
        weight = zero
        for k in range(g * run, (g + 1) * run):
            cell = cell_ref[k]
            at = (cell // (ny * LANES)) * LANES + cell % LANES
            weight = weight + jnp.where(spot == at, index_ref[k], 0.0)
        weight_ref[g * SUB : (g + 1) * SUB, :] = weight
        slab = pl.ds((cell_ref[g * run] // LANES) % ny, planes, ny)
        cwi_ref[slab, :] = cwi_ref[slab, :] + weight

    lane = iota((SUB, LANES), 1)
    sub = iota((SUB, LANES), 0)
    for x in range(planes):
        for copy in copies[x * len(moves) : (x + 1) * len(moves)]:
            copy.wait()

        @pl.loop(0, ny // SUB, unroll=4)
        def _(r):
            y0 = pl.multiple_of(r * SUB, SUB)
            ypos = sub + y0
            at = pl.ds(y0 + x * ny, SUB)
            tx = tx_ref[at, :]
            if x == planes - 1:
                tx = tx * keep_last
                tx_ref[at, :] = tx
            ty = jnp.where(ypos == ny - 1, 0.0, raw_ty[pl.ds(y0 + (x * ny + SUB), SUB), :])
            tyl = jnp.where(ypos == 0, 0.0, raw_ty[pl.ds(y0 + (x * ny + SUB - 1), SUB), :])
            tz = jnp.where(lane == LANES - 1, 0.0, tz_ref[at, :])
            tzl = pltpu.roll(tz, 1, 1)
            ty_ref[at, :] = ty
            tyl_ref[at, :] = tyl
            tz_ref[at, :] = tz
            tzl_ref[at, :] = tzl
            tsum = tx + ty + tyl + tz + tzl
            if x > 0:
                tsum = tsum + tx_ref[pl.ds(y0 + (x - 1) * ny, SUB), :]
            accel = ip_ref[at, :]
            coupling = cc_ref[at, :]
            upwind = uu_ref[at, :]
            to_p = accel * (1.0 + jnp.abs(coupling))
            to_s = accel * jnp.abs(upwind)
            dp = to_p * tsum + accel * cwi_ref[at, :]
            ds = to_s * tsum + raw_storage[at, :]
            if x == 0:
                here = pl.ds(y0, SUB)
                extra_ref[here, :] = to_p
                extra_ref[pl.ds(y0 + ny, SUB), :] = to_s
                extra_ref[pl.ds(y0 + 2 * ny, SUB), :] = ds
                ip_ref[at, :] = dp
            else:
                ip = 1.0 / dp
                is_ = 1.0 / ds
                ip_ref[at, :] = ip
                cc_ref[at, :] = coupling * ip
                rp_ref[at, :] = rp_ref[at, :] * ip
                rs_ref[at, :] = rs_ref[at, :] * is_
                uu_ref[at, :] = upwind * is_
                xx_ref[at, :] = xx_ref[at, :] * is_


def own_lanes(ref, place, groups):
    shape = (groups, LANES)
    start = place * groups
    row = jnp.broadcast_to(ref[pl.ds(start // LANES, 1), :].astype(F32), shape)
    mine = iota(shape, 1) == iota(shape, 0) + start % LANES
    return spread(lane_sum(jnp.where(mine, row, 0.0)), groups)


def clear_ends(rows, *refs):
    zero = jnp.zeros((SUB, LANES), F32)
    for ref in refs:
        ref[0:SUB, :] = zero
        ref[rows + SUB : rows + 2 * SUB, :] = zero


def path_y(sizes, cell_ref, g):
    return cell_ref[g]


def slab_of(sizes, cell_ref, g, pad):
    return pl.ds(path_y(sizes, cell_ref, g) + pad, sizes.planes, sizes.ny)


def add_wells(sizes, cell_ref, mu_ref, wp_ref, ws_ref, p_ref, s_ref, pad):
    for g in range(sizes.groups):
        slab = slab_of(sizes, cell_ref, g, pad)
        at = pl.ds(g * SUB, SUB)
        mu = mu_ref[g : g + 1, :]
        p_ref[slab, :] = p_ref[slab, :] + mu * wp_ref[at, :]
        s_ref[slab, :] = s_ref[slab, :] - mu * ws_ref[at, :]


def add_wells_to_plane(sizes, cell_ref, mu_ref, wp_ref, ws_ref, x, send_ref):
    for g in range(sizes.groups):
        y = path_y(sizes, cell_ref, g)
        in_p, in_s, at = pl.ds(y, 1), pl.ds(y + sizes.ny, 1), pl.ds(x + g * SUB, 1)
        mu = mu_ref[g : g + 1, :]
        send_ref[in_p, :] = send_ref[in_p, :] + mu * wp_ref[at, :]
        send_ref[in_s, :] = send_ref[in_s, :] - mu * ws_ref[at, :]


def path_rows(sizes, cell_ref, weight_ref, p_ref, rows_ref):
    for g in range(sizes.groups):
        slab = slab_of(sizes, cell_ref, g, SUB)
        at = pl.ds(g * SUB, SUB)
        rows_ref[g : g + 1, :] = jnp.sum(p_ref[slab, :] * weight_ref[at, :], axis=0, keepdims=True)


def facing(sizes, even):
    last = sizes.planes - 1
    return jnp.where(even, 0, last), jnp.where(even, last, 0)


def finish_plane(sizes, x, p_ref, s_ref, halo_ref, plane_ref, send_ref):
    ny = sizes.ny
    start = pl.multiple_of(x * ny + SUB, SUB)
    for r in range(0, ny, SUB):
        at = slice(r, r + SUB)
        at_s = slice(ny + r, ny + r + SUB)
        p, s = p_ref[pl.ds(start + r, SUB), :], s_ref[pl.ds(start + r, SUB), :]
        if halo_ref is not None:
            hp, hs = halo_ref[at, :], halo_ref[at_s, :]
            a, b, c, xx = [plane_ref[i * ny + r : i * ny + r + SUB, :] for i in range(4)]
            change = a * hp + b * hs
            p = p + change
            s = s + c * hs - xx * change
        send_ref[at, :] = p
        send_ref[at_s, :] = s


BEFORE, RHS_OWN, INV_OWN, SUM_OWN, RHS, INV, SLOT_OWN, SLOT_BEFORE, TABLE = range(9)


def shared_cells(sizes, cell_ref, weight_ref, wp_ref, out_ref):
    groups = sizes.groups
    shape = (groups, LANES)
    sub, lane = iota(shape, 0), iota(shape, 1)
    y_row = jnp.full(shape, -1, jnp.int32)
    y_col = y_row
    for g in range(groups):
        y = path_y(sizes, cell_ref, g)
        y_row = jnp.where(lane == g, y, y_row)
        y_col = jnp.where(sub == g, y, y_col)
    total = jnp.zeros(shape, F32)
    empty = jnp.zeros((LANES - groups, LANES), F32)
    for x in range(sizes.planes):
        at = pl.ds(x, groups, SUB)
        other = jnp.concatenate([wp_ref[at, :], empty], axis=0)
        total = total + lax.dot_general(
            weight_ref[at, :], other, (((1,), (1,)), ((), ())),
            precision=lax.Precision.HIGHEST, preferred_element_type=F32,
        )
    out_ref[...] = jnp.where(y_row == y_col, total, 0.0)


def start_kernel(
    sizes,
    cell_ref,
    from_o,
    from_e,
    wells_ref,
    rhs_hbm,
    slot_hbm,
    tx_ref,
    rp_ref,
    ip_ref,
    cc_ref,
    rs_ref,
    uu_ref,
    xx_ref,
    extra_ref,
    weight_ref,
    p_ref,
    s_ref,
    edge_ref,
    plane_e,
    plane_o,
    wp_ref,
    ws_ref,
    shared_ref,
    table_ref,
    mu_ref,
    sums_out,
    send_o,
    rows_ref,
    rhs_ref,
    slot_ref,
    sems,
):
    ny, planes, groups = sizes.ny, sizes.planes, sizes.groups
    rows = planes * ny
    place = lax.axis_index("gx")
    even = place % 2 == 0
    x_o, _ = facing(sizes, even)
    fetches = [
        pltpu.make_async_copy(rhs_hbm, rhs_ref, sems.at[0]),
        pltpu.make_async_copy(slot_hbm, slot_ref, sems.at[1]),
    ]
    for fetch in fetches:
        fetch.start()

    @pl.loop(0, ny // SUB)
    def _(r):
        y0 = pl.multiple_of(r * SUB, SUB)
        at = pl.ds(y0, SUB)
        txl = jnp.where(even, from_o[at, :], from_e[at, :])
        ip = 1.0 / (ip_ref[at, :] + extra_ref[at, :] * txl)
        is_ = 1.0 / (extra_ref[pl.ds(y0 + 2 * ny, SUB), :] + extra_ref[pl.ds(y0 + ny, SUB), :] * txl)
        cc, uu = cc_ref[at, :] * ip, uu_ref[at, :] * is_
        rp, rs, xx = rp_ref[at, :] * ip, rs_ref[at, :] * is_, xx_ref[at, :] * is_
        for i, value in enumerate([ip, cc, rp, rs, uu, xx]):
            edge_ref[pl.ds(y0 + i * ny, SUB), :] = value
        end = pl.ds(y0 + (planes - 1) * ny, SUB)
        tx = tx_ref[end, :]
        low = [ip * txl, cc * txl, uu * txl, xx]
        high = [ip_ref[end, :] * tx, cc_ref[end, :] * tx, uu_ref[end, :] * tx, xx_ref[end, :]]
        for i in range(4):
            to = pl.ds(y0 + i * ny, SUB)
            plane_o[to, :] = jnp.where(even, low[i], high[i])
            plane_e[to, :] = jnp.where(even, high[i], low[i])
        p_ref[pl.ds(y0 + SUB, SUB), :] = rp
        s_ref[pl.ds(y0 + SUB, SUB), :] = rs - xx * rp
        for x in range(1, planes):
            at = pl.ds(y0 + x * ny, SUB)
            to = pl.ds(y0 + (x * ny + SUB), SUB)
            rp = rp_ref[at, :]
            p_ref[to, :] = rp
            s_ref[to, :] = rs_ref[at, :] - xx_ref[at, :] * rp

    clear_ends(rows, p_ref, s_ref)
    sub = iota((SUB, LANES), 0)
    for g in range(groups):
        y = path_y(sizes, cell_ref, g)
        at = pl.ds(g * SUB, SUB)
        slab = pl.ds(y, planes, ny)
        ip = jnp.where(sub == 0, edge_ref[pl.ds(y, 1), :], ip_ref[slab, :])
        xx = jnp.where(sub == 0, edge_ref[pl.ds(y + 5 * ny, 1), :], xx_ref[slab, :])
        wp = weight_ref[at, :] * ip
        wp_ref[at, :] = wp
        ws_ref[at, :] = wp * xx
    shared_cells(sizes, cell_ref, weight_ref, wp_ref, shared_ref)

    tile_e, tile_o = from_e[ny : ny + SUB, :], from_o[ny : ny + SUB, :]
    low = jnp.where(even, tile_o, tile_e)
    high = jnp.where(even, tile_e, tile_o)
    before = wells_ref[0:groups, :]
    mine = wells_ref[groups : 2 * groups, :]
    is_before = before > 0.5
    sum_own = mine * (1.0 - before) + column_of(high[1:2, :], groups)
    sum_before = mine * before + column_of(low[0:1, :], groups)
    for fetch in fetches:
        fetch.wait()
    rhs_own = own_lanes(rhs_ref, place, groups)
    rhs_before = own_lanes(rhs_ref, jnp.maximum(place - 1, 0), groups)
    inv_own = 1.0 / (1.5 * sum_own + 0.5)
    inv_before = 1.0 / (1.5 * sum_before + 0.5)
    rhs = jnp.where(is_before, rhs_before, rhs_own)
    inv = jnp.where(is_before, inv_before, inv_own)
    entries = {
        BEFORE: before,
        RHS_OWN: rhs_own,
        INV_OWN: inv_own,
        SUM_OWN: sum_own,
        RHS: rhs,
        INV: inv,
        SLOT_OWN: own_lanes(slot_ref, place, groups),
        SLOT_BEFORE: own_lanes(slot_ref, jnp.maximum(place - 1, 0), groups),
    }
    for i, entry in entries.items():
        table_ref[i * groups : (i + 1) * groups, :] = entry
    mu = rhs * inv
    mu_ref[...] = mu

    finish_plane(sizes, x_o, p_ref, s_ref, None, None, send_o)
    add_wells_to_plane(sizes, cell_ref, mu_ref, wp_ref, ws_ref, x_o, send_o)
    path_rows(sizes, cell_ref, weight_ref, p_ref, rows_ref)
    put_sums(sizes, even, before, rows_ref[...] + shared_ref[...] * row_of(mu, groups), sums_out, send_o)


def put_sums(sizes, to_before, before, by_lane, rows_out, send_ref):
    ny, groups = sizes.ny, sizes.groups
    rows_out[...] = by_lane
    send_ref[2 * ny : 2 * ny + groups, :] = by_lane * jnp.where(to_before, before, 1.0 - before)


def finish_core_plane(sizes, cell_ref, p_ref, s_ref, mu_ref, wp_ref, ws_ref, halo, plane_e, send_e):
    even = lax.axis_index("gx") % 2 == 0
    _, x_e = facing(sizes, even)
    finish_plane(sizes, x_e, p_ref, s_ref, halo, plane_e, send_e)
    add_wells_to_plane(sizes, cell_ref, mu_ref, wp_ref, ws_ref, x_e, send_e)


def near_weights(sizes, cell_ref, weight_ref, plane_e, plane_o, near_ref):
    ny, groups = sizes.ny, sizes.groups
    even = lax.axis_index("gx") % 2 == 0
    x_o, x_e = facing(sizes, even)
    for g in range(groups):
        y = path_y(sizes, cell_ref, g)
        for i, (x, plane) in enumerate(((x_o, plane_o), (x_e, plane_e))):
            weight = weight_ref[pl.ds(x + g * SUB, 1), :]
            for j in range(2):
                to = (2 * i + j) * groups + g
                near_ref[to : to + 1, :] = weight * plane[pl.ds(y + j * ny, 1), :]


def put_planes(sizes, even, send_e, send_o, p_ref, s_ref, pad):
    ny = sizes.ny
    x_o, x_e = facing(sizes, even)
    for send, x in ((send_o, x_o), (send_e, x_e)):
        start = pl.multiple_of(x * ny + pad, SUB)
        for r in range(0, ny, SUB):
            p_ref[pl.ds(start + r, SUB), :] = send[r : r + SUB, :]
            s_ref[pl.ds(start + r, SUB), :] = send[ny + r : ny + r + SUB, :]


def inner_kernel(
    sizes,
    first,
    cell_ref,
    p_in,
    s_in,
    mu_ref,
    wp_ref,
    ws_ref,
    weight_ref,
    send_o,
    sums_in,
    table_ref,
    tx_ref,
    ty_ref,
    tyl_ref,
    tz_ref,
    tzl_ref,
    rp_ref,
    ip_ref,
    cc_ref,
    rs_ref,
    uu_ref,
    xx_ref,
    edge_ref,
    plane_e,
    *refs,
):
    ny, planes = sizes.ny, sizes.planes
    rows = planes * ny
    even = lax.axis_index("gx") % 2 == 0
    if first:
        plane_o, p_old, s_old, p_ref, s_ref, rows_ref, sums_out, send_e, near_ref = refs
        halo = None
        near_weights(sizes, cell_ref, weight_ref, plane_e, plane_o, near_ref)
    else:
        halo, p_old, s_old, p_ref, s_ref, rows_ref, sums_out, send_e = refs
    finish_core_plane(sizes, cell_ref, p_old, s_old, mu_ref, wp_ref, ws_ref, halo, plane_e, send_e)
    before = table_ref[BEFORE * sizes.groups : (BEFORE + 1) * sizes.groups, :]
    put_sums(sizes, jnp.logical_not(even), before, sums_in[...], sums_out, send_e)
    add_wells(sizes, cell_ref, mu_ref, wp_ref, ws_ref, p_old, s_old, SUB)
    put_planes(sizes, even, send_e, send_o, p_old, s_old, SUB)

    @pl.loop(0, ny // SUB)
    def _(r):
        y0 = pl.multiple_of(r * SUB, SUB)
        here = [pl.ds(y0 + (x * ny + SUB), SUB) for x in range(planes)]
        ps = [p_old[at, :] for at in here]
        ss = [s_old[at, :] for at in here]
        tx = None
        for x in range(planes):
            at = pl.ds(y0 + x * ny, SUB)
            up = pl.ds(y0 + (x * ny + SUB + 1), SUB)
            down = pl.ds(y0 + (x * ny + SUB - 1), SUB)
            txl = tx
            tx = tx_ref[at, :] if x < planes - 1 else None
            ty, tyl, tz, tzl = ty_ref[at, :], tyl_ref[at, :], tz_ref[at, :], tzl_ref[at, :]

            def neighbours(fields, old):
                mid = fields[x]
                total = tz * pltpu.roll(mid, LANES - 1, 1) + tzl * pltpu.roll(mid, 1, 1)
                total = total + (ty * old[up, :] + tyl * old[down, :])
                if x < planes - 1:
                    total = total + tx * fields[x + 1]
                if x > 0:
                    total = total + txl * fields[x - 1]
                return total

            sum_p = neighbours(ps, p_old)
            sum_s = neighbours(ss, s_old)
            if x == 0:
                ip, cc, rp, rs, uu, xx = [edge_ref[pl.ds(y0 + i * ny, SUB), :] for i in range(6)]
            else:
                ip, cc, rp, rs, uu, xx = [ref[at, :] for ref in (ip_ref, cc_ref, rp_ref, rs_ref, uu_ref, xx_ref)]
            p = rp + ip * sum_p + cc * sum_s
            p_ref[here[x], :] = p
            s_ref[here[x], :] = rs + uu * sum_s - xx * p

    clear_ends(rows, p_ref, s_ref)
    path_rows(sizes, cell_ref, weight_ref, p_ref, rows_ref)


def facing_kernel(sizes, cell_ref, from_o, p_ref, s_ref, plane_o, near_ref, send_o, sums_ref):
    even = lax.axis_index("gx") % 2 == 0
    x_o, _ = facing(sizes, even)
    finish_plane(sizes, x_o, p_ref, s_ref, from_o, plane_o, send_o)
    near_sums(sizes, cell_ref, from_o, near_ref, 0, sums_ref)


def near_sums(sizes, cell_ref, halo, near_ref, side, sums_ref):
    groups = sizes.groups
    for g in range(groups):
        y = path_y(sizes, cell_ref, g)
        row = jnp.zeros((1, LANES), F32)
        for j in range(2):
            at = (2 * side + j) * groups + g
            row = row + near_ref[at : at + 1, :] * halo[pl.ds(y + j * sizes.ny, 1), :]
        sums_ref[g : g + 1, :] = row


def outer_kernel(
    sizes,
    final,
    cell_ref,
    send_in,
    from_o,
    from_e,
    rows_ref,
    near_o,
    sums_in,
    table_ref,
    wp_ref,
    ws_ref,
    shared_ref,
    near_ref,
    send_o,
    mu_ref,
    *rest,
):
    ny, groups = sizes.ny, sizes.groups
    near_e = rest[-1]
    even = lax.axis_index("gx") % 2 == 0
    x_o, _ = facing(sizes, even)

    def table(i):
        return table_ref[i * groups : (i + 1) * groups, :]

    tail = slice(2 * ny, 2 * ny + groups)
    come_e, come_o = from_e[tail, :], from_o[tail, :]
    low = jnp.where(even, come_o, come_e)
    high = jnp.where(even, come_e, come_o)
    before = table(BEFORE)
    total = spread(lane_sum(sums_in[...] + jnp.where(before > 0.5, low, high)), groups)
    mu = (table(RHS) + total) * table(INV)
    mu_ref[...] = mu
    near_sums(sizes, cell_ref, from_e, near_ref, 1, near_e)
    by_lane = rows_ref[...] + near_o[...] + near_e[...] + shared_ref[...] * row_of(mu, groups)
    add_wells_to_plane(sizes, cell_ref, mu_ref, wp_ref, ws_ref, x_o, send_o)
    if not final:
        put_sums(sizes, even, before, by_lane, rest[0], send_o)
        return
    total_own = spread(lane_sum(sums_in[...] * (1.0 - before) + high), groups)
    total = spread(lane_sum(by_lane), groups)
    part_own, part_before = total * (1.0 - before), total * before
    grads_ref = rest[0]
    mu_own = (table(RHS_OWN) + total_own) * table(INV_OWN)
    grad_own = mu_own * table(SUM_OWN) - part_own
    grad_before = -part_before
    lane = iota((groups, LANES), 1)
    slot_own, slot_before = table(SLOT_OWN), table(SLOT_BEFORE)
    inside = lane < groups
    for d in range(sizes.devices):
        want = (lane + d * groups).astype(F32)
        own = jnp.where(inside & (slot_own == want), grad_own, 0.0)
        other = jnp.where(inside & (slot_before == want), grad_before, 0.0)
        row = jnp.sum(own + other, axis=0, keepdims=True)
        grads_ref[d * SUB : (d + 1) * SUB, :] = jnp.where(
            iota((SUB, LANES), 0) == 0, jnp.broadcast_to(row, (SUB, LANES)), 0.0
        )


def final_kernel(
    sizes,
    cell_ref,
    p_in,
    s_in,
    mu_ref,
    wp_ref,
    ws_ref,
    plane_e,
    send_o,
    from_e,
    p_old,
    s_old,
    p_out,
    s_out,
    send_e,
    sems,
):
    rows = sizes.planes * sizes.ny
    even = lax.axis_index("gx") % 2 == 0
    finish_core_plane(sizes, cell_ref, p_old, s_old, mu_ref, wp_ref, ws_ref, from_e, plane_e, send_e)
    add_wells(sizes, cell_ref, mu_ref, wp_ref, ws_ref, p_old, s_old, SUB)
    put_planes(sizes, even, send_e, send_o, p_old, s_old, SUB)
    copies = [
        pltpu.make_async_copy(field.at[pl.ds(SUB, rows)], out, sems.at[i])
        for i, (field, out) in enumerate(((p_old, p_out), (s_old, s_out)))
    ]
    for copy in copies:
        copy.start()
    for copy in copies:
        copy.wait()


class Sizes:
    def __init__(self, planes, ny, groups, run, devices):
        self.planes, self.ny, self.groups, self.run, self.devices = planes, ny, groups, run, devices


def body(
    rhs_pressure,
    rhs_saturation,
    trans_x,
    trans_y,
    trans_z,
    coupling,
    upwind,
    storage,
    cross,
    accel,
    perf_cell,
    perf_well,
    perf_index,
    well_rhs,
    well_slot,
):
    planes, ny, nz = trans_x.shape
    devices = lax.axis_size("gx")
    groups = well_rhs.shape[0] // devices
    run = perf_cell.shape[0] // groups
    sizes = Sizes(planes, ny, groups, run, devices)
    rows = planes * ny
    padded = rows + 2 * SUB
    SMEM, VMEM, HBM, DMA = pltpu.SMEM, pltpu.VMEM, pltpu.HBM, pltpu.SemaphoreType.DMA

    def flat(array):
        return array.reshape(rows, nz)

    def lines(array):
        return array.reshape(-1, LANES)

    def call(kernel, args, spaces, outs, scratch, name, micros, aliases=None):
        return pl.pallas_call(
            kernel,
            in_specs=[spec(space) for space in spaces],
            out_specs=[spec(out.memory_space) for out in outs],
            out_shape=outs,
            scratch_shapes=scratch,
            input_output_aliases=aliases or {},
            compiler_params=pltpu.CompilerParams(vmem_limit_bytes=16 * 1024 * 1024),
            cost_estimate=pl.CostEstimate(flops=int(micros * 4e6), bytes_accessed=int(micros * 3e6), transcendentals=0),
            name=name,
        )(*[placed(a, space) for a, space in zip(args, spaces)])

    def call_vmem(kernel, args, outs, scratch, name, micros, aliases=None):
        return call(
            functools.partial(kernel, sizes), [y] + args, [SMEM] + [VMEM] * len(args), outs, scratch,
            name, micros, aliases,
        )

    pairs_e = [(i, i ^ 1) for i in range(devices) if i ^ 1 < devices]
    pairs_o = []
    for i in range(1, devices - 1, 2):
        pairs_o += [(i, i + 1), (i + 1, i)]

    def to_core(block):
        return lax.ppermute(block, "gx", pairs_e)

    def to_chip(block):
        return lax.ppermute(block, "gx", pairs_o)

    tx = flat(trans_x)
    index = lines(perf_index)
    send, wells = call(
        functools.partial(first_kernel, sizes),
        [tx, lines(perf_well), index],
        [HBM, HBM, HBM],
        [vmem(ny + SUB), vmem(2 * groups)],
        [VMEM(index.shape, jnp.int32), VMEM(index.shape, F32), DMA((3,))],
        "first",
        1,
    )
    from_o = to_chip(send)
    from_e = to_core(send)
    big = [tx] + [
        flat(a)
        for a in (trans_y, trans_z, accel, coupling, upwind, storage, rhs_pressure, rhs_saturation, cross)
    ]
    made = call(
        functools.partial(setup_kernel, sizes),
        [perf_cell, perf_index] + big,
        [HBM] * (2 + len(big)),
        [vmem(rows)] * 11 + [vmem(3 * ny), vmem(groups * SUB), SMEM((groups,), jnp.int32)],
        [
            VMEM((padded, LANES), F32),
            VMEM((rows, LANES), F32),
            VMEM((rows, LANES), F32),
            SMEM(perf_cell.shape, jnp.int32),
            SMEM(perf_index.shape, F32),
            DMA((planes, 10)),
            DMA((2,)),
        ],
        "setup",
        4,
    )
    coefficients, (extra, weight, y) = list(made[:11]), made[11:]
    group_row = VMEM((groups, LANES), F32)
    fields = [vmem(padded), vmem(padded)]
    block = vmem(2 * ny + groups)
    slabs = vmem(groups * SUB)
    p, s, edge, plane_e, plane_o, wp, ws, shared, table, mu, sums, send_o = call(
        functools.partial(start_kernel, sizes),
        [y, from_o, from_e, wells, lines(well_rhs), lines(well_slot), coefficients[0]]
        + coefficients[5:]
        + [extra, weight],
        [SMEM] + [VMEM] * 3 + [HBM] * 2 + [VMEM] * 9,
        fields
        + [vmem(6 * ny), vmem(4 * ny), vmem(4 * ny), slabs, slabs, vmem(groups), vmem(TABLE * groups)]
        + [vmem(groups), vmem(groups), block],
        [
            group_row,
            VMEM(lines(well_rhs).shape, F32),
            VMEM(lines(well_slot).shape, jnp.int32),
            DMA((2,)),
        ],
        "start",
        2,
    )
    near = None
    for sweep in range(1, SWEEPS):
        final = sweep == SWEEPS - 1
        next_o = to_chip(send_o)
        first = sweep == 1
        _, _, p, s, by_lane, sums, send_e, *rest = call_vmem(
            lambda sz, *refs: inner_kernel(sz, first, *refs),
            [p, s, mu, wp, ws, weight, send_o, sums, table] + coefficients + [edge, plane_e, plane_o if first else from_e],
            fields + fields + [vmem(groups), vmem(groups), block] + ([vmem(4 * groups)] if first else []),
            [],
            "inner",
            2,
            {1: 0, 2: 1},
        )
        if first:
            near = rest[0]
        next_e = to_core(send_e)
        from_e, from_o = next_e, next_o
        half_o, near_o = call_vmem(
            facing_kernel, [from_o, p, s, plane_o, near], [block, vmem(groups)], [], "facing", 0.5
        )
        send_o, mu, sums = call_vmem(
            lambda sz, *refs: outer_kernel(sz, final, *refs),
            [half_o, from_o, from_e, by_lane, near_o, sums, table, wp, ws, shared, near],
            [block, vmem(groups), vmem(devices * SUB if final else groups)],
            [group_row],
            "outer",
            1,
            {1: 0},
        )
    grads = lax.all_to_all(sums.reshape(devices, SUB, LANES), "gx", 0, 0)
    result = pltpu.HBM((rows, nz), F32)
    _, _, p, s = call_vmem(
        final_kernel,
        [p, s, mu, wp, ws, plane_e, send_o, from_e],
        fields + [result, result],
        [VMEM((2 * ny + groups, LANES), F32), DMA((2,))],
        "final",
        2,
        {1: 0, 2: 1},
    )
    control = jnp.sum(grads, axis=(0, 1))[:groups]
    shape = trans_x.shape
    return p.reshape(shape), s.reshape(shape), control


def solution(mesh):
    grid = P(("ens", "gx"), None, None)
    line = P(("ens", "gx"))
    return jax.shard_map(
        body,
        mesh=mesh,
        in_specs=(grid,) * 10 + (line,) * 3 + (P("ens"), P("ens")),
        out_specs=(grid, grid, line),
        check_vma=False,
    )
```

```python
import functools

import jax
import jax.numpy as jnp
from jax import lax
from jax.experimental import pallas as pl
from jax.experimental.pallas import tpu as pltpu
from jax.sharding import PartitionSpec as P

SWEEPS = 6
SUB = 8
LANES = 128
F32 = jnp.float32
CHUNKS = 4


def vmem(rows):
    return pltpu.VMEM((rows, LANES), F32)


def placed(array, space):
    return array if space is pltpu.SMEM else pltpu.with_memory_space_constraint(array, space)


def spec(space):
    return pl.BlockSpec(memory_space=space)


def iota(shape, dim):
    return lax.broadcasted_iota(jnp.int32, shape, dim)


def lane_sum(block):
    return jnp.sum(block, axis=1, keepdims=True)


def spread(column, groups):
    return jnp.broadcast_to(column, (groups, LANES))


def row_of(column, groups):
    mine = iota((groups, LANES), 0) == iota((groups, LANES), 1)
    return jnp.sum(jnp.where(mine, column, 0.0), axis=0, keepdims=True)


def column_of(row, groups):
    mine = iota((groups, LANES), 0) == iota((groups, LANES), 1)
    return spread(lane_sum(jnp.where(mine, jnp.broadcast_to(row, (groups, LANES)), 0.0)), groups)


def well_block(part_own, part_before, groups):
    sub = iota((SUB, LANES), 0)
    own = jnp.broadcast_to(row_of(part_own, groups), (SUB, LANES))
    before = jnp.broadcast_to(row_of(part_before, groups), (SUB, LANES))
    return jnp.where(sub == 0, own, jnp.where(sub == 1, before, 0.0))


def group_rows(ref, groups, run):
    per_row = LANES // run
    return jnp.concatenate(
        [jnp.broadcast_to(ref[i : i + 1, :], (per_row, LANES)) for i in range(groups // per_row)], axis=0
    )


def first_kernel(sizes, tx_hbm, well_hbm, index_hbm, send_ref, wells_ref, well_ref, index_ref, sems):
    ny, groups, run = sizes.ny, sizes.groups, sizes.run
    plane = pltpu.make_async_copy(
        tx_hbm.at[pl.ds((sizes.planes - 1) * ny, ny)], send_ref.at[pl.ds(0, ny)], sems.at[0]
    )
    get_well = pltpu.make_async_copy(well_hbm, well_ref, sems.at[1])
    get_index = pltpu.make_async_copy(index_hbm, index_ref, sems.at[2])
    for copy in (get_well, get_index, plane):
        copy.start()
    place = lax.axis_index("gx")
    shape = (groups, LANES)
    per_row = LANES // run
    local = iota(shape, 0) % per_row
    lane = iota(shape, 1)
    get_well.wait()
    get_index.wait()
    weights = jnp.where(lane // run == local, group_rows(index_ref, groups, run), 0.0)
    total = lane_sum(weights)
    first = jnp.where(lane == local * run, group_rows(well_ref, groups, run).astype(F32), 0.0)
    well = lane_sum(first)
    before = well < (place * groups).astype(F32)
    before = spread(jnp.where(before, 1.0, 0.0), groups)
    total = spread(total, groups)
    wells_ref[0:groups, :] = before
    wells_ref[groups : 2 * groups, :] = total
    send_ref[ny : ny + SUB, :] = well_block(total * (1.0 - before), total * before, groups)
    plane.wait()


def setup_kernel(
    sizes,
    cell_hbm,
    index_hbm,
    tx_hbm,
    ty_hbm,
    tz_hbm,
    accel_hbm,
    coupling_hbm,
    upwind_hbm,
    storage_hbm,
    rhs_p_hbm,
    rhs_s_hbm,
    cross_hbm,
    tx_ref,
    ty_ref,
    tyl_ref,
    tz_ref,
    tzl_ref,
    rp_ref,
    ip_ref,
    cc_ref,
    rs_ref,
    uu_ref,
    xx_ref,
    extra_ref,
    weight_ref,
    y_ref,
    raw_tx,
    raw_ty,
    raw_tz,
    raw_accel,
    raw_coupling,
    raw_upwind,
    raw_storage,
    raw_rhs_p,
    raw_rhs_s,
    raw_cross,
    cwi_ref,
    cell_ref,
    index_ref,
    sems,
    fetch_sems,
):
    ny, planes, groups, run = sizes.ny, sizes.planes, sizes.groups, sizes.run
    rows = planes * ny
    part = ny // CHUNKS
    moves = [
        (tx_hbm, raw_tx),
        (ty_hbm, raw_ty),
        (tz_hbm, raw_tz),
        (accel_hbm, raw_accel),
        (coupling_hbm, raw_coupling),
        (upwind_hbm, raw_upwind),
        (storage_hbm, raw_storage),
        (rhs_p_hbm, raw_rhs_p),
        (rhs_s_hbm, raw_rhs_s),
        (cross_hbm, raw_cross),
    ]

    def copies(c):
        found = []
        for i, (src, dst) in enumerate(moves):
            start = pl.multiple_of(c * part, SUB)
            to = pl.multiple_of(start + SUB, SUB) if dst is raw_ty else start
            found.append(
                pltpu.make_async_copy(src.at[:, pl.ds(start, part)], dst.at[:, pl.ds(to, part)], sems.at[c, i])
            )
        return found

    fetches = [
        pltpu.make_async_copy(src, dst, fetch_sems.at[i])
        for i, (src, dst) in enumerate(((cell_hbm, cell_ref), (index_hbm, index_ref)))
    ]
    for fetch in fetches:
        fetch.start()
    for c in range(CHUNKS):
        for copy in copies(c):
            copy.start()

    last = lax.axis_index("gx") == lax.axis_size("gx") - 1
    keep_last = jnp.where(last, 0.0, 1.0)
    zero = jnp.zeros((SUB, LANES), F32)

    @pl.loop(0, rows // SUB, unroll=8)
    def _(i):
        cwi_ref[pl.ds(pl.multiple_of(i * SUB, SUB), SUB), :] = zero

    for fetch in fetches:
        fetch.wait()
    spot = iota((SUB, LANES), 0) * LANES + iota((SUB, LANES), 1)
    for g in range(groups):
        y_ref[g] = (cell_ref[g * run] // LANES) % ny
        weight = zero
        for k in range(g * run, (g + 1) * run):
            cell = cell_ref[k]
            at = (cell // (ny * LANES)) * LANES + cell % LANES
            weight = weight + jnp.where(spot == at, index_ref[k], 0.0)
        weight_ref[g * SUB : (g + 1) * SUB, :] = weight
        slab = pl.ds((cell_ref[g * run] // LANES) % ny, planes, ny)
        cwi_ref[slab, :] = cwi_ref[slab, :] + weight

    lane = iota((SUB, LANES), 1)
    sub = iota((SUB, LANES), 0)

    @pl.loop(0, CHUNKS)
    def _(c):
        for copy in copies(c):
            copy.wait()

        @pl.loop(0, part // SUB)
        def _(r):
            y0 = pl.multiple_of(c * part + r * SUB, SUB)
            ypos = sub + y0
            here = pl.ds(y0, SUB)
            txl = None
            for x in range(planes):
                at = pl.ds(y0 + x * ny, SUB)
                tx = raw_tx[x, here, :]
                if x == planes - 1:
                    tx = tx * keep_last
                tx_ref[at, :] = tx
                ty = jnp.where(ypos == ny - 1, 0.0, raw_ty[x, pl.ds(y0 + SUB, SUB), :])
                tyl = jnp.where(ypos == 0, 0.0, raw_ty[x, pl.ds(y0 + SUB - 1, SUB), :])
                tz = jnp.where(lane == LANES - 1, 0.0, raw_tz[x, here, :])
                tzl = pltpu.roll(tz, 1, 1)
                ty_ref[at, :] = ty
                tyl_ref[at, :] = tyl
                tz_ref[at, :] = tz
                tzl_ref[at, :] = tzl
                tsum = tx + ty + tyl + tz + tzl
                if x > 0:
                    tsum = tsum + txl
                accel = raw_accel[x, here, :]
                coupling = raw_coupling[x, here, :]
                upwind = raw_upwind[x, here, :]
                to_p = accel * (1.0 + jnp.abs(coupling))
                to_s = accel * jnp.abs(upwind)
                dp = to_p * tsum + accel * cwi_ref[at, :]
                ds = to_s * tsum + raw_storage[x, here, :]
                rhs_p, rhs_s, cross = raw_rhs_p[x, here, :], raw_rhs_s[x, here, :], raw_cross[x, here, :]
                if x == 0:
                    extra_ref[here, :] = to_p
                    extra_ref[pl.ds(y0 + ny, SUB), :] = to_s
                    extra_ref[pl.ds(y0 + 2 * ny, SUB), :] = ds
                    ip_ref[at, :] = dp
                    ip, is_ = 1.0, 1.0
                else:
                    ip = 1.0 / dp
                    is_ = 1.0 / ds
                    ip_ref[at, :] = ip
                cc_ref[at, :] = coupling * ip
                rp_ref[at, :] = rhs_p * ip
                rs_ref[at, :] = rhs_s * is_
                uu_ref[at, :] = upwind * is_
                xx_ref[at, :] = cross * is_
                txl = tx


def own_lanes(ref, place, groups):
    shape = (groups, LANES)
    start = place * groups
    row = jnp.broadcast_to(ref[pl.ds(start // LANES, 1), :].astype(F32), shape)
    mine = iota(shape, 1) == iota(shape, 0) + start % LANES
    return spread(lane_sum(jnp.where(mine, row, 0.0)), groups)


def clear_ends(rows, *refs):
    zero = jnp.zeros((SUB, LANES), F32)
    for ref in refs:
        ref[0:SUB, :] = zero
        ref[rows + SUB : rows + 2 * SUB, :] = zero


def path_y(sizes, cell_ref, g):
    return cell_ref[g]


def slab_of(sizes, cell_ref, g, pad):
    return pl.ds(path_y(sizes, cell_ref, g) + pad, sizes.planes, sizes.ny)


def add_wells(sizes, cell_ref, mu_ref, wp_ref, ws_ref, p_ref, s_ref, pad):
    for g in range(sizes.groups):
        slab = slab_of(sizes, cell_ref, g, pad)
        at = pl.ds(g * SUB, SUB)
        mu = mu_ref[g : g + 1, :]
        p_ref[slab, :] = p_ref[slab, :] + mu * wp_ref[at, :]
        s_ref[slab, :] = s_ref[slab, :] - mu * ws_ref[at, :]


def add_wells_to_plane(sizes, cell_ref, mu_ref, wp_ref, ws_ref, x, send_ref):
    for g in range(sizes.groups):
        y = path_y(sizes, cell_ref, g)
        in_p, in_s, at = pl.ds(y, 1), pl.ds(y + sizes.ny, 1), pl.ds(x + g * SUB, 1)
        mu = mu_ref[g : g + 1, :]
        send_ref[in_p, :] = send_ref[in_p, :] + mu * wp_ref[at, :]
        send_ref[in_s, :] = send_ref[in_s, :] - mu * ws_ref[at, :]


def path_rows(sizes, cell_ref, weight_ref, p_ref, rows_ref):
    for g in range(sizes.groups):
        slab = slab_of(sizes, cell_ref, g, SUB)
        at = pl.ds(g * SUB, SUB)
        rows_ref[g : g + 1, :] = jnp.sum(p_ref[slab, :] * weight_ref[at, :], axis=0, keepdims=True)


def facing(sizes, even):
    last = sizes.planes - 1
    return jnp.where(even, 0, last), jnp.where(even, last, 0)


def finish_plane(sizes, x, p_ref, s_ref, halo_ref, plane_ref, send_ref):
    ny = sizes.ny
    start = pl.multiple_of(x * ny + SUB, SUB)
    for r in range(0, ny, SUB):
        at = slice(r, r + SUB)
        at_s = slice(ny + r, ny + r + SUB)
        p, s = p_ref[pl.ds(start + r, SUB), :], s_ref[pl.ds(start + r, SUB), :]
        if halo_ref is not None:
            hp, hs = halo_ref[at, :], halo_ref[at_s, :]
            a, b, c, xx = [plane_ref[i * ny + r : i * ny + r + SUB, :] for i in range(4)]
            change = a * hp + b * hs
            p = p + change
            s = s + c * hs - xx * change
        send_ref[at, :] = p
        send_ref[at_s, :] = s


BEFORE, RHS_OWN, INV_OWN, SUM_OWN, RHS, INV, SLOT_OWN, SLOT_BEFORE, TABLE = range(9)


def shared_cells(sizes, cell_ref, weight_ref, wp_ref, out_ref):
    groups = sizes.groups
    shape = (groups, LANES)
    sub, lane = iota(shape, 0), iota(shape, 1)
    y_row = jnp.full(shape, -1, jnp.int32)
    y_col = y_row
    for g in range(groups):
        y = path_y(sizes, cell_ref, g)
        y_row = jnp.where(lane == g, y, y_row)
        y_col = jnp.where(sub == g, y, y_col)
    total = jnp.zeros(shape, F32)
    empty = jnp.zeros((LANES - groups, LANES), F32)
    for x in range(sizes.planes):
        at = pl.ds(x, groups, SUB)
        other = jnp.concatenate([wp_ref[at, :], empty], axis=0)
        total = total + lax.dot_general(
            weight_ref[at, :], other, (((1,), (1,)), ((), ())),
            precision=lax.Precision.HIGHEST, preferred_element_type=F32,
        )
    out_ref[...] = jnp.where(y_row == y_col, total, 0.0)


def start_kernel(
    sizes,
    cell_ref,
    from_o,
    from_e,
    wells_ref,
    rhs_hbm,
    slot_hbm,
    tx_ref,
    rp_ref,
    ip_ref,
    cc_ref,
    rs_ref,
    uu_ref,
    xx_ref,
    extra_ref,
    weight_ref,
    p_ref,
    s_ref,
    edge_ref,
    plane_e,
    plane_o,
    wp_ref,
    ws_ref,
    shared_ref,
    table_ref,
    mu_ref,
    sums_out,
    send_o,
    rows_ref,
    rhs_ref,
    slot_ref,
    sems,
):
    ny, planes, groups = sizes.ny, sizes.planes, sizes.groups
    rows = planes * ny
    place = lax.axis_index("gx")
    even = place % 2 == 0
    x_o, _ = facing(sizes, even)
    fetches = [
        pltpu.make_async_copy(rhs_hbm, rhs_ref, sems.at[0]),
        pltpu.make_async_copy(slot_hbm, slot_ref, sems.at[1]),
    ]
    for fetch in fetches:
        fetch.start()

    @pl.loop(0, ny // SUB)
    def _(r):
        y0 = pl.multiple_of(r * SUB, SUB)
        at = pl.ds(y0, SUB)
        txl = jnp.where(even, from_o[at, :], from_e[at, :])
        ip = 1.0 / (ip_ref[at, :] + extra_ref[at, :] * txl)
        is_ = 1.0 / (extra_ref[pl.ds(y0 + 2 * ny, SUB), :] + extra_ref[pl.ds(y0 + ny, SUB), :] * txl)
        cc, uu = cc_ref[at, :] * ip, uu_ref[at, :] * is_
        rp, rs, xx = rp_ref[at, :] * ip, rs_ref[at, :] * is_, xx_ref[at, :] * is_
        for i, value in enumerate([ip, cc, rp, rs, uu, xx]):
            edge_ref[pl.ds(y0 + i * ny, SUB), :] = value
        end = pl.ds(y0 + (planes - 1) * ny, SUB)
        tx = tx_ref[end, :]
        low = [ip * txl, cc * txl, uu * txl, xx]
        high = [ip_ref[end, :] * tx, cc_ref[end, :] * tx, uu_ref[end, :] * tx, xx_ref[end, :]]
        for i in range(4):
            to = pl.ds(y0 + i * ny, SUB)
            plane_o[to, :] = jnp.where(even, low[i], high[i])
            plane_e[to, :] = jnp.where(even, high[i], low[i])
        p_ref[pl.ds(y0 + SUB, SUB), :] = rp
        s_ref[pl.ds(y0 + SUB, SUB), :] = rs - xx * rp
        for x in range(1, planes):
            at = pl.ds(y0 + x * ny, SUB)
            to = pl.ds(y0 + (x * ny + SUB), SUB)
            rp = rp_ref[at, :]
            p_ref[to, :] = rp
            s_ref[to, :] = rs_ref[at, :] - xx_ref[at, :] * rp

    clear_ends(rows, p_ref, s_ref)
    sub = iota((SUB, LANES), 0)
    for g in range(groups):
        y = path_y(sizes, cell_ref, g)
        at = pl.ds(g * SUB, SUB)
        slab = pl.ds(y, planes, ny)
        ip = jnp.where(sub == 0, edge_ref[pl.ds(y, 1), :], ip_ref[slab, :])
        xx = jnp.where(sub == 0, edge_ref[pl.ds(y + 5 * ny, 1), :], xx_ref[slab, :])
        wp = weight_ref[at, :] * ip
        wp_ref[at, :] = wp
        ws_ref[at, :] = wp * xx
    shared_cells(sizes, cell_ref, weight_ref, wp_ref, shared_ref)

    tile_e, tile_o = from_e[ny : ny + SUB, :], from_o[ny : ny + SUB, :]
    low = jnp.where(even, tile_o, tile_e)
    high = jnp.where(even, tile_e, tile_o)
    before = wells_ref[0:groups, :]
    mine = wells_ref[groups : 2 * groups, :]
    is_before = before > 0.5
    sum_own = mine * (1.0 - before) + column_of(high[1:2, :], groups)
    sum_before = mine * before + column_of(low[0:1, :], groups)
    for fetch in fetches:
        fetch.wait()
    rhs_own = own_lanes(rhs_ref, place, groups)
    rhs_before = own_lanes(rhs_ref, jnp.maximum(place - 1, 0), groups)
    inv_own = 1.0 / (1.5 * sum_own + 0.5)
    inv_before = 1.0 / (1.5 * sum_before + 0.5)
    rhs = jnp.where(is_before, rhs_before, rhs_own)
    inv = jnp.where(is_before, inv_before, inv_own)
    entries = {
        BEFORE: before,
        RHS_OWN: rhs_own,
        INV_OWN: inv_own,
        SUM_OWN: sum_own,
        RHS: rhs,
        INV: inv,
        SLOT_OWN: own_lanes(slot_ref, place, groups),
        SLOT_BEFORE: own_lanes(slot_ref, jnp.maximum(place - 1, 0), groups),
    }
    for i, entry in entries.items():
        table_ref[i * groups : (i + 1) * groups, :] = entry
    mu = rhs * inv
    mu_ref[...] = mu

    finish_plane(sizes, x_o, p_ref, s_ref, None, None, send_o)
    add_wells_to_plane(sizes, cell_ref, mu_ref, wp_ref, ws_ref, x_o, send_o)
    path_rows(sizes, cell_ref, weight_ref, p_ref, rows_ref)
    put_sums(sizes, even, before, rows_ref[...] + shared_ref[...] * row_of(mu, groups), sums_out, send_o)


def put_sums(sizes, to_before, before, by_lane, rows_out, send_ref):
    ny, groups = sizes.ny, sizes.groups
    rows_out[...] = by_lane
    send_ref[2 * ny : 2 * ny + groups, :] = by_lane * jnp.where(to_before, before, 1.0 - before)


def finish_core_plane(sizes, cell_ref, p_ref, s_ref, mu_ref, wp_ref, ws_ref, halo, plane_e, send_e):
    even = lax.axis_index("gx") % 2 == 0
    _, x_e = facing(sizes, even)
    finish_plane(sizes, x_e, p_ref, s_ref, halo, plane_e, send_e)
    add_wells_to_plane(sizes, cell_ref, mu_ref, wp_ref, ws_ref, x_e, send_e)


def near_weights(sizes, cell_ref, weight_ref, plane_e, plane_o, near_ref):
    ny, groups = sizes.ny, sizes.groups
    even = lax.axis_index("gx") % 2 == 0
    x_o, x_e = facing(sizes, even)
    for g in range(groups):
        y = path_y(sizes, cell_ref, g)
        for i, (x, plane) in enumerate(((x_o, plane_o), (x_e, plane_e))):
            weight = weight_ref[pl.ds(x + g * SUB, 1), :]
            for j in range(2):
                to = (2 * i + j) * groups + g
                near_ref[to : to + 1, :] = weight * plane[pl.ds(y + j * ny, 1), :]


def put_planes(sizes, even, send_e, send_o, p_ref, s_ref, pad):
    ny = sizes.ny
    x_o, x_e = facing(sizes, even)
    for send, x in ((send_o, x_o), (send_e, x_e)):
        start = pl.multiple_of(x * ny + pad, SUB)
        for r in range(0, ny, SUB):
            p_ref[pl.ds(start + r, SUB), :] = send[r : r + SUB, :]
            s_ref[pl.ds(start + r, SUB), :] = send[ny + r : ny + r + SUB, :]


def inner_kernel(
    sizes,
    first,
    cell_ref,
    p_in,
    s_in,
    mu_ref,
    wp_ref,
    ws_ref,
    weight_ref,
    send_o,
    sums_in,
    table_ref,
    tx_ref,
    ty_ref,
    tyl_ref,
    tz_ref,
    tzl_ref,
    rp_ref,
    ip_ref,
    cc_ref,
    rs_ref,
    uu_ref,
    xx_ref,
    edge_ref,
    plane_e,
    *refs,
):
    ny, planes = sizes.ny, sizes.planes
    rows = planes * ny
    even = lax.axis_index("gx") % 2 == 0
    if first:
        plane_o, p_old, s_old, p_ref, s_ref, rows_ref, sums_out, send_e, near_ref = refs
        halo = None
        near_weights(sizes, cell_ref, weight_ref, plane_e, plane_o, near_ref)
    else:
        halo, p_old, s_old, p_ref, s_ref, rows_ref, sums_out, send_e = refs
    finish_core_plane(sizes, cell_ref, p_old, s_old, mu_ref, wp_ref, ws_ref, halo, plane_e, send_e)
    before = table_ref[BEFORE * sizes.groups : (BEFORE + 1) * sizes.groups, :]
    put_sums(sizes, jnp.logical_not(even), before, sums_in[...], sums_out, send_e)
    add_wells(sizes, cell_ref, mu_ref, wp_ref, ws_ref, p_old, s_old, SUB)
    put_planes(sizes, even, send_e, send_o, p_old, s_old, SUB)

    @pl.loop(0, ny // SUB)
    def _(r):
        y0 = pl.multiple_of(r * SUB, SUB)
        here = [pl.ds(y0 + (x * ny + SUB), SUB) for x in range(planes)]
        ps = [p_old[at, :] for at in here]
        ss = [s_old[at, :] for at in here]
        tx = None
        for x in range(planes):
            at = pl.ds(y0 + x * ny, SUB)
            up = pl.ds(y0 + (x * ny + SUB + 1), SUB)
            down = pl.ds(y0 + (x * ny + SUB - 1), SUB)
            txl = tx
            tx = tx_ref[at, :] if x < planes - 1 else None
            ty, tyl, tz, tzl = ty_ref[at, :], tyl_ref[at, :], tz_ref[at, :], tzl_ref[at, :]

            def neighbours(fields, old):
                mid = fields[x]
                total = tz * pltpu.roll(mid, LANES - 1, 1) + tzl * pltpu.roll(mid, 1, 1)
                total = total + (ty * old[up, :] + tyl * old[down, :])
                if x < planes - 1:
                    total = total + tx * fields[x + 1]
                if x > 0:
                    total = total + txl * fields[x - 1]
                return total

            sum_p = neighbours(ps, p_old)
            sum_s = neighbours(ss, s_old)
            if x == 0:
                ip, cc, rp, rs, uu, xx = [edge_ref[pl.ds(y0 + i * ny, SUB), :] for i in range(6)]
            else:
                ip, cc, rp, rs, uu, xx = [ref[at, :] for ref in (ip_ref, cc_ref, rp_ref, rs_ref, uu_ref, xx_ref)]
            p = rp + ip * sum_p + cc * sum_s
            p_ref[here[x], :] = p
            s_ref[here[x], :] = rs + uu * sum_s - xx * p

    clear_ends(rows, p_ref, s_ref)
    path_rows(sizes, cell_ref, weight_ref, p_ref, rows_ref)


def facing_kernel(sizes, cell_ref, from_o, p_ref, s_ref, plane_o, near_ref, send_o, sums_ref):
    even = lax.axis_index("gx") % 2 == 0
    x_o, _ = facing(sizes, even)
    finish_plane(sizes, x_o, p_ref, s_ref, from_o, plane_o, send_o)
    near_sums(sizes, cell_ref, from_o, near_ref, 0, sums_ref)


def near_sums(sizes, cell_ref, halo, near_ref, side, sums_ref):
    groups = sizes.groups
    for g in range(groups):
        y = path_y(sizes, cell_ref, g)
        row = jnp.zeros((1, LANES), F32)
        for j in range(2):
            at = (2 * side + j) * groups + g
            row = row + near_ref[at : at + 1, :] * halo[pl.ds(y + j * sizes.ny, 1), :]
        sums_ref[g : g + 1, :] = row


def outer_kernel(
    sizes,
    final,
    cell_ref,
    send_in,
    from_o,
    from_e,
    rows_ref,
    near_o,
    sums_in,
    table_ref,
    wp_ref,
    ws_ref,
    shared_ref,
    near_ref,
    send_o,
    mu_ref,
    *rest,
):
    ny, groups = sizes.ny, sizes.groups
    near_e = rest[-1]
    even = lax.axis_index("gx") % 2 == 0
    x_o, _ = facing(sizes, even)

    def table(i):
        return table_ref[i * groups : (i + 1) * groups, :]

    tail = slice(2 * ny, 2 * ny + groups)
    come_e, come_o = from_e[tail, :], from_o[tail, :]
    low = jnp.where(even, come_o, come_e)
    high = jnp.where(even, come_e, come_o)
    before = table(BEFORE)
    total = spread(lane_sum(sums_in[...] + jnp.where(before > 0.5, low, high)), groups)
    mu = (table(RHS) + total) * table(INV)
    mu_ref[...] = mu
    near_sums(sizes, cell_ref, from_e, near_ref, 1, near_e)
    by_lane = rows_ref[...] + near_o[...] + near_e[...] + shared_ref[...] * row_of(mu, groups)
    add_wells_to_plane(sizes, cell_ref, mu_ref, wp_ref, ws_ref, x_o, send_o)
    if not final:
        put_sums(sizes, even, before, by_lane, rest[0], send_o)
        return
    total_own = spread(lane_sum(sums_in[...] * (1.0 - before) + high), groups)
    total = spread(lane_sum(by_lane), groups)
    part_own, part_before = total * (1.0 - before), total * before
    grads_ref = rest[0]
    mu_own = (table(RHS_OWN) + total_own) * table(INV_OWN)
    grad_own = mu_own * table(SUM_OWN) - part_own
    grad_before = -part_before
    lane = iota((groups, LANES), 1)
    slot_own, slot_before = table(SLOT_OWN), table(SLOT_BEFORE)
    inside = lane < groups
    for d in range(sizes.devices):
        want = (lane + d * groups).astype(F32)
        own = jnp.where(inside & (slot_own == want), grad_own, 0.0)
        other = jnp.where(inside & (slot_before == want), grad_before, 0.0)
        row = jnp.sum(own + other, axis=0, keepdims=True)
        grads_ref[d * SUB : (d + 1) * SUB, :] = jnp.where(
            iota((SUB, LANES), 0) == 0, jnp.broadcast_to(row, (SUB, LANES)), 0.0
        )


def final_kernel(
    sizes,
    cell_ref,
    p_in,
    s_in,
    mu_ref,
    wp_ref,
    ws_ref,
    plane_e,
    send_o,
    from_e,
    p_old,
    s_old,
    p_out,
    s_out,
    send_e,
    sems,
):
    rows = sizes.planes * sizes.ny
    even = lax.axis_index("gx") % 2 == 0
    finish_core_plane(sizes, cell_ref, p_old, s_old, mu_ref, wp_ref, ws_ref, from_e, plane_e, send_e)
    add_wells(sizes, cell_ref, mu_ref, wp_ref, ws_ref, p_old, s_old, SUB)
    put_planes(sizes, even, send_e, send_o, p_old, s_old, SUB)
    copies = [
        pltpu.make_async_copy(field.at[pl.ds(SUB, rows)], out, sems.at[i])
        for i, (field, out) in enumerate(((p_old, p_out), (s_old, s_out)))
    ]
    for copy in copies:
        copy.start()
    for copy in copies:
        copy.wait()


class Sizes:
    def __init__(self, planes, ny, groups, run, devices):
        self.planes, self.ny, self.groups, self.run, self.devices = planes, ny, groups, run, devices


def body(
    rhs_pressure,
    rhs_saturation,
    trans_x,
    trans_y,
    trans_z,
    coupling,
    upwind,
    storage,
    cross,
    accel,
    perf_cell,
    perf_well,
    perf_index,
    well_rhs,
    well_slot,
):
    planes, ny, nz = trans_x.shape
    devices = lax.axis_size("gx")
    groups = well_rhs.shape[0] // devices
    run = perf_cell.shape[0] // groups
    sizes = Sizes(planes, ny, groups, run, devices)
    rows = planes * ny
    padded = rows + 2 * SUB
    SMEM, VMEM, HBM, DMA = pltpu.SMEM, pltpu.VMEM, pltpu.HBM, pltpu.SemaphoreType.DMA

    def flat(array):
        return array.reshape(rows, nz)

    def lines(array):
        return array.reshape(-1, LANES)

    def call(kernel, args, spaces, outs, scratch, name, micros, aliases=None):
        return pl.pallas_call(
            kernel,
            in_specs=[spec(space) for space in spaces],
            out_specs=[spec(out.memory_space) for out in outs],
            out_shape=outs,
            scratch_shapes=scratch,
            input_output_aliases=aliases or {},
            compiler_params=pltpu.CompilerParams(vmem_limit_bytes=16 * 1024 * 1024),
            cost_estimate=pl.CostEstimate(flops=int(micros * 4e6), bytes_accessed=int(micros * 3e6), transcendentals=0),
            name=name,
        )(*[placed(a, space) for a, space in zip(args, spaces)])

    def call_vmem(kernel, args, outs, scratch, name, micros, aliases=None):
        return call(
            functools.partial(kernel, sizes), [y] + args, [SMEM] + [VMEM] * len(args), outs, scratch,
            name, micros, aliases,
        )

    pairs_e = [(i, i ^ 1) for i in range(devices) if i ^ 1 < devices]
    pairs_o = []
    for i in range(1, devices - 1, 2):
        pairs_o += [(i, i + 1), (i + 1, i)]

    def to_core(block):
        return lax.ppermute(block, "gx", pairs_e)

    def to_chip(block):
        return lax.ppermute(block, "gx", pairs_o)

    index = lines(perf_index)
    send, wells = call(
        functools.partial(first_kernel, sizes),
        [flat(trans_x), lines(perf_well), index],
        [HBM, HBM, HBM],
        [vmem(ny + SUB), vmem(2 * groups)],
        [VMEM(index.shape, jnp.int32), VMEM(index.shape, F32), DMA((3,))],
        "first",
        1,
    )
    from_o = to_chip(send)
    from_e = to_core(send)
    big = [trans_x, trans_y, trans_z, accel, coupling, upwind, storage, rhs_pressure, rhs_saturation, cross]
    made = call(
        functools.partial(setup_kernel, sizes),
        [perf_cell, perf_index] + big,
        [HBM] * (2 + len(big)),
        [vmem(rows)] * 11 + [vmem(3 * ny), vmem(groups * SUB), SMEM((groups,), jnp.int32)],
        [
            VMEM((planes, ny, LANES), F32),
            VMEM((planes, ny + SUB, LANES), F32),
        ]
        + [VMEM((planes, ny, LANES), F32)] * 8
        + [
            VMEM((rows, LANES), F32),
            SMEM(perf_cell.shape, jnp.int32),
            SMEM(perf_index.shape, F32),
            DMA((CHUNKS, 10)),
            DMA((2,)),
        ],
        "setup",
        4,
    )
    coefficients, (extra, weight, y) = list(made[:11]), made[11:]
    group_row = VMEM((groups, LANES), F32)
    fields = [vmem(padded), vmem(padded)]
    block = vmem(2 * ny + groups)
    slabs = vmem(groups * SUB)
    p, s, edge, plane_e, plane_o, wp, ws, shared, table, mu, sums, send_o = call(
        functools.partial(start_kernel, sizes),
        [y, from_o, from_e, wells, lines(well_rhs), lines(well_slot), coefficients[0]]
        + coefficients[5:]
        + [extra, weight],
        [SMEM] + [VMEM] * 3 + [HBM] * 2 + [VMEM] * 9,
        fields
        + [vmem(6 * ny), vmem(4 * ny), vmem(4 * ny), slabs, slabs, vmem(groups), vmem(TABLE * groups)]
        + [vmem(groups), vmem(groups), block],
        [
            group_row,
            VMEM(lines(well_rhs).shape, F32),
            VMEM(lines(well_slot).shape, jnp.int32),
            DMA((2,)),
        ],
        "start",
        2,
    )
    near = None
    for sweep in range(1, SWEEPS):
        final = sweep == SWEEPS - 1
        next_o = to_chip(send_o)
        first = sweep == 1
        _, _, p, s, by_lane, sums, send_e, *rest = call_vmem(
            lambda sz, *refs: inner_kernel(sz, first, *refs),
            [p, s, mu, wp, ws, weight, send_o, sums, table] + coefficients + [edge, plane_e, plane_o if first else from_e],
            fields + fields + [vmem(groups), vmem(groups), block] + ([vmem(4 * groups)] if first else []),
            [],
            "inner",
            2,
            {1: 0, 2: 1},
        )
        if first:
            near = rest[0]
        next_e = to_core(send_e)
        from_e, from_o = next_e, next_o
        half_o, near_o = call_vmem(
            facing_kernel, [from_o, p, s, plane_o, near], [block, vmem(groups)], [], "facing", 0.5
        )
        send_o, mu, sums = call_vmem(
            lambda sz, *refs: outer_kernel(sz, final, *refs),
            [half_o, from_o, from_e, by_lane, near_o, sums, table, wp, ws, shared, near],
            [block, vmem(groups), vmem(devices * SUB if final else groups)],
            [group_row],
            "outer",
            1,
            {1: 0},
        )
    grads = lax.all_to_all(sums.reshape(devices, SUB, LANES), "gx", 0, 0)
    result = pltpu.HBM((rows, nz), F32)
    _, _, p, s = call_vmem(
        final_kernel,
        [p, s, mu, wp, ws, plane_e, send_o, from_e],
        fields + [result, result],
        [VMEM((2 * ny + groups, LANES), F32), DMA((2,))],
        "final",
        2,
        {1: 0, 2: 1},
    )
    control = jnp.sum(grads, axis=(0, 1))[:groups]
    shape = trans_x.shape
    return p.reshape(shape), s.reshape(shape), control


def solution(mesh):
    grid = P(("ens", "gx"), None, None)
    line = P(("ens", "gx"))
    return jax.shard_map(
        body,
        mesh=mesh,
        in_specs=(grid,) * 10 + (line,) * 3 + (P("ens"), P("ens")),
        out_specs=(grid, grid, line),
        check_vma=False,
    )
```

```python
import functools

import jax
import jax.numpy as jnp
from jax import lax
from jax.experimental import pallas as pl
from jax.experimental.pallas import tpu as pltpu
from jax.sharding import PartitionSpec as P

SWEEPS = 6
SUB = 8
LANES = 128
F32 = jnp.float32
CHUNKS = 4


def vmem(rows):
    return pltpu.VMEM((rows, LANES), F32)


def placed(array, space):
    return array if space is pltpu.SMEM else pltpu.with_memory_space_constraint(array, space)


def spec(space):
    return pl.BlockSpec(memory_space=space)


def iota(shape, dim):
    return lax.broadcasted_iota(jnp.int32, shape, dim)


def lane_sum(block):
    return jnp.sum(block, axis=1, keepdims=True)


def spread(column, groups):
    return jnp.broadcast_to(column, (groups, LANES))


def row_of(column, groups):
    mine = iota((groups, LANES), 0) == iota((groups, LANES), 1)
    return jnp.sum(jnp.where(mine, column, 0.0), axis=0, keepdims=True)


def column_of(row, groups):
    mine = iota((groups, LANES), 0) == iota((groups, LANES), 1)
    return spread(lane_sum(jnp.where(mine, jnp.broadcast_to(row, (groups, LANES)), 0.0)), groups)


def well_block(part_own, part_before, groups):
    sub = iota((SUB, LANES), 0)
    own = jnp.broadcast_to(row_of(part_own, groups), (SUB, LANES))
    before = jnp.broadcast_to(row_of(part_before, groups), (SUB, LANES))
    return jnp.where(sub == 0, own, jnp.where(sub == 1, before, 0.0))


def group_rows(ref, groups, run):
    per_row = LANES // run
    return jnp.concatenate(
        [jnp.broadcast_to(ref[i : i + 1, :], (per_row, LANES)) for i in range(groups // per_row)], axis=0
    )


def first_kernel(sizes, tx_hbm, well_hbm, index_hbm, send_ref, wells_ref, well_ref, index_ref, sems):
    ny, groups, run = sizes.ny, sizes.groups, sizes.run
    plane = pltpu.make_async_copy(
        tx_hbm.at[pl.ds((sizes.planes - 1) * ny, ny)], send_ref.at[pl.ds(0, ny)], sems.at[0]
    )
    get_well = pltpu.make_async_copy(well_hbm, well_ref, sems.at[1])
    get_index = pltpu.make_async_copy(index_hbm, index_ref, sems.at[2])
    for copy in (get_well, get_index, plane):
        copy.start()
    place = lax.axis_index("gx")
    shape = (groups, LANES)
    per_row = LANES // run
    local = iota(shape, 0) % per_row
    lane = iota(shape, 1)
    get_well.wait()
    get_index.wait()
    weights = jnp.where(lane // run == local, group_rows(index_ref, groups, run), 0.0)
    total = lane_sum(weights)
    first = jnp.where(lane == local * run, group_rows(well_ref, groups, run).astype(F32), 0.0)
    well = lane_sum(first)
    before = well < (place * groups).astype(F32)
    before = spread(jnp.where(before, 1.0, 0.0), groups)
    total = spread(total, groups)
    wells_ref[0:groups, :] = before
    wells_ref[groups : 2 * groups, :] = total
    send_ref[ny : ny + SUB, :] = well_block(total * (1.0 - before), total * before, groups)
    plane.wait()


def split_cell(cell, ny):
    if ny & (ny - 1):
        row = lax.div(cell, LANES)
        return lax.div(row, ny), lax.rem(row, ny), lax.rem(cell, LANES)
    bits_z, bits_y = LANES.bit_length() - 1, ny.bit_length() - 1
    row = lax.shift_right_logical(cell, bits_z)
    return lax.shift_right_logical(row, bits_y), row & (ny - 1), cell & (LANES - 1)


def setup_kernel(
    sizes,
    cell_hbm,
    index_hbm,
    tx_hbm,
    ty_hbm,
    tz_hbm,
    accel_hbm,
    coupling_hbm,
    upwind_hbm,
    storage_hbm,
    rhs_p_hbm,
    rhs_s_hbm,
    cross_hbm,
    tx_ref,
    ty_ref,
    tyl_ref,
    tz_ref,
    tzl_ref,
    rp_ref,
    ip_ref,
    cc_ref,
    rs_ref,
    uu_ref,
    xx_ref,
    extra_ref,
    weight_ref,
    y_ref,
    raw_tx,
    raw_ty,
    raw_tz,
    raw_accel,
    raw_coupling,
    raw_upwind,
    raw_storage,
    raw_rhs_p,
    raw_rhs_s,
    raw_cross,
    cwi_ref,
    cell_ref,
    index_ref,
    sems,
    fetch_sems,
):
    ny, planes, groups, run = sizes.ny, sizes.planes, sizes.groups, sizes.run
    rows = planes * ny
    part = ny // CHUNKS
    moves = [
        (tx_hbm, raw_tx),
        (ty_hbm, raw_ty),
        (tz_hbm, raw_tz),
        (accel_hbm, raw_accel),
        (coupling_hbm, raw_coupling),
        (upwind_hbm, raw_upwind),
        (storage_hbm, raw_storage),
        (rhs_p_hbm, raw_rhs_p),
        (rhs_s_hbm, raw_rhs_s),
        (cross_hbm, raw_cross),
    ]

    def copies(c):
        found = []
        for i, (src, dst) in enumerate(moves):
            start = pl.multiple_of(c * part, SUB)
            to = pl.multiple_of(start + SUB, SUB) if dst is raw_ty else start
            found.append(
                pltpu.make_async_copy(src.at[:, pl.ds(start, part)], dst.at[:, pl.ds(to, part)], sems.at[c, i])
            )
        return found

    fetches = [
        pltpu.make_async_copy(src, dst, fetch_sems.at[i])
        for i, (src, dst) in enumerate(((cell_hbm, cell_ref), (index_hbm, index_ref)))
    ]
    for fetch in fetches:
        fetch.start()
    for c in range(CHUNKS):
        for copy in copies(c):
            copy.start()

    last = lax.axis_index("gx") == lax.axis_size("gx") - 1
    keep_last = jnp.where(last, 0.0, 1.0)
    zero = jnp.zeros((SUB, LANES), F32)

    @pl.loop(0, rows // SUB, unroll=8)
    def _(i):
        cwi_ref[pl.ds(pl.multiple_of(i * SUB, SUB), SUB), :] = zero

    for fetch in fetches:
        fetch.wait()
    spot = iota((SUB, LANES), 0) * LANES + iota((SUB, LANES), 1)
    for g in range(groups):
        _, y, _ = split_cell(cell_ref[g * run], ny)
        y_ref[g] = y
        weight = zero
        for k in range(g * run, (g + 1) * run):
            x, _, z = split_cell(cell_ref[k], ny)
            weight = weight + jnp.where(spot == x * LANES + z, index_ref[k], 0.0)
        weight_ref[g * SUB : (g + 1) * SUB, :] = weight
        slab = pl.ds(y, planes, ny)
        cwi_ref[slab, :] = cwi_ref[slab, :] + weight

    lane = iota((SUB, LANES), 1)
    sub = iota((SUB, LANES), 0)

    @pl.loop(0, CHUNKS)
    def _(c):
        for copy in copies(c):
            copy.wait()

        @pl.loop(0, part // SUB)
        def _(r):
            y0 = pl.multiple_of(c * part + r * SUB, SUB)
            ypos = sub + y0
            here = pl.ds(y0, SUB)
            txl = None
            for x in range(planes):
                at = pl.ds(y0 + x * ny, SUB)
                tx = raw_tx[x, here, :]
                if x == planes - 1:
                    tx = tx * keep_last
                tx_ref[at, :] = tx
                ty = jnp.where(ypos == ny - 1, 0.0, raw_ty[x, pl.ds(y0 + SUB, SUB), :])
                tyl = jnp.where(ypos == 0, 0.0, raw_ty[x, pl.ds(y0 + SUB - 1, SUB), :])
                tz = jnp.where(lane == LANES - 1, 0.0, raw_tz[x, here, :])
                tzl = pltpu.roll(tz, 1, 1)
                ty_ref[at, :] = ty
                tyl_ref[at, :] = tyl
                tz_ref[at, :] = tz
                tzl_ref[at, :] = tzl
                tsum = tx + ty + tyl + tz + tzl
                if x > 0:
                    tsum = tsum + txl
                accel = raw_accel[x, here, :]
                coupling = raw_coupling[x, here, :]
                upwind = raw_upwind[x, here, :]
                to_p = accel * (1.0 + jnp.abs(coupling))
                to_s = accel * jnp.abs(upwind)
                dp = to_p * tsum + accel * cwi_ref[at, :]
                ds = to_s * tsum + raw_storage[x, here, :]
                rhs_p, rhs_s, cross = raw_rhs_p[x, here, :], raw_rhs_s[x, here, :], raw_cross[x, here, :]
                if x == 0:
                    extra_ref[here, :] = to_p
                    extra_ref[pl.ds(y0 + ny, SUB), :] = to_s
                    extra_ref[pl.ds(y0 + 2 * ny, SUB), :] = ds
                    ip_ref[at, :] = dp
                    ip, is_ = 1.0, 1.0
                else:
                    ip = 1.0 / dp
                    is_ = 1.0 / ds
                    ip_ref[at, :] = ip
                cc_ref[at, :] = coupling * ip
                rp_ref[at, :] = rhs_p * ip
                rs_ref[at, :] = rhs_s * is_
                uu_ref[at, :] = upwind * is_
                xx_ref[at, :] = cross * is_
                txl = tx


def own_lanes(ref, place, groups):
    shape = (groups, LANES)
    start = place * groups
    row = jnp.broadcast_to(ref[pl.ds(start // LANES, 1), :].astype(F32), shape)
    mine = iota(shape, 1) == iota(shape, 0) + start % LANES
    return spread(lane_sum(jnp.where(mine, row, 0.0)), groups)


def clear_ends(rows, *refs):
    zero = jnp.zeros((SUB, LANES), F32)
    for ref in refs:
        ref[0:SUB, :] = zero
        ref[rows + SUB : rows + 2 * SUB, :] = zero


def path_y(sizes, cell_ref, g):
    return cell_ref[g]


def slab_of(sizes, cell_ref, g, pad):
    return pl.ds(path_y(sizes, cell_ref, g) + pad, sizes.planes, sizes.ny)


def add_wells(sizes, cell_ref, mu_ref, wp_ref, ws_ref, p_ref, s_ref, pad):
    for g in range(sizes.groups):
        slab = slab_of(sizes, cell_ref, g, pad)
        at = pl.ds(g * SUB, SUB)
        mu = mu_ref[g : g + 1, :]
        p_ref[slab, :] = p_ref[slab, :] + mu * wp_ref[at, :]
        s_ref[slab, :] = s_ref[slab, :] - mu * ws_ref[at, :]


def add_wells_to_plane(sizes, cell_ref, mu_ref, wp_ref, ws_ref, x, send_ref):
    for g in range(sizes.groups):
        y = path_y(sizes, cell_ref, g)
        in_p, in_s, at = pl.ds(y, 1), pl.ds(y + sizes.ny, 1), pl.ds(x + g * SUB, 1)
        mu = mu_ref[g : g + 1, :]
        send_ref[in_p, :] = send_ref[in_p, :] + mu * wp_ref[at, :]
        send_ref[in_s, :] = send_ref[in_s, :] - mu * ws_ref[at, :]


def path_rows(sizes, cell_ref, weight_ref, p_ref, rows_ref):
    for g in range(sizes.groups):
        slab = slab_of(sizes, cell_ref, g, SUB)
        at = pl.ds(g * SUB, SUB)
        rows_ref[g : g + 1, :] = jnp.sum(p_ref[slab, :] * weight_ref[at, :], axis=0, keepdims=True)


def facing(sizes, even):
    last = sizes.planes - 1
    return jnp.where(even, 0, last), jnp.where(even, last, 0)


def finish_plane(sizes, x, p_ref, s_ref, halo_ref, plane_ref, send_ref):
    ny = sizes.ny
    start = pl.multiple_of(x * ny + SUB, SUB)
    for r in range(0, ny, SUB):
        at = slice(r, r + SUB)
        at_s = slice(ny + r, ny + r + SUB)
        p, s = p_ref[pl.ds(start + r, SUB), :], s_ref[pl.ds(start + r, SUB), :]
        if halo_ref is not None:
            hp, hs = halo_ref[at, :], halo_ref[at_s, :]
            a, b, c, xx = [plane_ref[i * ny + r : i * ny + r + SUB, :] for i in range(4)]
            change = a * hp + b * hs
            p = p + change
            s = s + c * hs - xx * change
        send_ref[at, :] = p
        send_ref[at_s, :] = s


BEFORE, RHS_OWN, INV_OWN, SUM_OWN, RHS, INV, SLOT_OWN, SLOT_BEFORE, TABLE = range(9)


def shared_cells(sizes, cell_ref, weight_ref, wp_ref, out_ref):
    groups = sizes.groups
    shape = (groups, LANES)
    sub, lane = iota(shape, 0), iota(shape, 1)
    y_row = jnp.full(shape, -1, jnp.int32)
    y_col = y_row
    for g in range(groups):
        y = path_y(sizes, cell_ref, g)
        y_row = jnp.where(lane == g, y, y_row)
        y_col = jnp.where(sub == g, y, y_col)
    total = jnp.zeros(shape, F32)
    empty = jnp.zeros((LANES - groups, LANES), F32)
    for x in range(sizes.planes):
        at = pl.ds(x, groups, SUB)
        other = jnp.concatenate([wp_ref[at, :], empty], axis=0)
        total = total + lax.dot_general(
            weight_ref[at, :], other, (((1,), (1,)), ((), ())),
            precision=lax.Precision.HIGHEST, preferred_element_type=F32,
        )
    out_ref[...] = jnp.where(y_row == y_col, total, 0.0)


def start_kernel(
    sizes,
    cell_ref,
    from_o,
    from_e,
    wells_ref,
    rhs_hbm,
    slot_hbm,
    tx_ref,
    rp_ref,
    ip_ref,
    cc_ref,
    rs_ref,
    uu_ref,
    xx_ref,
    extra_ref,
    weight_ref,
    p_ref,
    s_ref,
    edge_ref,
    plane_e,
    plane_o,
    wp_ref,
    ws_ref,
    shared_ref,
    table_ref,
    mu_ref,
    sums_out,
    send_o,
    rows_ref,
    rhs_ref,
    slot_ref,
    sems,
):
    ny, planes, groups = sizes.ny, sizes.planes, sizes.groups
    rows = planes * ny
    place = lax.axis_index("gx")
    even = place % 2 == 0
    x_o, _ = facing(sizes, even)
    fetches = [
        pltpu.make_async_copy(rhs_hbm, rhs_ref, sems.at[0]),
        pltpu.make_async_copy(slot_hbm, slot_ref, sems.at[1]),
    ]
    for fetch in fetches:
        fetch.start()

    @pl.loop(0, ny // SUB)
    def _(r):
        y0 = pl.multiple_of(r * SUB, SUB)
        at = pl.ds(y0, SUB)
        txl = jnp.where(even, from_o[at, :], from_e[at, :])
        ip = 1.0 / (ip_ref[at, :] + extra_ref[at, :] * txl)
        is_ = 1.0 / (extra_ref[pl.ds(y0 + 2 * ny, SUB), :] + extra_ref[pl.ds(y0 + ny, SUB), :] * txl)
        cc, uu = cc_ref[at, :] * ip, uu_ref[at, :] * is_
        rp, rs, xx = rp_ref[at, :] * ip, rs_ref[at, :] * is_, xx_ref[at, :] * is_
        for i, value in enumerate([ip, cc, rp, rs, uu, xx]):
            edge_ref[pl.ds(y0 + i * ny, SUB), :] = value
        end = pl.ds(y0 + (planes - 1) * ny, SUB)
        tx = tx_ref[end, :]
        low = [ip * txl, cc * txl, uu * txl, xx]
        high = [ip_ref[end, :] * tx, cc_ref[end, :] * tx, uu_ref[end, :] * tx, xx_ref[end, :]]
        for i in range(4):
            to = pl.ds(y0 + i * ny, SUB)
            plane_o[to, :] = jnp.where(even, low[i], high[i])
            plane_e[to, :] = jnp.where(even, high[i], low[i])
        p_ref[pl.ds(y0 + SUB, SUB), :] = rp
        s_ref[pl.ds(y0 + SUB, SUB), :] = rs - xx * rp
        for x in range(1, planes):
            at = pl.ds(y0 + x * ny, SUB)
            to = pl.ds(y0 + (x * ny + SUB), SUB)
            rp = rp_ref[at, :]
            p_ref[to, :] = rp
            s_ref[to, :] = rs_ref[at, :] - xx_ref[at, :] * rp

    clear_ends(rows, p_ref, s_ref)
    sub = iota((SUB, LANES), 0)
    for g in range(groups):
        y = path_y(sizes, cell_ref, g)
        at = pl.ds(g * SUB, SUB)
        slab = pl.ds(y, planes, ny)
        ip = jnp.where(sub == 0, edge_ref[pl.ds(y, 1), :], ip_ref[slab, :])
        xx = jnp.where(sub == 0, edge_ref[pl.ds(y + 5 * ny, 1), :], xx_ref[slab, :])
        wp = weight_ref[at, :] * ip
        wp_ref[at, :] = wp
        ws_ref[at, :] = wp * xx
    shared_cells(sizes, cell_ref, weight_ref, wp_ref, shared_ref)

    tile_e, tile_o = from_e[ny : ny + SUB, :], from_o[ny : ny + SUB, :]
    low = jnp.where(even, tile_o, tile_e)
    high = jnp.where(even, tile_e, tile_o)
    before = wells_ref[0:groups, :]
    mine = wells_ref[groups : 2 * groups, :]
    is_before = before > 0.5
    sum_own = mine * (1.0 - before) + column_of(high[1:2, :], groups)
    sum_before = mine * before + column_of(low[0:1, :], groups)
    for fetch in fetches:
        fetch.wait()
    rhs_own = own_lanes(rhs_ref, place, groups)
    rhs_before = own_lanes(rhs_ref, jnp.maximum(place - 1, 0), groups)
    inv_own = 1.0 / (1.5 * sum_own + 0.5)
    inv_before = 1.0 / (1.5 * sum_before + 0.5)
    rhs = jnp.where(is_before, rhs_before, rhs_own)
    inv = jnp.where(is_before, inv_before, inv_own)
    entries = {
        BEFORE: before,
        RHS_OWN: rhs_own,
        INV_OWN: inv_own,
        SUM_OWN: sum_own,
        RHS: rhs,
        INV: inv,
        SLOT_OWN: own_lanes(slot_ref, place, groups),
        SLOT_BEFORE: own_lanes(slot_ref, jnp.maximum(place - 1, 0), groups),
    }
    for i, entry in entries.items():
        table_ref[i * groups : (i + 1) * groups, :] = entry
    mu = rhs * inv
    mu_ref[...] = mu

    finish_plane(sizes, x_o, p_ref, s_ref, None, None, send_o)
    add_wells_to_plane(sizes, cell_ref, mu_ref, wp_ref, ws_ref, x_o, send_o)
    path_rows(sizes, cell_ref, weight_ref, p_ref, rows_ref)
    put_sums(sizes, even, before, rows_ref[...] + shared_ref[...] * row_of(mu, groups), sums_out, send_o)


def put_sums(sizes, to_before, before, by_lane, rows_out, send_ref):
    ny, groups = sizes.ny, sizes.groups
    rows_out[...] = by_lane
    shared = by_lane * jnp.where(to_before, before, 1.0 - before)
    parts = groups // SUB
    lane = iota((SUB, LANES), 1)
    tile = jnp.zeros((SUB, LANES), F32)
    for q in range(parts):
        part = shared[q * SUB : (q + 1) * SUB, :]
        width = LANES
        while width > LANES // parts:
            width //= 2
            part = part + pltpu.roll(part, width, 1)
        tile = jnp.where(lane // (LANES // parts) == q, part, tile)
    send_ref[2 * ny : 2 * ny + SUB, :] = tile


def rows_of(tile, groups):
    parts = groups // SUB
    lane = iota((SUB, LANES), 1)
    return jnp.concatenate(
        [jnp.where(lane // (LANES // parts) == q, tile, 0.0) for q in range(parts)], axis=0
    )


def finish_core_plane(sizes, cell_ref, p_ref, s_ref, mu_ref, wp_ref, ws_ref, halo, plane_e, send_e):
    even = lax.axis_index("gx") % 2 == 0
    _, x_e = facing(sizes, even)
    finish_plane(sizes, x_e, p_ref, s_ref, halo, plane_e, send_e)
    add_wells_to_plane(sizes, cell_ref, mu_ref, wp_ref, ws_ref, x_e, send_e)


def near_weights(sizes, cell_ref, weight_ref, plane_e, plane_o, near_ref):
    ny, groups = sizes.ny, sizes.groups
    even = lax.axis_index("gx") % 2 == 0
    x_o, x_e = facing(sizes, even)
    for g in range(groups):
        y = path_y(sizes, cell_ref, g)
        for i, (x, plane) in enumerate(((x_o, plane_o), (x_e, plane_e))):
            weight = weight_ref[pl.ds(x + g * SUB, 1), :]
            for j in range(2):
                to = (2 * i + j) * groups + g
                near_ref[to : to + 1, :] = weight * plane[pl.ds(y + j * ny, 1), :]


def put_planes(sizes, even, send_e, send_o, p_ref, s_ref, pad):
    ny = sizes.ny
    x_o, x_e = facing(sizes, even)
    for send, x in ((send_o, x_o), (send_e, x_e)):
        start = pl.multiple_of(x * ny + pad, SUB)
        for r in range(0, ny, SUB):
            p_ref[pl.ds(start + r, SUB), :] = send[r : r + SUB, :]
            s_ref[pl.ds(start + r, SUB), :] = send[ny + r : ny + r + SUB, :]


def inner_kernel(
    sizes,
    first,
    cell_ref,
    p_in,
    s_in,
    mu_ref,
    wp_ref,
    ws_ref,
    weight_ref,
    send_o,
    sums_in,
    table_ref,
    tx_ref,
    ty_ref,
    tyl_ref,
    tz_ref,
    tzl_ref,
    rp_ref,
    ip_ref,
    cc_ref,
    rs_ref,
    uu_ref,
    xx_ref,
    edge_ref,
    plane_e,
    *refs,
):
    ny, planes = sizes.ny, sizes.planes
    rows = planes * ny
    even = lax.axis_index("gx") % 2 == 0
    if first:
        plane_o, p_old, s_old, p_ref, s_ref, rows_ref, sums_out, send_e, near_ref = refs
        halo = None
        near_weights(sizes, cell_ref, weight_ref, plane_e, plane_o, near_ref)
    else:
        halo, p_old, s_old, p_ref, s_ref, rows_ref, sums_out, send_e = refs
    finish_core_plane(sizes, cell_ref, p_old, s_old, mu_ref, wp_ref, ws_ref, halo, plane_e, send_e)
    before = table_ref[BEFORE * sizes.groups : (BEFORE + 1) * sizes.groups, :]
    put_sums(sizes, jnp.logical_not(even), before, sums_in[...], sums_out, send_e)
    add_wells(sizes, cell_ref, mu_ref, wp_ref, ws_ref, p_old, s_old, SUB)
    put_planes(sizes, even, send_e, send_o, p_old, s_old, SUB)

    @pl.loop(0, ny // SUB)
    def _(r):
        y0 = pl.multiple_of(r * SUB, SUB)
        here = [pl.ds(y0 + (x * ny + SUB), SUB) for x in range(planes)]
        ps = [p_old[at, :] for at in here]
        ss = [s_old[at, :] for at in here]
        tx = None
        for x in range(planes):
            at = pl.ds(y0 + x * ny, SUB)
            up = pl.ds(y0 + (x * ny + SUB + 1), SUB)
            down = pl.ds(y0 + (x * ny + SUB - 1), SUB)
            txl = tx
            tx = tx_ref[at, :] if x < planes - 1 else None
            ty, tyl, tz, tzl = ty_ref[at, :], tyl_ref[at, :], tz_ref[at, :], tzl_ref[at, :]

            def neighbours(fields, old):
                mid = fields[x]
                total = tz * pltpu.roll(mid, LANES - 1, 1) + tzl * pltpu.roll(mid, 1, 1)
                total = total + (ty * old[up, :] + tyl * old[down, :])
                if x < planes - 1:
                    total = total + tx * fields[x + 1]
                if x > 0:
                    total = total + txl * fields[x - 1]
                return total

            sum_p = neighbours(ps, p_old)
            sum_s = neighbours(ss, s_old)
            if x == 0:
                ip, cc, rp, rs, uu, xx = [edge_ref[pl.ds(y0 + i * ny, SUB), :] for i in range(6)]
            else:
                ip, cc, rp, rs, uu, xx = [ref[at, :] for ref in (ip_ref, cc_ref, rp_ref, rs_ref, uu_ref, xx_ref)]
            p = rp + ip * sum_p + cc * sum_s
            p_ref[here[x], :] = p
            s_ref[here[x], :] = rs + uu * sum_s - xx * p

    clear_ends(rows, p_ref, s_ref)
    path_rows(sizes, cell_ref, weight_ref, p_ref, rows_ref)


def facing_kernel(sizes, cell_ref, from_o, p_ref, s_ref, plane_o, near_ref, send_o, sums_ref):
    even = lax.axis_index("gx") % 2 == 0
    x_o, _ = facing(sizes, even)
    finish_plane(sizes, x_o, p_ref, s_ref, from_o, plane_o, send_o)
    near_sums(sizes, cell_ref, from_o, near_ref, 0, sums_ref)


def near_sums(sizes, cell_ref, halo, near_ref, side, sums_ref):
    groups = sizes.groups
    for g in range(groups):
        y = path_y(sizes, cell_ref, g)
        row = jnp.zeros((1, LANES), F32)
        for j in range(2):
            at = (2 * side + j) * groups + g
            row = row + near_ref[at : at + 1, :] * halo[pl.ds(y + j * sizes.ny, 1), :]
        sums_ref[g : g + 1, :] = row


def outer_kernel(
    sizes,
    final,
    cell_ref,
    send_in,
    from_o,
    from_e,
    rows_ref,
    near_o,
    sums_in,
    table_ref,
    wp_ref,
    ws_ref,
    shared_ref,
    near_ref,
    send_o,
    mu_ref,
    *rest,
):
    ny, groups = sizes.ny, sizes.groups
    near_e = rest[-1]
    even = lax.axis_index("gx") % 2 == 0
    x_o, _ = facing(sizes, even)

    def table(i):
        return table_ref[i * groups : (i + 1) * groups, :]

    tail = slice(2 * ny, 2 * ny + SUB)
    come_e, come_o = from_e[tail, :], from_o[tail, :]
    low = rows_of(jnp.where(even, come_o, come_e), groups)
    high = rows_of(jnp.where(even, come_e, come_o), groups)
    before = table(BEFORE)
    total = spread(lane_sum(sums_in[...] + jnp.where(before > 0.5, low, high)), groups)
    mu = (table(RHS) + total) * table(INV)
    mu_ref[...] = mu
    near_sums(sizes, cell_ref, from_e, near_ref, 1, near_e)
    by_lane = rows_ref[...] + near_o[...] + near_e[...] + shared_ref[...] * row_of(mu, groups)
    add_wells_to_plane(sizes, cell_ref, mu_ref, wp_ref, ws_ref, x_o, send_o)
    if not final:
        put_sums(sizes, even, before, by_lane, rest[0], send_o)
        return
    total_own = spread(lane_sum(sums_in[...] * (1.0 - before) + high), groups)
    total = spread(lane_sum(by_lane), groups)
    part_own, part_before = total * (1.0 - before), total * before
    grads_ref = rest[0]
    mu_own = (table(RHS_OWN) + total_own) * table(INV_OWN)
    grad_own = mu_own * table(SUM_OWN) - part_own
    grad_before = -part_before
    lane = iota((SUB, LANES), 1).astype(F32)
    outside = lane >= groups
    values = []
    for slots, grad in ((table(SLOT_OWN), grad_own), (table(SLOT_BEFORE), grad_before)):
        for q in range(groups // SUB):
            part = slice(q * SUB, (q + 1) * SUB)
            values.append((jnp.where(outside, -1.0, slots[part, :] - lane), grad[part, :]))
    for d in range(sizes.devices):
        total = jnp.zeros((SUB, LANES), F32)
        for slot, grad in values:
            total = total + jnp.where(slot == float(d * groups), grad, 0.0)
        grads_ref[d * SUB : (d + 1) * SUB, :] = total


def final_kernel(
    sizes,
    cell_ref,
    p_in,
    s_in,
    mu_ref,
    wp_ref,
    ws_ref,
    plane_e,
    send_o,
    from_e,
    p_old,
    s_old,
    p_out,
    s_out,
    send_e,
    sems,
):
    rows = sizes.planes * sizes.ny
    even = lax.axis_index("gx") % 2 == 0
    finish_core_plane(sizes, cell_ref, p_old, s_old, mu_ref, wp_ref, ws_ref, from_e, plane_e, send_e)
    add_wells(sizes, cell_ref, mu_ref, wp_ref, ws_ref, p_old, s_old, SUB)
    put_planes(sizes, even, send_e, send_o, p_old, s_old, SUB)
    copies = [
        pltpu.make_async_copy(field.at[pl.ds(SUB, rows)], out, sems.at[i])
        for i, (field, out) in enumerate(((p_old, p_out), (s_old, s_out)))
    ]
    for copy in copies:
        copy.start()
    for copy in copies:
        copy.wait()


class Sizes:
    def __init__(self, planes, ny, groups, run, devices):
        self.planes, self.ny, self.groups, self.run, self.devices = planes, ny, groups, run, devices


def body(
    rhs_pressure,
    rhs_saturation,
    trans_x,
    trans_y,
    trans_z,
    coupling,
    upwind,
    storage,
    cross,
    accel,
    perf_cell,
    perf_well,
    perf_index,
    well_rhs,
    well_slot,
):
    planes, ny, nz = trans_x.shape
    devices = lax.axis_size("gx")
    groups = well_rhs.shape[0] // devices
    run = perf_cell.shape[0] // groups
    sizes = Sizes(planes, ny, groups, run, devices)
    rows = planes * ny
    padded = rows + 2 * SUB
    SMEM, VMEM, HBM, DMA = pltpu.SMEM, pltpu.VMEM, pltpu.HBM, pltpu.SemaphoreType.DMA

    def flat(array):
        return array.reshape(rows, nz)

    def lines(array):
        return array.reshape(-1, LANES)

    def call(kernel, args, spaces, outs, scratch, name, micros, aliases=None):
        return pl.pallas_call(
            kernel,
            in_specs=[spec(space) for space in spaces],
            out_specs=[spec(out.memory_space) for out in outs],
            out_shape=outs,
            scratch_shapes=scratch,
            input_output_aliases=aliases or {},
            compiler_params=pltpu.CompilerParams(vmem_limit_bytes=16 * 1024 * 1024),
            cost_estimate=pl.CostEstimate(flops=int(micros * 4e6), bytes_accessed=int(micros * 3e6), transcendentals=0),
            name=name,
        )(*[placed(a, space) for a, space in zip(args, spaces)])

    def call_vmem(kernel, args, outs, scratch, name, micros, aliases=None):
        return call(
            functools.partial(kernel, sizes), [y] + args, [SMEM] + [VMEM] * len(args), outs, scratch,
            name, micros, aliases,
        )

    pairs_e = [(i, i ^ 1) for i in range(devices) if i ^ 1 < devices]
    pairs_o = []
    for i in range(1, devices - 1, 2):
        pairs_o += [(i, i + 1), (i + 1, i)]

    def to_core(block):
        return lax.ppermute(block, "gx", pairs_e)

    def to_chip(block):
        return lax.ppermute(block, "gx", pairs_o)

    index = lines(perf_index)
    send, wells = call(
        functools.partial(first_kernel, sizes),
        [flat(trans_x), lines(perf_well), index],
        [HBM, HBM, HBM],
        [vmem(ny + SUB), vmem(2 * groups)],
        [VMEM(index.shape, jnp.int32), VMEM(index.shape, F32), DMA((3,))],
        "first",
        1,
    )
    from_o = to_chip(send)
    from_e = to_core(send)
    big = [trans_x, trans_y, trans_z, accel, coupling, upwind, storage, rhs_pressure, rhs_saturation, cross]
    made = call(
        functools.partial(setup_kernel, sizes),
        [perf_cell, perf_index] + big,
        [HBM] * (2 + len(big)),
        [vmem(rows)] * 11 + [vmem(3 * ny), vmem(groups * SUB), SMEM((groups,), jnp.int32)],
        [
            VMEM((planes, ny, LANES), F32),
            VMEM((planes, ny + SUB, LANES), F32),
        ]
        + [VMEM((planes, ny, LANES), F32)] * 8
        + [
            VMEM((rows, LANES), F32),
            SMEM(perf_cell.shape, jnp.int32),
            SMEM(perf_index.shape, F32),
            DMA((CHUNKS, 10)),
            DMA((2,)),
        ],
        "setup",
        4,
    )
    coefficients, (extra, weight, y) = list(made[:11]), made[11:]
    group_row = VMEM((groups, LANES), F32)
    fields = [vmem(padded), vmem(padded)]
    block = vmem(2 * ny + SUB)
    slabs = vmem(groups * SUB)
    p, s, edge, plane_e, plane_o, wp, ws, shared, table, mu, sums, send_o = call(
        functools.partial(start_kernel, sizes),
        [y, from_o, from_e, wells, lines(well_rhs), lines(well_slot), coefficients[0]]
        + coefficients[5:]
        + [extra, weight],
        [SMEM] + [VMEM] * 3 + [HBM] * 2 + [VMEM] * 9,
        fields
        + [vmem(6 * ny), vmem(4 * ny), vmem(4 * ny), slabs, slabs, vmem(groups), vmem(TABLE * groups)]
        + [vmem(groups), vmem(groups), block],
        [
            group_row,
            VMEM(lines(well_rhs).shape, F32),
            VMEM(lines(well_slot).shape, jnp.int32),
            DMA((2,)),
        ],
        "start",
        2,
    )
    near = None
    for sweep in range(1, SWEEPS):
        final = sweep == SWEEPS - 1
        next_o = to_chip(send_o)
        first = sweep == 1
        _, _, p, s, by_lane, sums, send_e, *rest = call_vmem(
            lambda sz, *refs: inner_kernel(sz, first, *refs),
            [p, s, mu, wp, ws, weight, send_o, sums, table] + coefficients + [edge, plane_e, plane_o if first else from_e],
            fields + fields + [vmem(groups), vmem(groups), block] + ([vmem(4 * groups)] if first else []),
            [],
            "inner",
            2,
            {1: 0, 2: 1},
        )
        if first:
            near = rest[0]
        next_e = to_core(send_e)
        from_e, from_o = next_e, next_o
        half_o, near_o = call_vmem(
            facing_kernel, [from_o, p, s, plane_o, near], [block, vmem(groups)], [], "facing", 0.5
        )
        send_o, mu, sums = call_vmem(
            lambda sz, *refs: outer_kernel(sz, final, *refs),
            [half_o, from_o, from_e, by_lane, near_o, sums, table, wp, ws, shared, near],
            [block, vmem(groups), vmem(devices * SUB if final else groups)],
            [group_row],
            "outer",
            1,
            {1: 0},
        )
    grads = lax.all_to_all(sums.reshape(devices, SUB, LANES), "gx", 0, 0)
    result = pltpu.HBM((rows, nz), F32)
    _, _, p, s = call_vmem(
        final_kernel,
        [p, s, mu, wp, ws, plane_e, send_o, from_e],
        fields + [result, result],
        [VMEM((2 * ny + SUB, LANES), F32), DMA((2,))],
        "final",
        2,
        {1: 0, 2: 1},
    )
    control = jnp.sum(grads, axis=(0, 1))[:groups]
    shape = trans_x.shape
    return p.reshape(shape), s.reshape(shape), control


def solution(mesh):
    grid = P(("ens", "gx"), None, None)
    line = P(("ens", "gx"))
    return jax.shard_map(
        body,
        mesh=mesh,
        in_specs=(grid,) * 10 + (line,) * 3 + (P("ens"), P("ens")),
        out_specs=(grid, grid, line),
        check_vma=False,
    )
```

```python
import functools

import jax
import jax.numpy as jnp
from jax import lax
from jax.experimental import pallas as pl
from jax.experimental.pallas import tpu as pltpu
from jax.sharding import PartitionSpec as P

SWEEPS = 6
SUB = 8
LANES = 128
F32 = jnp.float32
CHUNKS = 4


def vmem(rows):
    return pltpu.VMEM((rows, LANES), F32)


def placed(array, space):
    return array if space is pltpu.SMEM else pltpu.with_memory_space_constraint(array, space)


def spec(space):
    return pl.BlockSpec(memory_space=space)


def iota(shape, dim):
    return lax.broadcasted_iota(jnp.int32, shape, dim)


def lane_sum(block):
    return jnp.sum(block, axis=1, keepdims=True)


def spread(column, groups):
    return jnp.broadcast_to(column, (groups, LANES))


def row_of(column, groups):
    mine = iota((groups, LANES), 0) == iota((groups, LANES), 1)
    return jnp.sum(jnp.where(mine, column, 0.0), axis=0, keepdims=True)


def column_of(row, groups):
    mine = iota((groups, LANES), 0) == iota((groups, LANES), 1)
    return spread(lane_sum(jnp.where(mine, jnp.broadcast_to(row, (groups, LANES)), 0.0)), groups)


def well_block(part_own, part_before, groups):
    sub = iota((SUB, LANES), 0)
    own = jnp.broadcast_to(row_of(part_own, groups), (SUB, LANES))
    before = jnp.broadcast_to(row_of(part_before, groups), (SUB, LANES))
    return jnp.where(sub == 0, own, jnp.where(sub == 1, before, 0.0))


def group_rows(ref, groups, run):
    per_row = LANES // run
    return jnp.concatenate(
        [jnp.broadcast_to(ref[i : i + 1, :], (per_row, LANES)) for i in range(groups // per_row)], axis=0
    )


def first_kernel(sizes, tx_hbm, well_hbm, index_hbm, send_ref, wells_ref, well_ref, index_ref, sems):
    ny, groups, run = sizes.ny, sizes.groups, sizes.run
    plane = pltpu.make_async_copy(
        tx_hbm.at[pl.ds((sizes.planes - 1) * ny, ny)], send_ref.at[pl.ds(0, ny)], sems.at[0]
    )
    get_well = pltpu.make_async_copy(well_hbm, well_ref, sems.at[1])
    get_index = pltpu.make_async_copy(index_hbm, index_ref, sems.at[2])
    for copy in (get_well, get_index, plane):
        copy.start()
    place = lax.axis_index("gx")
    shape = (groups, LANES)
    per_row = LANES // run
    local = iota(shape, 0) % per_row
    lane = iota(shape, 1)
    get_well.wait()
    get_index.wait()
    weights = jnp.where(lane // run == local, group_rows(index_ref, groups, run), 0.0)
    total = lane_sum(weights)
    first = jnp.where(lane == local * run, group_rows(well_ref, groups, run).astype(F32), 0.0)
    well = lane_sum(first)
    before = well < (place * groups).astype(F32)
    before = spread(jnp.where(before, 1.0, 0.0), groups)
    total = spread(total, groups)
    wells_ref[0:groups, :] = before
    wells_ref[groups : 2 * groups, :] = total
    send_ref[ny : ny + SUB, :] = well_block(total * (1.0 - before), total * before, groups)
    plane.wait()


def split_cell(cell, ny):
    if ny & (ny - 1):
        row = lax.div(cell, LANES)
        return lax.div(row, ny), lax.rem(row, ny), lax.rem(cell, LANES)
    bits_z, bits_y = LANES.bit_length() - 1, ny.bit_length() - 1
    row = lax.shift_right_logical(cell, bits_z)
    return lax.shift_right_logical(row, bits_y), row & (ny - 1), cell & (LANES - 1)


def setup_kernel(
    sizes,
    cell_hbm,
    index_hbm,
    tx_hbm,
    ty_hbm,
    tz_hbm,
    accel_hbm,
    coupling_hbm,
    upwind_hbm,
    storage_hbm,
    rhs_p_hbm,
    rhs_s_hbm,
    cross_hbm,
    tx_ref,
    ty_ref,
    tyl_ref,
    tz_ref,
    tzl_ref,
    rp_ref,
    ip_ref,
    cc_ref,
    rs_ref,
    uu_ref,
    xx_ref,
    extra_ref,
    weight_ref,
    y_ref,
    raw_tx,
    raw_ty,
    raw_tz,
    raw_accel,
    raw_coupling,
    raw_upwind,
    raw_storage,
    raw_rhs_p,
    raw_rhs_s,
    raw_cross,
    cwi_ref,
    cell_ref,
    index_ref,
    sems,
    fetch_sems,
):
    ny, planes, groups, run = sizes.ny, sizes.planes, sizes.groups, sizes.run
    rows = planes * ny
    part = ny // CHUNKS
    moves = [
        (tx_hbm, raw_tx),
        (ty_hbm, raw_ty),
        (tz_hbm, raw_tz),
        (accel_hbm, raw_accel),
        (coupling_hbm, raw_coupling),
        (upwind_hbm, raw_upwind),
        (storage_hbm, raw_storage),
        (rhs_p_hbm, raw_rhs_p),
        (rhs_s_hbm, raw_rhs_s),
        (cross_hbm, raw_cross),
    ]

    def copies(c):
        found = []
        for i, (src, dst) in enumerate(moves):
            start = pl.multiple_of(c * part, SUB)
            to = pl.multiple_of(start + SUB, SUB) if dst is raw_ty else start
            found.append(
                pltpu.make_async_copy(src.at[:, pl.ds(start, part)], dst.at[:, pl.ds(to, part)], sems.at[c, i])
            )
        return found

    fetches = [
        pltpu.make_async_copy(src, dst, fetch_sems.at[i])
        for i, (src, dst) in enumerate(((cell_hbm, cell_ref), (index_hbm, index_ref)))
    ]
    for fetch in fetches:
        fetch.start()
    for c in range(CHUNKS):
        for copy in copies(c):
            copy.start()

    last = lax.axis_index("gx") == lax.axis_size("gx") - 1
    keep_last = jnp.where(last, 0.0, 1.0)
    zero = jnp.zeros((SUB, LANES), F32)

    @pl.loop(0, rows // SUB, unroll=8)
    def _(i):
        cwi_ref[pl.ds(pl.multiple_of(i * SUB, SUB), SUB), :] = zero

    for fetch in fetches:
        fetch.wait()
    spot = iota((SUB, LANES), 0) * LANES + iota((SUB, LANES), 1)
    for g in range(groups):
        _, y, _ = split_cell(cell_ref[g * run], ny)
        y_ref[g] = y
        weight = zero
        for k in range(g * run, (g + 1) * run):
            x, _, z = split_cell(cell_ref[k], ny)
            weight = weight + jnp.where(spot == x * LANES + z, index_ref[k], 0.0)
        weight_ref[g * SUB : (g + 1) * SUB, :] = weight
        slab = pl.ds(y, planes, ny)
        cwi_ref[slab, :] = cwi_ref[slab, :] + weight

    lane = iota((SUB, LANES), 1)
    sub = iota((SUB, LANES), 0)

    @pl.loop(0, CHUNKS)
    def _(c):
        for copy in copies(c):
            copy.wait()

        @pl.loop(0, part // SUB)
        def _(r):
            y0 = pl.multiple_of(c * part + r * SUB, SUB)
            ypos = sub + y0
            here = pl.ds(y0, SUB)
            txl = None
            for x in range(planes):
                at = pl.ds(y0 + x * ny, SUB)
                tx = raw_tx[x, here, :]
                if x == planes - 1:
                    tx = tx * keep_last
                tx_ref[at, :] = tx
                ty = jnp.where(ypos == ny - 1, 0.0, raw_ty[x, pl.ds(y0 + SUB, SUB), :])
                tyl = jnp.where(ypos == 0, 0.0, raw_ty[x, pl.ds(y0 + SUB - 1, SUB), :])
                tz = jnp.where(lane == LANES - 1, 0.0, raw_tz[x, here, :])
                tzl = pltpu.roll(tz, 1, 1)
                ty_ref[at, :] = ty
                tyl_ref[at, :] = tyl
                tz_ref[at, :] = tz
                tzl_ref[at, :] = tzl
                tsum = tx + ty + tyl + tz + tzl
                if x > 0:
                    tsum = tsum + txl
                accel = raw_accel[x, here, :]
                coupling = raw_coupling[x, here, :]
                upwind = raw_upwind[x, here, :]
                to_p = accel * (1.0 + jnp.abs(coupling))
                to_s = accel * jnp.abs(upwind)
                dp = to_p * tsum + accel * cwi_ref[at, :]
                ds = to_s * tsum + raw_storage[x, here, :]
                rhs_p, rhs_s, cross = raw_rhs_p[x, here, :], raw_rhs_s[x, here, :], raw_cross[x, here, :]
                if x == 0:
                    extra_ref[here, :] = to_p
                    extra_ref[pl.ds(y0 + ny, SUB), :] = to_s
                    extra_ref[pl.ds(y0 + 2 * ny, SUB), :] = ds
                    ip_ref[at, :] = dp
                    ip, is_ = 1.0, 1.0
                else:
                    ip = 1.0 / dp
                    is_ = 1.0 / ds
                    ip_ref[at, :] = ip
                cc_ref[at, :] = coupling * ip
                rp_ref[at, :] = rhs_p * ip
                rs_ref[at, :] = rhs_s * is_
                uu_ref[at, :] = upwind * is_
                xx_ref[at, :] = cross * is_
                txl = tx


def own_lanes(ref, place, groups):
    shape = (groups, LANES)
    start = place * groups
    row = jnp.broadcast_to(ref[pl.ds(start // LANES, 1), :].astype(F32), shape)
    mine = iota(shape, 1) == iota(shape, 0) + start % LANES
    return spread(lane_sum(jnp.where(mine, row, 0.0)), groups)


def clear_ends(rows, *refs):
    zero = jnp.zeros((SUB, LANES), F32)
    for ref in refs:
        ref[0:SUB, :] = zero
        ref[rows + SUB : rows + 2 * SUB, :] = zero


def path_y(sizes, cell_ref, g):
    return cell_ref[g]


def slab_of(sizes, cell_ref, g, pad):
    return pl.ds(path_y(sizes, cell_ref, g) + pad, sizes.planes, sizes.ny)


def add_wells(sizes, cell_ref, mu_ref, wp_ref, ws_ref, p_ref, s_ref, pad):
    for g in range(sizes.groups):
        slab = slab_of(sizes, cell_ref, g, pad)
        at = pl.ds(g * SUB, SUB)
        mu = mu_ref[g : g + 1, :]
        p_ref[slab, :] = p_ref[slab, :] + mu * wp_ref[at, :]
        s_ref[slab, :] = s_ref[slab, :] - mu * ws_ref[at, :]


def add_wells_to_plane(sizes, cell_ref, mu_ref, wp_ref, ws_ref, x, send_ref):
    for g in range(sizes.groups):
        y = path_y(sizes, cell_ref, g)
        in_p, in_s, at = pl.ds(y, 1), pl.ds(y + sizes.ny, 1), pl.ds(x + g * SUB, 1)
        mu = mu_ref[g : g + 1, :]
        send_ref[in_p, :] = send_ref[in_p, :] + mu * wp_ref[at, :]
        send_ref[in_s, :] = send_ref[in_s, :] - mu * ws_ref[at, :]


def path_rows(sizes, cell_ref, weight_ref, p_ref, rows_ref):
    for g in range(sizes.groups):
        slab = slab_of(sizes, cell_ref, g, SUB)
        at = pl.ds(g * SUB, SUB)
        rows_ref[g : g + 1, :] = jnp.sum(p_ref[slab, :] * weight_ref[at, :], axis=0, keepdims=True)


def facing(sizes, even):
    last = sizes.planes - 1
    return jnp.where(even, 0, last), jnp.where(even, last, 0)


def finish_plane(sizes, x, p_ref, s_ref, halo_ref, plane_ref, send_ref):
    ny = sizes.ny
    start = pl.multiple_of(x * ny + SUB, SUB)
    for r in range(0, ny, SUB):
        at = slice(r, r + SUB)
        at_s = slice(ny + r, ny + r + SUB)
        p, s = p_ref[pl.ds(start + r, SUB), :], s_ref[pl.ds(start + r, SUB), :]
        if halo_ref is not None:
            hp, hs = halo_ref[at, :], halo_ref[at_s, :]
            a, b, c, xx = [plane_ref[i * ny + r : i * ny + r + SUB, :] for i in range(4)]
            change = a * hp + b * hs
            p = p + change
            s = s + c * hs - xx * change
        send_ref[at, :] = p
        send_ref[at_s, :] = s


BEFORE, RHS_OWN, INV_OWN, SUM_OWN, RHS, INV, SLOT_OWN, SLOT_BEFORE, TABLE = range(9)


def shared_cells(sizes, cell_ref, weight_ref, wp_ref, out_ref):
    groups = sizes.groups
    shape = (groups, LANES)
    sub, lane = iota(shape, 0), iota(shape, 1)
    y_row = jnp.full(shape, -1, jnp.int32)
    y_col = y_row
    for g in range(groups):
        y = path_y(sizes, cell_ref, g)
        y_row = jnp.where(lane == g, y, y_row)
        y_col = jnp.where(sub == g, y, y_col)
    total = jnp.zeros(shape, F32)
    empty = jnp.zeros((LANES - groups, LANES), F32)
    for x in range(sizes.planes):
        at = pl.ds(x, groups, SUB)
        other = jnp.concatenate([wp_ref[at, :], empty], axis=0)
        total = total + lax.dot_general(
            weight_ref[at, :], other, (((1,), (1,)), ((), ())),
            precision=lax.Precision.HIGHEST, preferred_element_type=F32,
        )
    out_ref[...] = jnp.where(y_row == y_col, total, 0.0)


def start_kernel(
    sizes,
    cell_ref,
    from_o,
    from_e,
    wells_ref,
    rhs_hbm,
    slot_hbm,
    tx_ref,
    rp_ref,
    ip_ref,
    cc_ref,
    rs_ref,
    uu_ref,
    xx_ref,
    extra_ref,
    weight_ref,
    p_ref,
    s_ref,
    edge_ref,
    plane_e,
    plane_o,
    wp_ref,
    ws_ref,
    shared_ref,
    table_ref,
    mu_ref,
    sums_out,
    send_o,
    rows_ref,
    rhs_ref,
    slot_ref,
    sems,
):
    ny, planes, groups = sizes.ny, sizes.planes, sizes.groups
    rows = planes * ny
    place = lax.axis_index("gx")
    even = place % 2 == 0
    x_o, _ = facing(sizes, even)
    fetches = [
        pltpu.make_async_copy(rhs_hbm, rhs_ref, sems.at[0]),
        pltpu.make_async_copy(slot_hbm, slot_ref, sems.at[1]),
    ]
    for fetch in fetches:
        fetch.start()

    @pl.loop(0, ny // SUB)
    def _(r):
        y0 = pl.multiple_of(r * SUB, SUB)
        at = pl.ds(y0, SUB)
        txl = jnp.where(even, from_o[at, :], from_e[at, :])
        ip = 1.0 / (ip_ref[at, :] + extra_ref[at, :] * txl)
        is_ = 1.0 / (extra_ref[pl.ds(y0 + 2 * ny, SUB), :] + extra_ref[pl.ds(y0 + ny, SUB), :] * txl)
        cc, uu = cc_ref[at, :] * ip, uu_ref[at, :] * is_
        rp, rs, xx = rp_ref[at, :] * ip, rs_ref[at, :] * is_, xx_ref[at, :] * is_
        for i, value in enumerate([ip, cc, rp, rs, uu, xx]):
            edge_ref[pl.ds(y0 + i * ny, SUB), :] = value
        end = pl.ds(y0 + (planes - 1) * ny, SUB)
        tx = tx_ref[end, :]
        low = [ip * txl, cc * txl, uu * txl, xx]
        high = [ip_ref[end, :] * tx, cc_ref[end, :] * tx, uu_ref[end, :] * tx, xx_ref[end, :]]
        for i in range(4):
            to = pl.ds(y0 + i * ny, SUB)
            plane_o[to, :] = jnp.where(even, low[i], high[i])
            plane_e[to, :] = jnp.where(even, high[i], low[i])
        p_ref[pl.ds(y0 + SUB, SUB), :] = rp
        s_ref[pl.ds(y0 + SUB, SUB), :] = rs - xx * rp
        for x in range(1, planes):
            at = pl.ds(y0 + x * ny, SUB)
            to = pl.ds(y0 + (x * ny + SUB), SUB)
            rp = rp_ref[at, :]
            p_ref[to, :] = rp
            s_ref[to, :] = rs_ref[at, :] - xx_ref[at, :] * rp

    clear_ends(rows, p_ref, s_ref)
    sub = iota((SUB, LANES), 0)
    for g in range(groups):
        y = path_y(sizes, cell_ref, g)
        at = pl.ds(g * SUB, SUB)
        slab = pl.ds(y, planes, ny)
        ip = jnp.where(sub == 0, edge_ref[pl.ds(y, 1), :], ip_ref[slab, :])
        xx = jnp.where(sub == 0, edge_ref[pl.ds(y + 5 * ny, 1), :], xx_ref[slab, :])
        wp = weight_ref[at, :] * ip
        wp_ref[at, :] = wp
        ws_ref[at, :] = wp * xx
    shared_cells(sizes, cell_ref, weight_ref, wp_ref, shared_ref)

    tile_e, tile_o = from_e[ny : ny + SUB, :], from_o[ny : ny + SUB, :]
    low = jnp.where(even, tile_o, tile_e)
    high = jnp.where(even, tile_e, tile_o)
    before = wells_ref[0:groups, :]
    mine = wells_ref[groups : 2 * groups, :]
    is_before = before > 0.5
    sum_own = mine * (1.0 - before) + column_of(high[1:2, :], groups)
    sum_before = mine * before + column_of(low[0:1, :], groups)
    for fetch in fetches:
        fetch.wait()
    rhs_own = own_lanes(rhs_ref, place, groups)
    rhs_before = own_lanes(rhs_ref, jnp.maximum(place - 1, 0), groups)
    inv_own = 1.0 / (1.5 * sum_own + 0.5)
    inv_before = 1.0 / (1.5 * sum_before + 0.5)
    rhs = jnp.where(is_before, rhs_before, rhs_own)
    inv = jnp.where(is_before, inv_before, inv_own)
    entries = {
        BEFORE: before,
        RHS_OWN: rhs_own,
        INV_OWN: inv_own,
        SUM_OWN: sum_own,
        RHS: rhs,
        INV: inv,
        SLOT_OWN: own_lanes(slot_ref, place, groups),
        SLOT_BEFORE: own_lanes(slot_ref, jnp.maximum(place - 1, 0), groups),
    }
    for i, entry in entries.items():
        table_ref[i * groups : (i + 1) * groups, :] = entry
    mu = rhs * inv
    mu_ref[...] = mu

    finish_plane(sizes, x_o, p_ref, s_ref, None, None, send_o)
    add_wells_to_plane(sizes, cell_ref, mu_ref, wp_ref, ws_ref, x_o, send_o)
    path_rows(sizes, cell_ref, weight_ref, p_ref, rows_ref)
    put_sums(sizes, even, before, rows_ref[...] + shared_ref[...] * row_of(mu, groups), sums_out, send_o)


def put_sums(sizes, to_before, before, by_lane, rows_out, send_ref):
    ny, groups = sizes.ny, sizes.groups
    rows_out[...] = by_lane
    shared = by_lane * jnp.where(to_before, before, 1.0 - before)
    parts = groups // SUB
    lane = iota((SUB, LANES), 1)
    tile = jnp.zeros((SUB, LANES), F32)
    for q in range(parts):
        part = shared[q * SUB : (q + 1) * SUB, :]
        width = LANES
        while width > LANES // parts:
            width //= 2
            part = part + pltpu.roll(part, width, 1)
        tile = jnp.where(lane // (LANES // parts) == q, part, tile)
    send_ref[2 * ny : 2 * ny + SUB, :] = tile


def rows_of(tile, groups):
    parts = groups // SUB
    lane = iota((SUB, LANES), 1)
    return jnp.concatenate(
        [jnp.where(lane // (LANES // parts) == q, tile, 0.0) for q in range(parts)], axis=0
    )


def finish_core_plane(sizes, cell_ref, p_ref, s_ref, mu_ref, wp_ref, ws_ref, halo, plane_e, send_e):
    even = lax.axis_index("gx") % 2 == 0
    _, x_e = facing(sizes, even)
    finish_plane(sizes, x_e, p_ref, s_ref, halo, plane_e, send_e)
    add_wells_to_plane(sizes, cell_ref, mu_ref, wp_ref, ws_ref, x_e, send_e)


def near_weights(sizes, cell_ref, weight_ref, plane_e, plane_o, near_ref):
    ny, groups = sizes.ny, sizes.groups
    even = lax.axis_index("gx") % 2 == 0
    x_o, x_e = facing(sizes, even)
    for g in range(groups):
        y = path_y(sizes, cell_ref, g)
        for i, (x, plane) in enumerate(((x_o, plane_o), (x_e, plane_e))):
            weight = weight_ref[pl.ds(x + g * SUB, 1), :]
            for j in range(2):
                to = (2 * i + j) * groups + g
                near_ref[to : to + 1, :] = weight * plane[pl.ds(y + j * ny, 1), :]


def put_planes(sizes, even, send_e, send_o, p_ref, s_ref, pad):
    ny = sizes.ny
    x_o, x_e = facing(sizes, even)
    for send, x in ((send_o, x_o), (send_e, x_e)):
        start = pl.multiple_of(x * ny + pad, SUB)
        for r in range(0, ny, SUB):
            p_ref[pl.ds(start + r, SUB), :] = send[r : r + SUB, :]
            s_ref[pl.ds(start + r, SUB), :] = send[ny + r : ny + r + SUB, :]


def inner_kernel(
    sizes,
    first,
    cell_ref,
    p_in,
    s_in,
    mu_ref,
    wp_ref,
    ws_ref,
    weight_ref,
    send_o,
    sums_in,
    table_ref,
    tx_ref,
    ty_ref,
    tyl_ref,
    tz_ref,
    tzl_ref,
    rp_ref,
    ip_ref,
    cc_ref,
    rs_ref,
    uu_ref,
    xx_ref,
    edge_ref,
    plane_e,
    *refs,
):
    ny, planes = sizes.ny, sizes.planes
    rows = planes * ny
    even = lax.axis_index("gx") % 2 == 0
    if first:
        plane_o, p_old, s_old, p_ref, s_ref, rows_ref, sums_out, send_e, near_ref = refs
        halo = None
        near_weights(sizes, cell_ref, weight_ref, plane_e, plane_o, near_ref)
    else:
        halo, p_old, s_old, p_ref, s_ref, rows_ref, sums_out, send_e = refs
    finish_core_plane(sizes, cell_ref, p_old, s_old, mu_ref, wp_ref, ws_ref, halo, plane_e, send_e)
    before = table_ref[BEFORE * sizes.groups : (BEFORE + 1) * sizes.groups, :]
    put_sums(sizes, jnp.logical_not(even), before, sums_in[...], sums_out, send_e)
    add_wells(sizes, cell_ref, mu_ref, wp_ref, ws_ref, p_old, s_old, SUB)
    put_planes(sizes, even, send_e, send_o, p_old, s_old, SUB)

    @pl.loop(0, ny // SUB)
    def _(r):
        y0 = pl.multiple_of(r * SUB, SUB)
        here = [pl.ds(y0 + (x * ny + SUB), SUB) for x in range(planes)]
        ps = [p_old[at, :] for at in here]
        ss = [s_old[at, :] for at in here]
        tx = None
        for x in range(planes):
            at = pl.ds(y0 + x * ny, SUB)
            up = pl.ds(y0 + (x * ny + SUB + 1), SUB)
            down = pl.ds(y0 + (x * ny + SUB - 1), SUB)
            txl = tx
            tx = tx_ref[at, :] if x < planes - 1 else None
            ty, tyl, tz, tzl = ty_ref[at, :], tyl_ref[at, :], tz_ref[at, :], tzl_ref[at, :]

            def neighbours(fields, old):
                mid = fields[x]
                total = tz * pltpu.roll(mid, LANES - 1, 1) + tzl * pltpu.roll(mid, 1, 1)
                total = total + (ty * old[up, :] + tyl * old[down, :])
                if x < planes - 1:
                    total = total + tx * fields[x + 1]
                if x > 0:
                    total = total + txl * fields[x - 1]
                return total

            sum_p = neighbours(ps, p_old)
            sum_s = neighbours(ss, s_old)
            if x == 0:
                ip, cc, rp, rs, uu, xx = [edge_ref[pl.ds(y0 + i * ny, SUB), :] for i in range(6)]
            else:
                ip, cc, rp, rs, uu, xx = [ref[at, :] for ref in (ip_ref, cc_ref, rp_ref, rs_ref, uu_ref, xx_ref)]
            p = rp + ip * sum_p + cc * sum_s
            p_ref[here[x], :] = p
            s_ref[here[x], :] = rs + uu * sum_s - xx * p

    clear_ends(rows, p_ref, s_ref)
    path_rows(sizes, cell_ref, weight_ref, p_ref, rows_ref)


def facing_kernel(sizes, cell_ref, from_o, p_ref, s_ref, plane_o, near_ref, send_o, sums_ref):
    even = lax.axis_index("gx") % 2 == 0
    x_o, _ = facing(sizes, even)
    finish_plane(sizes, x_o, p_ref, s_ref, from_o, plane_o, send_o)
    near_sums(sizes, cell_ref, from_o, near_ref, 0, sums_ref)


def near_sums(sizes, cell_ref, halo, near_ref, side, sums_ref):
    groups = sizes.groups
    for g in range(groups):
        y = path_y(sizes, cell_ref, g)
        row = jnp.zeros((1, LANES), F32)
        for j in range(2):
            at = (2 * side + j) * groups + g
            row = row + near_ref[at : at + 1, :] * halo[pl.ds(y + j * sizes.ny, 1), :]
        sums_ref[g : g + 1, :] = row


def outer_kernel(
    sizes,
    final,
    cell_ref,
    send_in,
    from_o,
    from_e,
    rows_ref,
    near_o,
    sums_in,
    table_ref,
    wp_ref,
    ws_ref,
    shared_ref,
    near_ref,
    send_o,
    mu_ref,
    *rest,
):
    ny, groups = sizes.ny, sizes.groups
    near_e = rest[-1]
    even = lax.axis_index("gx") % 2 == 0
    x_o, _ = facing(sizes, even)

    def table(i):
        return table_ref[i * groups : (i + 1) * groups, :]

    tail = slice(2 * ny, 2 * ny + SUB)
    come_e, come_o = from_e[tail, :], from_o[tail, :]
    low = rows_of(jnp.where(even, come_o, come_e), groups)
    high = rows_of(jnp.where(even, come_e, come_o), groups)
    before = table(BEFORE)
    total = spread(lane_sum(sums_in[...] + jnp.where(before > 0.5, low, high)), groups)
    mu = (table(RHS) + total) * table(INV)
    mu_ref[...] = mu
    near_sums(sizes, cell_ref, from_e, near_ref, 1, near_e)
    by_lane = rows_ref[...] + near_o[...] + near_e[...] + shared_ref[...] * row_of(mu, groups)
    add_wells_to_plane(sizes, cell_ref, mu_ref, wp_ref, ws_ref, x_o, send_o)
    if not final:
        put_sums(sizes, even, before, by_lane, rest[0], send_o)
        return
    total_own = spread(lane_sum(sums_in[...] * (1.0 - before) + high), groups)
    total = spread(lane_sum(by_lane), groups)
    part_own, part_before = total * (1.0 - before), total * before
    grads_ref = rest[0]
    mu_own = (table(RHS_OWN) + total_own) * table(INV_OWN)
    grad_own = mu_own * table(SUM_OWN) - part_own
    grad_before = -part_before
    lane = iota((SUB, LANES), 1).astype(F32)
    outside = lane >= groups
    values = []
    for slots, grad in ((table(SLOT_OWN), grad_own), (table(SLOT_BEFORE), grad_before)):
        for q in range(groups // SUB):
            part = slice(q * SUB, (q + 1) * SUB)
            values.append((jnp.where(outside, -1.0, slots[part, :] - lane), grad[part, :]))
    for d in range(sizes.devices):
        total = jnp.zeros((SUB, LANES), F32)
        for slot, grad in values:
            total = total + jnp.where(slot == float(d * groups), grad, 0.0)
        grads_ref[d] = jnp.sum(total, axis=0, keepdims=True)


def final_kernel(
    sizes,
    cell_ref,
    p_in,
    s_in,
    mu_ref,
    wp_ref,
    ws_ref,
    plane_e,
    send_o,
    from_e,
    p_old,
    s_old,
    p_out,
    s_out,
    send_e,
    sems,
):
    rows = sizes.planes * sizes.ny
    even = lax.axis_index("gx") % 2 == 0
    finish_core_plane(sizes, cell_ref, p_old, s_old, mu_ref, wp_ref, ws_ref, from_e, plane_e, send_e)
    add_wells(sizes, cell_ref, mu_ref, wp_ref, ws_ref, p_old, s_old, SUB)
    put_planes(sizes, even, send_e, send_o, p_old, s_old, SUB)
    copies = [
        pltpu.make_async_copy(field.at[pl.ds(SUB, rows)], out, sems.at[i])
        for i, (field, out) in enumerate(((p_old, p_out), (s_old, s_out)))
    ]
    for copy in copies:
        copy.start()
    for copy in copies:
        copy.wait()


class Sizes:
    def __init__(self, planes, ny, groups, run, devices):
        self.planes, self.ny, self.groups, self.run, self.devices = planes, ny, groups, run, devices


def body(
    rhs_pressure,
    rhs_saturation,
    trans_x,
    trans_y,
    trans_z,
    coupling,
    upwind,
    storage,
    cross,
    accel,
    perf_cell,
    perf_well,
    perf_index,
    well_rhs,
    well_slot,
):
    planes, ny, nz = trans_x.shape
    devices = lax.axis_size("gx")
    groups = well_rhs.shape[0] // devices
    run = perf_cell.shape[0] // groups
    sizes = Sizes(planes, ny, groups, run, devices)
    rows = planes * ny
    padded = rows + 2 * SUB
    SMEM, VMEM, HBM, DMA = pltpu.SMEM, pltpu.VMEM, pltpu.HBM, pltpu.SemaphoreType.DMA

    def flat(array):
        return array.reshape(rows, nz)

    def lines(array):
        return array.reshape(-1, LANES)

    def call(kernel, args, spaces, outs, scratch, name, micros, aliases=None):
        return pl.pallas_call(
            kernel,
            in_specs=[spec(space) for space in spaces],
            out_specs=[spec(out.memory_space) for out in outs],
            out_shape=outs,
            scratch_shapes=scratch,
            input_output_aliases=aliases or {},
            compiler_params=pltpu.CompilerParams(vmem_limit_bytes=16 * 1024 * 1024),
            cost_estimate=pl.CostEstimate(flops=int(micros * 4e6), bytes_accessed=int(micros * 3e6), transcendentals=0),
            name=name,
        )(*[placed(a, space) for a, space in zip(args, spaces)])

    def call_vmem(kernel, args, outs, scratch, name, micros, aliases=None):
        return call(
            functools.partial(kernel, sizes), [y] + args, [SMEM] + [VMEM] * len(args), outs, scratch,
            name, micros, aliases,
        )

    pairs_e = [(i, i ^ 1) for i in range(devices) if i ^ 1 < devices]
    pairs_o = []
    for i in range(1, devices - 1, 2):
        pairs_o += [(i, i + 1), (i + 1, i)]

    def to_core(block):
        return lax.ppermute(block, "gx", pairs_e)

    def to_chip(block):
        return lax.ppermute(block, "gx", pairs_o)

    index = lines(perf_index)
    send, wells = call(
        functools.partial(first_kernel, sizes),
        [flat(trans_x), lines(perf_well), index],
        [HBM, HBM, HBM],
        [vmem(ny + SUB), vmem(2 * groups)],
        [VMEM(index.shape, jnp.int32), VMEM(index.shape, F32), DMA((3,))],
        "first",
        1,
    )
    from_o = to_chip(send)
    from_e = to_core(send)
    big = [trans_x, trans_y, trans_z, accel, coupling, upwind, storage, rhs_pressure, rhs_saturation, cross]
    made = call(
        functools.partial(setup_kernel, sizes),
        [perf_cell, perf_index] + big,
        [HBM] * (2 + len(big)),
        [vmem(rows)] * 11 + [vmem(3 * ny), vmem(groups * SUB), SMEM((groups,), jnp.int32)],
        [
            VMEM((planes, ny, LANES), F32),
            VMEM((planes, ny + SUB, LANES), F32),
        ]
        + [VMEM((planes, ny, LANES), F32)] * 8
        + [
            VMEM((rows, LANES), F32),
            SMEM(perf_cell.shape, jnp.int32),
            SMEM(perf_index.shape, F32),
            DMA((CHUNKS, 10)),
            DMA((2,)),
        ],
        "setup",
        4,
    )
    coefficients, (extra, weight, y) = list(made[:11]), made[11:]
    group_row = VMEM((groups, LANES), F32)
    fields = [vmem(padded), vmem(padded)]
    block = vmem(2 * ny + SUB)
    slabs = vmem(groups * SUB)
    p, s, edge, plane_e, plane_o, wp, ws, shared, table, mu, sums, send_o = call(
        functools.partial(start_kernel, sizes),
        [y, from_o, from_e, wells, lines(well_rhs), lines(well_slot), coefficients[0]]
        + coefficients[5:]
        + [extra, weight],
        [SMEM] + [VMEM] * 3 + [HBM] * 2 + [VMEM] * 9,
        fields
        + [vmem(6 * ny), vmem(4 * ny), vmem(4 * ny), slabs, slabs, vmem(groups), vmem(TABLE * groups)]
        + [vmem(groups), vmem(groups), block],
        [
            group_row,
            VMEM(lines(well_rhs).shape, F32),
            VMEM(lines(well_slot).shape, jnp.int32),
            DMA((2,)),
        ],
        "start",
        2,
    )
    near = None
    for sweep in range(1, SWEEPS):
        final = sweep == SWEEPS - 1
        next_o = to_chip(send_o)
        first = sweep == 1
        _, _, p, s, by_lane, sums, send_e, *rest = call_vmem(
            lambda sz, *refs: inner_kernel(sz, first, *refs),
            [p, s, mu, wp, ws, weight, send_o, sums, table] + coefficients + [edge, plane_e, plane_o if first else from_e],
            fields + fields + [vmem(groups), vmem(groups), block] + ([vmem(4 * groups)] if first else []),
            [],
            "inner",
            2,
            {1: 0, 2: 1},
        )
        if first:
            near = rest[0]
        next_e = to_core(send_e)
        from_e, from_o = next_e, next_o
        half_o, near_o = call_vmem(
            facing_kernel, [from_o, p, s, plane_o, near], [block, vmem(groups)], [], "facing", 0.5
        )
        send_o, mu, sums = call_vmem(
            lambda sz, *refs: outer_kernel(sz, final, *refs),
            [half_o, from_o, from_e, by_lane, near_o, sums, table, wp, ws, shared, near],
            [block, vmem(groups), pltpu.VMEM((devices, 1, LANES), F32) if final else vmem(groups)],
            [group_row],
            "outer",
            1,
            {1: 0},
        )
    grads = lax.all_to_all(sums, "gx", 0, 0)
    result = pltpu.HBM((rows, nz), F32)
    _, _, p, s = call_vmem(
        final_kernel,
        [p, s, mu, wp, ws, plane_e, send_o, from_e],
        fields + [result, result],
        [VMEM((2 * ny + SUB, LANES), F32), DMA((2,))],
        "final",
        2,
        {1: 0, 2: 1},
    )
    control = jnp.sum(grads, axis=(0, 1))[:groups]
    shape = trans_x.shape
    return p.reshape(shape), s.reshape(shape), control


def solution(mesh):
    grid = P(("ens", "gx"), None, None)
    line = P(("ens", "gx"))
    return jax.shard_map(
        body,
        mesh=mesh,
        in_specs=(grid,) * 10 + (line,) * 3 + (P("ens"), P("ens")),
        out_specs=(grid, grid, line),
        check_vma=False,
    )
```

```python
import functools

import jax
import jax.numpy as jnp
from jax import lax
from jax.experimental import pallas as pl
from jax.experimental.pallas import tpu as pltpu
from jax.sharding import PartitionSpec as P

SWEEPS = 6
SUB = 8
LANES = 128
F32 = jnp.float32
CHUNKS = 4


def vmem(rows):
    return pltpu.VMEM((rows, LANES), F32)


def placed(array, space):
    return array if space is pltpu.SMEM else pltpu.with_memory_space_constraint(array, space)


def spec(space):
    return pl.BlockSpec(memory_space=space)


def iota(shape, dim):
    return lax.broadcasted_iota(jnp.int32, shape, dim)


def lane_sum(block):
    return jnp.sum(block, axis=1, keepdims=True)


def spread(column, groups):
    return jnp.broadcast_to(column, (groups, LANES))


def row_of(column, groups):
    mine = iota((groups, LANES), 0) == iota((groups, LANES), 1)
    return jnp.sum(jnp.where(mine, column, 0.0), axis=0, keepdims=True)


def column_of(row, groups):
    mine = iota((groups, LANES), 0) == iota((groups, LANES), 1)
    return spread(lane_sum(jnp.where(mine, jnp.broadcast_to(row, (groups, LANES)), 0.0)), groups)


def well_block(part_own, part_before, groups):
    sub = iota((SUB, LANES), 0)
    own = jnp.broadcast_to(row_of(part_own, groups), (SUB, LANES))
    before = jnp.broadcast_to(row_of(part_before, groups), (SUB, LANES))
    return jnp.where(sub == 0, own, jnp.where(sub == 1, before, 0.0))


def group_rows(ref, groups, run):
    per_row = LANES // run
    return jnp.concatenate(
        [jnp.broadcast_to(ref[i : i + 1, :], (per_row, LANES)) for i in range(groups // per_row)], axis=0
    )


def first_kernel(sizes, tx_hbm, well_hbm, index_hbm, send_ref, wells_ref, well_ref, index_ref, sems):
    ny, groups, run = sizes.ny, sizes.groups, sizes.run
    plane = pltpu.make_async_copy(
        tx_hbm.at[pl.ds((sizes.planes - 1) * ny, ny)], send_ref.at[pl.ds(0, ny)], sems.at[0]
    )
    get_well = pltpu.make_async_copy(well_hbm, well_ref, sems.at[1])
    get_index = pltpu.make_async_copy(index_hbm, index_ref, sems.at[2])
    for copy in (get_well, get_index, plane):
        copy.start()
    place = lax.axis_index("gx")
    shape = (groups, LANES)
    per_row = LANES // run
    local = iota(shape, 0) % per_row
    lane = iota(shape, 1)
    get_well.wait()
    get_index.wait()
    weights = jnp.where(lane // run == local, group_rows(index_ref, groups, run), 0.0)
    total = lane_sum(weights)
    first = jnp.where(lane == local * run, group_rows(well_ref, groups, run).astype(F32), 0.0)
    well = lane_sum(first)
    before = well < (place * groups).astype(F32)
    before = spread(jnp.where(before, 1.0, 0.0), groups)
    total = spread(total, groups)
    wells_ref[0:groups, :] = before
    wells_ref[groups : 2 * groups, :] = total
    send_ref[ny : ny + SUB, :] = well_block(total * (1.0 - before), total * before, groups)
    plane.wait()


def split_cell(cell, ny):
    if ny & (ny - 1):
        row = lax.div(cell, LANES)
        return lax.div(row, ny), lax.rem(row, ny), lax.rem(cell, LANES)
    bits_z, bits_y = LANES.bit_length() - 1, ny.bit_length() - 1
    row = lax.shift_right_logical(cell, bits_z)
    return lax.shift_right_logical(row, bits_y), row & (ny - 1), cell & (LANES - 1)


def setup_kernel(
    sizes,
    cell_hbm,
    index_hbm,
    tx_hbm,
    ty_hbm,
    tz_hbm,
    accel_hbm,
    coupling_hbm,
    upwind_hbm,
    storage_hbm,
    rhs_p_hbm,
    rhs_s_hbm,
    cross_hbm,
    tx_ref,
    ty_ref,
    tyl_ref,
    tz_ref,
    tzl_ref,
    rp_ref,
    ip_ref,
    cc_ref,
    rs_ref,
    uu_ref,
    xx_ref,
    extra_ref,
    weight_ref,
    y_ref,
    raw_tx,
    raw_ty,
    raw_tz,
    raw_accel,
    raw_coupling,
    raw_upwind,
    raw_storage,
    raw_rhs_p,
    raw_rhs_s,
    raw_cross,
    cwi_ref,
    cell_ref,
    index_ref,
    sems,
    fetch_sems,
):
    ny, planes, groups, run = sizes.ny, sizes.planes, sizes.groups, sizes.run
    rows = planes * ny
    part = ny // CHUNKS
    moves = [
        (tx_hbm, raw_tx),
        (ty_hbm, raw_ty),
        (tz_hbm, raw_tz),
        (accel_hbm, raw_accel),
        (coupling_hbm, raw_coupling),
        (upwind_hbm, raw_upwind),
        (storage_hbm, raw_storage),
        (rhs_p_hbm, raw_rhs_p),
        (rhs_s_hbm, raw_rhs_s),
        (cross_hbm, raw_cross),
    ]

    def copies(c):
        found = []
        for i, (src, dst) in enumerate(moves):
            start = pl.multiple_of(c * part, SUB)
            to = pl.multiple_of(start + SUB, SUB) if dst is raw_ty else start
            found.append(
                pltpu.make_async_copy(src.at[:, pl.ds(start, part)], dst.at[:, pl.ds(to, part)], sems.at[c, i])
            )
        return found

    fetches = [
        pltpu.make_async_copy(src, dst, fetch_sems.at[i])
        for i, (src, dst) in enumerate(((cell_hbm, cell_ref), (index_hbm, index_ref)))
    ]
    for fetch in fetches:
        fetch.start()
    for c in range(CHUNKS):
        for copy in copies(c):
            copy.start()

    last = lax.axis_index("gx") == lax.axis_size("gx") - 1
    keep_last = jnp.where(last, 0.0, 1.0)
    zero = jnp.zeros((SUB, LANES), F32)

    @pl.loop(0, rows // SUB, unroll=8)
    def _(i):
        cwi_ref[pl.ds(pl.multiple_of(i * SUB, SUB), SUB), :] = zero

    for fetch in fetches:
        fetch.wait()
    spot = iota((SUB, LANES), 0) * LANES + iota((SUB, LANES), 1)
    for g in range(groups):
        _, y, _ = split_cell(cell_ref[g * run], ny)
        y_ref[g] = y
        weight = zero
        for k in range(g * run, (g + 1) * run):
            x, _, z = split_cell(cell_ref[k], ny)
            weight = weight + jnp.where(spot == x * LANES + z, index_ref[k], 0.0)
        weight_ref[g * SUB : (g + 1) * SUB, :] = weight
        slab = pl.ds(y, planes, ny)
        cwi_ref[slab, :] = cwi_ref[slab, :] + weight

    lane = iota((SUB, LANES), 1)
    sub = iota((SUB, LANES), 0)

    @pl.loop(0, CHUNKS)
    def _(c):
        for copy in copies(c):
            copy.wait()

        @pl.loop(0, part // SUB)
        def _(r):
            y0 = pl.multiple_of(c * part + r * SUB, SUB)
            ypos = sub + y0
            here = pl.ds(y0, SUB)
            txl = None
            for x in range(planes):
                at = pl.ds(y0 + x * ny, SUB)
                tx = raw_tx[x, here, :]
                if x == planes - 1:
                    tx = tx * keep_last
                tx_ref[at, :] = tx
                ty = jnp.where(ypos == ny - 1, 0.0, raw_ty[x, pl.ds(y0 + SUB, SUB), :])
                tyl = jnp.where(ypos == 0, 0.0, raw_ty[x, pl.ds(y0 + SUB - 1, SUB), :])
                tz = jnp.where(lane == LANES - 1, 0.0, raw_tz[x, here, :])
                tzl = pltpu.roll(tz, 1, 1)
                ty_ref[at, :] = ty
                tyl_ref[at, :] = tyl
                tz_ref[at, :] = tz
                tzl_ref[at, :] = tzl
                tsum = tx + ty + tyl + tz + tzl
                if x > 0:
                    tsum = tsum + txl
                accel = raw_accel[x, here, :]
                coupling = raw_coupling[x, here, :]
                upwind = raw_upwind[x, here, :]
                to_p = accel * (1.0 + jnp.abs(coupling))
                to_s = accel * jnp.abs(upwind)
                dp = to_p * tsum + accel * cwi_ref[at, :]
                ds = to_s * tsum + raw_storage[x, here, :]
                rhs_p, rhs_s, cross = raw_rhs_p[x, here, :], raw_rhs_s[x, here, :], raw_cross[x, here, :]
                if x == 0:
                    extra_ref[here, :] = to_p
                    extra_ref[pl.ds(y0 + ny, SUB), :] = to_s
                    extra_ref[pl.ds(y0 + 2 * ny, SUB), :] = ds
                    ip_ref[at, :] = dp
                    ip, is_ = 1.0, 1.0
                else:
                    ip = 1.0 / dp
                    is_ = 1.0 / ds
                    ip_ref[at, :] = ip
                cc_ref[at, :] = coupling * ip
                rp_ref[at, :] = rhs_p * ip
                rs_ref[at, :] = rhs_s * is_
                uu_ref[at, :] = upwind * is_
                xx_ref[at, :] = cross * is_
                txl = tx


def own_lanes(ref, place, groups):
    shape = (groups, LANES)
    start = place * groups
    row = jnp.broadcast_to(ref[pl.ds(start // LANES, 1), :].astype(F32), shape)
    mine = iota(shape, 1) == iota(shape, 0) + start % LANES
    return spread(lane_sum(jnp.where(mine, row, 0.0)), groups)


def clear_ends(rows, *refs):
    zero = jnp.zeros((SUB, LANES), F32)
    for ref in refs:
        ref[0:SUB, :] = zero
        ref[rows + SUB : rows + 2 * SUB, :] = zero


def path_y(sizes, cell_ref, g):
    return cell_ref[g]


def slab_of(sizes, cell_ref, g, pad):
    return pl.ds(path_y(sizes, cell_ref, g) + pad, sizes.planes, sizes.ny)


def add_wells(sizes, cell_ref, mu_ref, wp_ref, ws_ref, p_ref, s_ref, pad):
    for g in range(sizes.groups):
        slab = slab_of(sizes, cell_ref, g, pad)
        at = pl.ds(g * SUB, SUB)
        mu = mu_ref[g : g + 1, :]
        p_ref[slab, :] = p_ref[slab, :] + mu * wp_ref[at, :]
        s_ref[slab, :] = s_ref[slab, :] - mu * ws_ref[at, :]


def add_wells_to_plane(sizes, cell_ref, mu_ref, wp_ref, ws_ref, x, send_ref):
    for g in range(sizes.groups):
        y = path_y(sizes, cell_ref, g)
        in_p, in_s, at = pl.ds(y, 1), pl.ds(y + sizes.ny, 1), pl.ds(x + g * SUB, 1)
        mu = mu_ref[g : g + 1, :]
        send_ref[in_p, :] = send_ref[in_p, :] + mu * wp_ref[at, :]
        send_ref[in_s, :] = send_ref[in_s, :] - mu * ws_ref[at, :]


def path_rows(sizes, cell_ref, weight_ref, p_ref, rows_ref):
    for g in range(sizes.groups):
        slab = slab_of(sizes, cell_ref, g, SUB)
        at = pl.ds(g * SUB, SUB)
        rows_ref[g : g + 1, :] = jnp.sum(p_ref[slab, :] * weight_ref[at, :], axis=0, keepdims=True)


def facing(sizes, even):
    last = sizes.planes - 1
    return jnp.where(even, 0, last), jnp.where(even, last, 0)


def finish_plane(sizes, x, p_ref, s_ref, halo_ref, plane_ref, send_ref):
    ny = sizes.ny
    start = pl.multiple_of(x * ny + SUB, SUB)
    for r in range(0, ny, SUB):
        at = slice(r, r + SUB)
        at_s = slice(ny + r, ny + r + SUB)
        p, s = p_ref[pl.ds(start + r, SUB), :], s_ref[pl.ds(start + r, SUB), :]
        if halo_ref is not None:
            hp, hs = halo_ref[at, :], halo_ref[at_s, :]
            a, b, c, xx = [plane_ref[i * ny + r : i * ny + r + SUB, :] for i in range(4)]
            change = a * hp + b * hs
            p = p + change
            s = s + c * hs - xx * change
        send_ref[at, :] = p
        send_ref[at_s, :] = s


BEFORE, RHS_OWN, INV_OWN, SUM_OWN, RHS, INV, SLOT_OWN, SLOT_BEFORE, TABLE = range(9)


def shared_cells(sizes, cell_ref, weight_ref, wp_ref, out_ref):
    groups = sizes.groups
    shape = (groups, LANES)
    sub, lane = iota(shape, 0), iota(shape, 1)
    y_row = jnp.full(shape, -1, jnp.int32)
    y_col = y_row
    for g in range(groups):
        y = path_y(sizes, cell_ref, g)
        y_row = jnp.where(lane == g, y, y_row)
        y_col = jnp.where(sub == g, y, y_col)
    total = jnp.zeros(shape, F32)
    empty = jnp.zeros((LANES - groups, LANES), F32)
    for x in range(sizes.planes):
        at = pl.ds(x, groups, SUB)
        other = jnp.concatenate([wp_ref[at, :], empty], axis=0)
        total = total + lax.dot_general(
            weight_ref[at, :], other, (((1,), (1,)), ((), ())),
            precision=lax.Precision.HIGHEST, preferred_element_type=F32,
        )
    out_ref[...] = jnp.where(y_row == y_col, total, 0.0)


def start_kernel(
    sizes,
    cell_ref,
    from_o,
    from_e,
    wells_ref,
    rhs_hbm,
    slot_hbm,
    tx_ref,
    rp_ref,
    ip_ref,
    cc_ref,
    rs_ref,
    uu_ref,
    xx_ref,
    extra_ref,
    weight_ref,
    edge_ref,
    plane_e,
    plane_o,
    wp_ref,
    ws_ref,
    shared_ref,
    table_ref,
    mu_ref,
    sums_out,
    send_o,
    rows_ref,
    rhs_ref,
    slot_ref,
    sems,
):
    ny, planes, groups = sizes.ny, sizes.planes, sizes.groups
    place = lax.axis_index("gx")
    even = place % 2 == 0
    x_o, _ = facing(sizes, even)
    fetches = [
        pltpu.make_async_copy(rhs_hbm, rhs_ref, sems.at[0]),
        pltpu.make_async_copy(slot_hbm, slot_ref, sems.at[1]),
    ]
    for fetch in fetches:
        fetch.start()

    @pl.loop(0, ny // SUB)
    def _(r):
        y0 = pl.multiple_of(r * SUB, SUB)
        at = pl.ds(y0, SUB)
        txl = jnp.where(even, from_o[at, :], from_e[at, :])
        ip = 1.0 / (ip_ref[at, :] + extra_ref[at, :] * txl)
        is_ = 1.0 / (extra_ref[pl.ds(y0 + 2 * ny, SUB), :] + extra_ref[pl.ds(y0 + ny, SUB), :] * txl)
        cc, uu = cc_ref[at, :] * ip, uu_ref[at, :] * is_
        rp, rs, xx = rp_ref[at, :] * ip, rs_ref[at, :] * is_, xx_ref[at, :] * is_
        for i, value in enumerate([ip, cc, rp, rs, uu, xx]):
            edge_ref[pl.ds(y0 + i * ny, SUB), :] = value
        end = pl.ds(y0 + (planes - 1) * ny, SUB)
        tx = tx_ref[end, :]
        low = [ip * txl, cc * txl, uu * txl, xx]
        high = [ip_ref[end, :] * tx, cc_ref[end, :] * tx, uu_ref[end, :] * tx, xx_ref[end, :]]
        for i in range(4):
            to = pl.ds(y0 + i * ny, SUB)
            plane_o[to, :] = jnp.where(even, low[i], high[i])
            plane_e[to, :] = jnp.where(even, high[i], low[i])
        rp_end = rp_ref[end, :]
        send_o[at, :] = jnp.where(even, rp, rp_end)
        send_o[pl.ds(y0 + ny, SUB), :] = jnp.where(
            even, rs - xx * rp, rs_ref[end, :] - xx_ref[end, :] * rp_end
        )

    sub = iota((SUB, LANES), 0)
    for g in range(groups):
        y = path_y(sizes, cell_ref, g)
        at = pl.ds(g * SUB, SUB)
        slab = pl.ds(y, planes, ny)
        ip = jnp.where(sub == 0, edge_ref[pl.ds(y, 1), :], ip_ref[slab, :])
        xx = jnp.where(sub == 0, edge_ref[pl.ds(y + 5 * ny, 1), :], xx_ref[slab, :])
        rp = jnp.where(sub == 0, edge_ref[pl.ds(y + 2 * ny, 1), :], rp_ref[slab, :])
        rows_ref[g : g + 1, :] = jnp.sum(weight_ref[at, :] * rp, axis=0, keepdims=True)
        wp = weight_ref[at, :] * ip
        wp_ref[at, :] = wp
        ws_ref[at, :] = wp * xx
    shared_cells(sizes, cell_ref, weight_ref, wp_ref, shared_ref)

    tile_e, tile_o = from_e[ny : ny + SUB, :], from_o[ny : ny + SUB, :]
    low = jnp.where(even, tile_o, tile_e)
    high = jnp.where(even, tile_e, tile_o)
    before = wells_ref[0:groups, :]
    mine = wells_ref[groups : 2 * groups, :]
    is_before = before > 0.5
    sum_own = mine * (1.0 - before) + column_of(high[1:2, :], groups)
    sum_before = mine * before + column_of(low[0:1, :], groups)
    for fetch in fetches:
        fetch.wait()
    rhs_own = own_lanes(rhs_ref, place, groups)
    rhs_before = own_lanes(rhs_ref, jnp.maximum(place - 1, 0), groups)
    inv_own = 1.0 / (1.5 * sum_own + 0.5)
    inv_before = 1.0 / (1.5 * sum_before + 0.5)
    rhs = jnp.where(is_before, rhs_before, rhs_own)
    inv = jnp.where(is_before, inv_before, inv_own)
    entries = {
        BEFORE: before,
        RHS_OWN: rhs_own,
        INV_OWN: inv_own,
        SUM_OWN: sum_own,
        RHS: rhs,
        INV: inv,
        SLOT_OWN: own_lanes(slot_ref, place, groups),
        SLOT_BEFORE: own_lanes(slot_ref, jnp.maximum(place - 1, 0), groups),
    }
    for i, entry in entries.items():
        table_ref[i * groups : (i + 1) * groups, :] = entry
    mu = rhs * inv
    mu_ref[...] = mu

    add_wells_to_plane(sizes, cell_ref, mu_ref, wp_ref, ws_ref, x_o, send_o)
    put_sums(sizes, even, before, rows_ref[...] + shared_ref[...] * row_of(mu, groups), sums_out, send_o)


def put_sums(sizes, to_before, before, by_lane, rows_out, send_ref):
    ny, groups = sizes.ny, sizes.groups
    rows_out[...] = by_lane
    shared = by_lane * jnp.where(to_before, before, 1.0 - before)
    parts = groups // SUB
    lane = iota((SUB, LANES), 1)
    tile = jnp.zeros((SUB, LANES), F32)
    for q in range(parts):
        part = shared[q * SUB : (q + 1) * SUB, :]
        width = LANES
        while width > LANES // parts:
            width //= 2
            part = part + pltpu.roll(part, width, 1)
        tile = jnp.where(lane // (LANES // parts) == q, part, tile)
    send_ref[2 * ny : 2 * ny + SUB, :] = tile


def rows_of(tile, groups):
    parts = groups // SUB
    lane = iota((SUB, LANES), 1)
    return jnp.concatenate(
        [jnp.where(lane // (LANES // parts) == q, tile, 0.0) for q in range(parts)], axis=0
    )


def finish_core_plane(sizes, cell_ref, p_ref, s_ref, mu_ref, wp_ref, ws_ref, halo, plane_e, send_e):
    even = lax.axis_index("gx") % 2 == 0
    _, x_e = facing(sizes, even)
    finish_plane(sizes, x_e, p_ref, s_ref, halo, plane_e, send_e)
    add_wells_to_plane(sizes, cell_ref, mu_ref, wp_ref, ws_ref, x_e, send_e)


def near_weights(sizes, cell_ref, weight_ref, plane_e, plane_o, near_ref):
    ny, groups = sizes.ny, sizes.groups
    even = lax.axis_index("gx") % 2 == 0
    x_o, x_e = facing(sizes, even)
    for g in range(groups):
        y = path_y(sizes, cell_ref, g)
        for i, (x, plane) in enumerate(((x_o, plane_o), (x_e, plane_e))):
            weight = weight_ref[pl.ds(x + g * SUB, 1), :]
            for j in range(2):
                to = (2 * i + j) * groups + g
                near_ref[to : to + 1, :] = weight * plane[pl.ds(y + j * ny, 1), :]


def put_planes(sizes, even, send_e, send_o, p_ref, s_ref, pad):
    ny = sizes.ny
    x_o, x_e = facing(sizes, even)
    for send, x in ((send_o, x_o), (send_e, x_e)):
        start = pl.multiple_of(x * ny + pad, SUB)
        for r in range(0, ny, SUB):
            p_ref[pl.ds(start + r, SUB), :] = send[r : r + SUB, :]
            s_ref[pl.ds(start + r, SUB), :] = send[ny + r : ny + r + SUB, :]


def inner_kernel(
    sizes,
    first,
    cell_ref,
    mu_ref,
    wp_ref,
    ws_ref,
    weight_ref,
    send_o,
    sums_in,
    table_ref,
    tx_ref,
    ty_ref,
    tyl_ref,
    tz_ref,
    tzl_ref,
    rp_ref,
    ip_ref,
    cc_ref,
    rs_ref,
    uu_ref,
    xx_ref,
    edge_ref,
    plane_e,
    *refs,
):
    ny, planes = sizes.ny, sizes.planes
    rows = planes * ny
    even = lax.axis_index("gx") % 2 == 0
    if first:
        plane_o, p_old, s_old, p_ref, s_ref, rows_ref, sums_out, send_e, near_ref = refs
        halo = None
        clear_ends(rows, p_old, s_old)

        @pl.loop(0, ny // SUB)
        def _(r):
            y0 = pl.multiple_of(r * SUB, SUB)
            for x in range(planes):
                at, to = pl.ds(y0 + x * ny, SUB), pl.ds(y0 + (x * ny + SUB), SUB)
                if x == 0:
                    rp, rs, xx = [edge_ref[pl.ds(y0 + i * ny, SUB), :] for i in (2, 3, 5)]
                else:
                    rp, rs, xx = rp_ref[at, :], rs_ref[at, :], xx_ref[at, :]
                p_old[to, :] = rp
                s_old[to, :] = rs - xx * rp

        near_weights(sizes, cell_ref, weight_ref, plane_e, plane_o, near_ref)
    else:
        halo, _, _, p_old, s_old, p_ref, s_ref, rows_ref, sums_out, send_e = refs
    finish_core_plane(sizes, cell_ref, p_old, s_old, mu_ref, wp_ref, ws_ref, halo, plane_e, send_e)
    before = table_ref[BEFORE * sizes.groups : (BEFORE + 1) * sizes.groups, :]
    put_sums(sizes, jnp.logical_not(even), before, sums_in[...], sums_out, send_e)
    add_wells(sizes, cell_ref, mu_ref, wp_ref, ws_ref, p_old, s_old, SUB)
    put_planes(sizes, even, send_e, send_o, p_old, s_old, SUB)

    @pl.loop(0, ny // SUB)
    def _(r):
        y0 = pl.multiple_of(r * SUB, SUB)
        here = [pl.ds(y0 + (x * ny + SUB), SUB) for x in range(planes)]
        ps = [p_old[at, :] for at in here]
        ss = [s_old[at, :] for at in here]
        tx = None
        for x in range(planes):
            at = pl.ds(y0 + x * ny, SUB)
            up = pl.ds(y0 + (x * ny + SUB + 1), SUB)
            down = pl.ds(y0 + (x * ny + SUB - 1), SUB)
            txl = tx
            tx = tx_ref[at, :] if x < planes - 1 else None
            ty, tyl, tz, tzl = ty_ref[at, :], tyl_ref[at, :], tz_ref[at, :], tzl_ref[at, :]

            def neighbours(fields, old):
                mid = fields[x]
                total = tz * pltpu.roll(mid, LANES - 1, 1) + tzl * pltpu.roll(mid, 1, 1)
                total = total + (ty * old[up, :] + tyl * old[down, :])
                if x < planes - 1:
                    total = total + tx * fields[x + 1]
                if x > 0:
                    total = total + txl * fields[x - 1]
                return total

            sum_p = neighbours(ps, p_old)
            sum_s = neighbours(ss, s_old)
            if x == 0:
                ip, cc, rp, rs, uu, xx = [edge_ref[pl.ds(y0 + i * ny, SUB), :] for i in range(6)]
            else:
                ip, cc, rp, rs, uu, xx = [ref[at, :] for ref in (ip_ref, cc_ref, rp_ref, rs_ref, uu_ref, xx_ref)]
            p = rp + ip * sum_p + cc * sum_s
            p_ref[here[x], :] = p
            s_ref[here[x], :] = rs + uu * sum_s - xx * p

    clear_ends(rows, p_ref, s_ref)
    path_rows(sizes, cell_ref, weight_ref, p_ref, rows_ref)


def facing_kernel(sizes, cell_ref, from_o, p_ref, s_ref, plane_o, near_ref, send_o, sums_ref):
    even = lax.axis_index("gx") % 2 == 0
    x_o, _ = facing(sizes, even)
    finish_plane(sizes, x_o, p_ref, s_ref, from_o, plane_o, send_o)
    near_sums(sizes, cell_ref, from_o, near_ref, 0, sums_ref)


def near_sums(sizes, cell_ref, halo, near_ref, side, sums_ref):
    groups = sizes.groups
    for g in range(groups):
        y = path_y(sizes, cell_ref, g)
        row = jnp.zeros((1, LANES), F32)
        for j in range(2):
            at = (2 * side + j) * groups + g
            row = row + near_ref[at : at + 1, :] * halo[pl.ds(y + j * sizes.ny, 1), :]
        sums_ref[g : g + 1, :] = row


def outer_kernel(
    sizes,
    final,
    cell_ref,
    send_in,
    from_o,
    from_e,
    rows_ref,
    near_o,
    sums_in,
    table_ref,
    wp_ref,
    ws_ref,
    shared_ref,
    near_ref,
    send_o,
    mu_ref,
    *rest,
):
    ny, groups = sizes.ny, sizes.groups
    near_e = rest[-1]
    even = lax.axis_index("gx") % 2 == 0
    x_o, _ = facing(sizes, even)

    def table(i):
        return table_ref[i * groups : (i + 1) * groups, :]

    tail = slice(2 * ny, 2 * ny + SUB)
    come_e, come_o = from_e[tail, :], from_o[tail, :]
    low = rows_of(jnp.where(even, come_o, come_e), groups)
    high = rows_of(jnp.where(even, come_e, come_o), groups)
    before = table(BEFORE)
    total = spread(lane_sum(sums_in[...] + jnp.where(before > 0.5, low, high)), groups)
    mu = (table(RHS) + total) * table(INV)
    mu_ref[...] = mu
    near_sums(sizes, cell_ref, from_e, near_ref, 1, near_e)
    by_lane = rows_ref[...] + near_o[...] + near_e[...] + shared_ref[...] * row_of(mu, groups)
    add_wells_to_plane(sizes, cell_ref, mu_ref, wp_ref, ws_ref, x_o, send_o)
    if not final:
        put_sums(sizes, even, before, by_lane, rest[0], send_o)
        return
    total_own = spread(lane_sum(sums_in[...] * (1.0 - before) + high), groups)
    total = spread(lane_sum(by_lane), groups)
    part_own, part_before = total * (1.0 - before), total * before
    grads_ref = rest[0]
    mu_own = (table(RHS_OWN) + total_own) * table(INV_OWN)
    grad_own = mu_own * table(SUM_OWN) - part_own
    grad_before = -part_before
    lane = iota((SUB, LANES), 1).astype(F32)
    outside = lane >= groups
    values = []
    for slots, grad in ((table(SLOT_OWN), grad_own), (table(SLOT_BEFORE), grad_before)):
        for q in range(groups // SUB):
            part = slice(q * SUB, (q + 1) * SUB)
            values.append((jnp.where(outside, -1.0, slots[part, :] - lane), grad[part, :]))
    for d in range(sizes.devices):
        total = jnp.zeros((SUB, LANES), F32)
        for slot, grad in values:
            total = total + jnp.where(slot == float(d * groups), grad, 0.0)
        grads_ref[d] = jnp.sum(total, axis=0, keepdims=True)


def final_kernel(
    sizes,
    cell_ref,
    p_in,
    s_in,
    mu_ref,
    wp_ref,
    ws_ref,
    plane_e,
    send_o,
    from_e,
    p_old,
    s_old,
    p_out,
    s_out,
    send_e,
    sems,
):
    rows = sizes.planes * sizes.ny
    even = lax.axis_index("gx") % 2 == 0
    finish_core_plane(sizes, cell_ref, p_old, s_old, mu_ref, wp_ref, ws_ref, from_e, plane_e, send_e)
    add_wells(sizes, cell_ref, mu_ref, wp_ref, ws_ref, p_old, s_old, SUB)
    put_planes(sizes, even, send_e, send_o, p_old, s_old, SUB)
    copies = [
        pltpu.make_async_copy(field.at[pl.ds(SUB, rows)], out, sems.at[i])
        for i, (field, out) in enumerate(((p_old, p_out), (s_old, s_out)))
    ]
    for copy in copies:
        copy.start()
    for copy in copies:
        copy.wait()


class Sizes:
    def __init__(self, planes, ny, groups, run, devices):
        self.planes, self.ny, self.groups, self.run, self.devices = planes, ny, groups, run, devices


def body(
    rhs_pressure,
    rhs_saturation,
    trans_x,
    trans_y,
    trans_z,
    coupling,
    upwind,
    storage,
    cross,
    accel,
    perf_cell,
    perf_well,
    perf_index,
    well_rhs,
    well_slot,
):
    planes, ny, nz = trans_x.shape
    devices = lax.axis_size("gx")
    groups = well_rhs.shape[0] // devices
    run = perf_cell.shape[0] // groups
    sizes = Sizes(planes, ny, groups, run, devices)
    rows = planes * ny
    padded = rows + 2 * SUB
    SMEM, VMEM, HBM, DMA = pltpu.SMEM, pltpu.VMEM, pltpu.HBM, pltpu.SemaphoreType.DMA

    def flat(array):
        return array.reshape(rows, nz)

    def lines(array):
        return array.reshape(-1, LANES)

    def call(kernel, args, spaces, outs, scratch, name, micros, aliases=None):
        return pl.pallas_call(
            kernel,
            in_specs=[spec(space) for space in spaces],
            out_specs=[spec(out.memory_space) for out in outs],
            out_shape=outs,
            scratch_shapes=scratch,
            input_output_aliases=aliases or {},
            compiler_params=pltpu.CompilerParams(vmem_limit_bytes=16 * 1024 * 1024),
            cost_estimate=pl.CostEstimate(flops=int(micros * 4e6), bytes_accessed=int(micros * 3e6), transcendentals=0),
            name=name,
        )(*[placed(a, space) for a, space in zip(args, spaces)])

    def call_vmem(kernel, args, outs, scratch, name, micros, aliases=None):
        return call(
            functools.partial(kernel, sizes), [y] + args, [SMEM] + [VMEM] * len(args), outs, scratch,
            name, micros, aliases,
        )

    pairs_e = [(i, i ^ 1) for i in range(devices) if i ^ 1 < devices]
    pairs_o = []
    for i in range(1, devices - 1, 2):
        pairs_o += [(i, i + 1), (i + 1, i)]

    def to_core(block):
        return lax.ppermute(block, "gx", pairs_e)

    def to_chip(block):
        return lax.ppermute(block, "gx", pairs_o)

    index = lines(perf_index)
    send, wells = call(
        functools.partial(first_kernel, sizes),
        [flat(trans_x), lines(perf_well), index],
        [HBM, HBM, HBM],
        [vmem(ny + SUB), vmem(2 * groups)],
        [VMEM(index.shape, jnp.int32), VMEM(index.shape, F32), DMA((3,))],
        "first",
        1,
    )
    from_o = to_chip(send)
    from_e = to_core(send)
    big = [trans_x, trans_y, trans_z, accel, coupling, upwind, storage, rhs_pressure, rhs_saturation, cross]
    made = call(
        functools.partial(setup_kernel, sizes),
        [perf_cell, perf_index] + big,
        [HBM] * (2 + len(big)),
        [vmem(rows)] * 11 + [vmem(3 * ny), vmem(groups * SUB), SMEM((groups,), jnp.int32)],
        [
            VMEM((planes, ny, LANES), F32),
            VMEM((planes, ny + SUB, LANES), F32),
        ]
        + [VMEM((planes, ny, LANES), F32)] * 8
        + [
            VMEM((rows, LANES), F32),
            SMEM(perf_cell.shape, jnp.int32),
            SMEM(perf_index.shape, F32),
            DMA((CHUNKS, 10)),
            DMA((2,)),
        ],
        "setup",
        4,
    )
    coefficients, (extra, weight, y) = list(made[:11]), made[11:]
    group_row = VMEM((groups, LANES), F32)
    fields = [vmem(padded), vmem(padded)]
    block = vmem(2 * ny + SUB)
    slabs = vmem(groups * SUB)
    edge, plane_e, plane_o, wp, ws, shared, table, mu, sums, send_o = call(
        functools.partial(start_kernel, sizes),
        [y, from_o, from_e, wells, lines(well_rhs), lines(well_slot), coefficients[0]]
        + coefficients[5:]
        + [extra, weight],
        [SMEM] + [VMEM] * 3 + [HBM] * 2 + [VMEM] * 9,
        [vmem(6 * ny), vmem(4 * ny), vmem(4 * ny), slabs, slabs, vmem(groups), vmem(TABLE * groups)]
        + [vmem(groups), vmem(groups), block],
        [
            group_row,
            VMEM(lines(well_rhs).shape, F32),
            VMEM(lines(well_slot).shape, jnp.int32),
            DMA((2,)),
        ],
        "start",
        2,
    )
    near = None
    for sweep in range(1, SWEEPS):
        final = sweep == SWEEPS - 1
        next_o = to_chip(send_o)
        first = sweep == 1
        _, _, p, s, by_lane, sums, send_e, *rest = call_vmem(
            lambda sz, *refs: inner_kernel(sz, first, *refs),
            [mu, wp, ws, weight, send_o, sums, table]
            + coefficients
            + ([edge, plane_e, plane_o] if first else [edge, plane_e, from_e, p, s]),
            fields + fields + [vmem(groups), vmem(groups), block] + ([vmem(4 * groups)] if first else []),
            [],
            "inner",
            2,
            {} if first else {22: 0, 23: 1},
        )
        if first:
            near = rest[0]
        next_e = to_core(send_e)
        from_e, from_o = next_e, next_o
        half_o, near_o = call_vmem(
            facing_kernel, [from_o, p, s, plane_o, near], [block, vmem(groups)], [], "facing", 0.5
        )
        send_o, mu, sums = call_vmem(
            lambda sz, *refs: outer_kernel(sz, final, *refs),
            [half_o, from_o, from_e, by_lane, near_o, sums, table, wp, ws, shared, near],
            [block, vmem(groups), pltpu.VMEM((devices, 1, LANES), F32) if final else vmem(groups)],
            [group_row],
            "outer",
            1,
            {1: 0},
        )
    grads = lax.all_to_all(sums, "gx", 0, 0)
    result = pltpu.HBM((rows, nz), F32)
    _, _, p, s = call_vmem(
        final_kernel,
        [p, s, mu, wp, ws, plane_e, send_o, from_e],
        fields + [result, result],
        [VMEM((2 * ny + SUB, LANES), F32), DMA((2,))],
        "final",
        2,
        {1: 0, 2: 1},
    )
    control = jnp.sum(grads, axis=(0, 1))[:groups]
    shape = trans_x.shape
    return p.reshape(shape), s.reshape(shape), control


def solution(mesh):
    grid = P(("ens", "gx"), None, None)
    line = P(("ens", "gx"))
    return jax.shard_map(
        body,
        mesh=mesh,
        in_specs=(grid,) * 10 + (line,) * 3 + (P("ens"), P("ens")),
        out_specs=(grid, grid, line),
        check_vma=False,
    )
```

```python
import functools

import jax
import jax.numpy as jnp
from jax import lax
from jax.experimental import pallas as pl
from jax.experimental.pallas import tpu as pltpu
from jax.sharding import PartitionSpec as P

SWEEPS = 6
SUB = 8
LANES = 128
F32 = jnp.float32
CHUNKS = 4


def vmem(rows):
    return pltpu.VMEM((rows, LANES), F32)


def placed(array, space):
    return array if space is pltpu.SMEM else pltpu.with_memory_space_constraint(array, space)


def spec(space):
    return pl.BlockSpec(memory_space=space)


def iota(shape, dim):
    return lax.broadcasted_iota(jnp.int32, shape, dim)


def lane_sum(block):
    return jnp.sum(block, axis=1, keepdims=True)


def spread(column, groups):
    return jnp.broadcast_to(column, (groups, LANES))


def row_of(column, groups):
    mine = iota((groups, LANES), 0) == iota((groups, LANES), 1)
    return jnp.sum(jnp.where(mine, column, 0.0), axis=0, keepdims=True)


def column_of(row, groups):
    mine = iota((groups, LANES), 0) == iota((groups, LANES), 1)
    return spread(lane_sum(jnp.where(mine, jnp.broadcast_to(row, (groups, LANES)), 0.0)), groups)


def well_block(part_own, part_before, groups):
    sub = iota((SUB, LANES), 0)
    own = jnp.broadcast_to(row_of(part_own, groups), (SUB, LANES))
    before = jnp.broadcast_to(row_of(part_before, groups), (SUB, LANES))
    return jnp.where(sub == 0, own, jnp.where(sub == 1, before, 0.0))


def group_rows(ref, groups, run):
    per_row = LANES // run
    return jnp.concatenate(
        [jnp.broadcast_to(ref[i : i + 1, :], (per_row, LANES)) for i in range(groups // per_row)], axis=0
    )


def first_kernel(sizes, tx_hbm, well_hbm, index_hbm, send_ref, wells_ref, well_ref, index_ref, sems):
    ny, groups, run = sizes.ny, sizes.groups, sizes.run
    plane = pltpu.make_async_copy(
        tx_hbm.at[pl.ds((sizes.planes - 1) * ny, ny)], send_ref.at[pl.ds(0, ny)], sems.at[0]
    )
    get_well = pltpu.make_async_copy(well_hbm, well_ref, sems.at[1])
    get_index = pltpu.make_async_copy(index_hbm, index_ref, sems.at[2])
    for copy in (get_well, get_index, plane):
        copy.start()
    place = lax.axis_index("gx")
    shape = (groups, LANES)
    per_row = LANES // run
    local = iota(shape, 0) % per_row
    lane = iota(shape, 1)
    get_well.wait()
    get_index.wait()
    weights = jnp.where(lane // run == local, group_rows(index_ref, groups, run), 0.0)
    total = lane_sum(weights)
    first = jnp.where(lane == local * run, group_rows(well_ref, groups, run).astype(F32), 0.0)
    well = lane_sum(first)
    before = well < (place * groups).astype(F32)
    before = spread(jnp.where(before, 1.0, 0.0), groups)
    total = spread(total, groups)
    wells_ref[0:groups, :] = before
    wells_ref[groups : 2 * groups, :] = total
    send_ref[ny : ny + SUB, :] = well_block(total * (1.0 - before), total * before, groups)
    plane.wait()


def split_cell(cell, ny):
    if ny & (ny - 1):
        row = lax.div(cell, LANES)
        return lax.div(row, ny), lax.rem(row, ny), lax.rem(cell, LANES)
    bits_z, bits_y = LANES.bit_length() - 1, ny.bit_length() - 1
    row = lax.shift_right_logical(cell, bits_z)
    return lax.shift_right_logical(row, bits_y), row & (ny - 1), cell & (LANES - 1)


def setup_kernel(
    sizes,
    cell_hbm,
    index_hbm,
    rhs_hbm,
    slot_hbm,
    tx_hbm,
    ty_hbm,
    tz_hbm,
    accel_hbm,
    coupling_hbm,
    upwind_hbm,
    storage_hbm,
    rhs_p_hbm,
    rhs_s_hbm,
    cross_hbm,
    tx_ref,
    ty_ref,
    tyl_ref,
    tz_ref,
    tzl_ref,
    rp_ref,
    ip_ref,
    cc_ref,
    rs_ref,
    uu_ref,
    xx_ref,
    extra_ref,
    weight_ref,
    y_ref,
    p_ref,
    s_ref,
    lanes_ref,
    raw_tx,
    raw_ty,
    raw_tz,
    raw_accel,
    raw_coupling,
    raw_upwind,
    raw_storage,
    raw_rhs_p,
    raw_rhs_s,
    raw_cross,
    cwi_ref,
    cell_ref,
    index_ref,
    rhs_ref,
    slot_ref,
    sems,
    fetch_sems,
):
    ny, planes, groups, run = sizes.ny, sizes.planes, sizes.groups, sizes.run
    rows = planes * ny
    part = ny // CHUNKS
    moves = [
        (tx_hbm, raw_tx),
        (ty_hbm, raw_ty),
        (tz_hbm, raw_tz),
        (accel_hbm, raw_accel),
        (coupling_hbm, raw_coupling),
        (upwind_hbm, raw_upwind),
        (storage_hbm, raw_storage),
        (rhs_p_hbm, raw_rhs_p),
        (rhs_s_hbm, raw_rhs_s),
        (cross_hbm, raw_cross),
    ]

    def copies(c):
        found = []
        for i, (src, dst) in enumerate(moves):
            start = pl.multiple_of(c * part, SUB)
            to = pl.multiple_of(start + SUB, SUB) if dst is raw_ty else start
            found.append(
                pltpu.make_async_copy(src.at[:, pl.ds(start, part)], dst.at[:, pl.ds(to, part)], sems.at[c, i])
            )
        return found

    wanted = ((cell_hbm, cell_ref), (index_hbm, index_ref), (rhs_hbm, rhs_ref), (slot_hbm, slot_ref))
    fetches = [pltpu.make_async_copy(src, dst, fetch_sems.at[i]) for i, (src, dst) in enumerate(wanted)]
    for fetch in fetches:
        fetch.start()
    for c in range(CHUNKS):
        for copy in copies(c):
            copy.start()

    last = lax.axis_index("gx") == lax.axis_size("gx") - 1
    keep_last = jnp.where(last, 0.0, 1.0)
    zero = jnp.zeros((SUB, LANES), F32)

    @pl.loop(0, rows // SUB, unroll=8)
    def _(i):
        cwi_ref[pl.ds(pl.multiple_of(i * SUB, SUB), SUB), :] = zero

    for fetch in fetches:
        fetch.wait()
    clear_ends(rows, p_ref, s_ref)
    place = lax.axis_index("gx")
    behind = jnp.maximum(place - 1, 0)
    for i, (ref, whose) in enumerate(((rhs_ref, place), (rhs_ref, behind), (slot_ref, place), (slot_ref, behind))):
        lanes_ref[i * groups : (i + 1) * groups, :] = own_lanes(ref, whose, groups)
    spot = iota((SUB, LANES), 0) * LANES + iota((SUB, LANES), 1)
    for g in range(groups):
        _, y, _ = split_cell(cell_ref[g * run], ny)
        y_ref[g] = y
        weight = zero
        for k in range(g * run, (g + 1) * run):
            x, _, z = split_cell(cell_ref[k], ny)
            weight = weight + jnp.where(spot == x * LANES + z, index_ref[k], 0.0)
        weight_ref[g * SUB : (g + 1) * SUB, :] = weight
        slab = pl.ds(y, planes, ny)
        cwi_ref[slab, :] = cwi_ref[slab, :] + weight

    lane = iota((SUB, LANES), 1)
    sub = iota((SUB, LANES), 0)

    @pl.loop(0, CHUNKS)
    def _(c):
        for copy in copies(c):
            copy.wait()

        @pl.loop(0, part // SUB)
        def _(r):
            y0 = pl.multiple_of(c * part + r * SUB, SUB)
            ypos = sub + y0
            here = pl.ds(y0, SUB)
            txl = None
            for x in range(planes):
                at = pl.ds(y0 + x * ny, SUB)
                tx = raw_tx[x, here, :]
                if x == planes - 1:
                    tx = tx * keep_last
                tx_ref[at, :] = tx
                ty = jnp.where(ypos == ny - 1, 0.0, raw_ty[x, pl.ds(y0 + SUB, SUB), :])
                tyl = jnp.where(ypos == 0, 0.0, raw_ty[x, pl.ds(y0 + SUB - 1, SUB), :])
                tz = jnp.where(lane == LANES - 1, 0.0, raw_tz[x, here, :])
                tzl = pltpu.roll(tz, 1, 1)
                ty_ref[at, :] = ty
                tyl_ref[at, :] = tyl
                tz_ref[at, :] = tz
                tzl_ref[at, :] = tzl
                tsum = tx + ty + tyl + tz + tzl
                if x > 0:
                    tsum = tsum + txl
                accel = raw_accel[x, here, :]
                coupling = raw_coupling[x, here, :]
                upwind = raw_upwind[x, here, :]
                to_p = accel * (1.0 + jnp.abs(coupling))
                to_s = accel * jnp.abs(upwind)
                dp = to_p * tsum + accel * cwi_ref[at, :]
                ds = to_s * tsum + raw_storage[x, here, :]
                rhs_p, rhs_s, cross = raw_rhs_p[x, here, :], raw_rhs_s[x, here, :], raw_cross[x, here, :]
                if x == 0:
                    extra_ref[here, :] = to_p
                    extra_ref[pl.ds(y0 + ny, SUB), :] = to_s
                    extra_ref[pl.ds(y0 + 2 * ny, SUB), :] = ds
                    ip_ref[at, :] = dp
                    ip, is_ = 1.0, 1.0
                else:
                    ip = 1.0 / dp
                    is_ = 1.0 / ds
                    ip_ref[at, :] = ip
                cc_ref[at, :] = coupling * ip
                rp, rs, xx = rhs_p * ip, rhs_s * is_, cross * is_
                rp_ref[at, :] = rp
                rs_ref[at, :] = rs
                uu_ref[at, :] = upwind * is_
                xx_ref[at, :] = xx
                if x > 0:
                    to = pl.ds(y0 + (x * ny + SUB), SUB)
                    p_ref[to, :] = rp
                    s_ref[to, :] = rs - xx * rp
                txl = tx


def own_lanes(ref, place, groups):
    shape = (groups, LANES)
    start = place * groups
    row = jnp.broadcast_to(ref[pl.ds(start // LANES, 1), :].astype(F32), shape)
    mine = iota(shape, 1) == iota(shape, 0) + start % LANES
    return spread(lane_sum(jnp.where(mine, row, 0.0)), groups)


def clear_ends(rows, *refs):
    zero = jnp.zeros((SUB, LANES), F32)
    for ref in refs:
        ref[0:SUB, :] = zero
        ref[rows + SUB : rows + 2 * SUB, :] = zero


def path_y(sizes, cell_ref, g):
    return cell_ref[g]


def slab_of(sizes, cell_ref, g, pad):
    return pl.ds(path_y(sizes, cell_ref, g) + pad, sizes.planes, sizes.ny)


def add_wells(sizes, cell_ref, mu_ref, wp_ref, ws_ref, p_ref, s_ref, pad):
    for g in range(sizes.groups):
        slab = slab_of(sizes, cell_ref, g, pad)
        at = pl.ds(g * SUB, SUB)
        mu = mu_ref[g : g + 1, :]
        p_ref[slab, :] = p_ref[slab, :] + mu * wp_ref[at, :]
        s_ref[slab, :] = s_ref[slab, :] - mu * ws_ref[at, :]


def add_wells_to_plane(sizes, cell_ref, mu_ref, wp_ref, ws_ref, x, send_ref):
    for g in range(sizes.groups):
        y = path_y(sizes, cell_ref, g)
        in_p, in_s, at = pl.ds(y, 1), pl.ds(y + sizes.ny, 1), pl.ds(x + g * SUB, 1)
        mu = mu_ref[g : g + 1, :]
        send_ref[in_p, :] = send_ref[in_p, :] + mu * wp_ref[at, :]
        send_ref[in_s, :] = send_ref[in_s, :] - mu * ws_ref[at, :]


def path_rows(sizes, cell_ref, weight_ref, p_ref, rows_ref):
    for g in range(sizes.groups):
        slab = slab_of(sizes, cell_ref, g, SUB)
        at = pl.ds(g * SUB, SUB)
        rows_ref[g : g + 1, :] = jnp.sum(p_ref[slab, :] * weight_ref[at, :], axis=0, keepdims=True)


def facing(sizes, even):
    last = sizes.planes - 1
    return jnp.where(even, 0, last), jnp.where(even, last, 0)


def finish_plane(sizes, x, p_ref, s_ref, halo_ref, plane_ref, send_ref):
    ny = sizes.ny
    start = pl.multiple_of(x * ny + SUB, SUB)
    for r in range(0, ny, SUB):
        at = slice(r, r + SUB)
        at_s = slice(ny + r, ny + r + SUB)
        p, s = p_ref[pl.ds(start + r, SUB), :], s_ref[pl.ds(start + r, SUB), :]
        if halo_ref is not None:
            hp, hs = halo_ref[at, :], halo_ref[at_s, :]
            a, b, c, xx = [plane_ref[i * ny + r : i * ny + r + SUB, :] for i in range(4)]
            change = a * hp + b * hs
            p = p + change
            s = s + c * hs - xx * change
        send_ref[at, :] = p
        send_ref[at_s, :] = s


BEFORE, RHS_OWN, INV_OWN, SUM_OWN, RHS, INV, SLOT_OWN, SLOT_BEFORE, TABLE = range(9)


def shared_cells(sizes, cell_ref, weight_ref, wp_ref, out_ref):
    groups = sizes.groups
    shape = (groups, LANES)
    sub, lane = iota(shape, 0), iota(shape, 1)
    y_row = jnp.full(shape, -1, jnp.int32)
    y_col = y_row
    for g in range(groups):
        y = path_y(sizes, cell_ref, g)
        y_row = jnp.where(lane == g, y, y_row)
        y_col = jnp.where(sub == g, y, y_col)
    total = jnp.zeros(shape, F32)
    empty = jnp.zeros((LANES - groups, LANES), F32)
    for x in range(sizes.planes):
        at = pl.ds(x, groups, SUB)
        other = jnp.concatenate([wp_ref[at, :], empty], axis=0)
        total = total + lax.dot_general(
            weight_ref[at, :], other, (((1,), (1,)), ((), ())),
            precision=lax.Precision.HIGHEST, preferred_element_type=F32,
        )
    out_ref[...] = jnp.where(y_row == y_col, total, 0.0)


def start_kernel(
    sizes,
    cell_ref,
    from_o,
    from_e,
    wells_ref,
    tx_ref,
    rp_ref,
    ip_ref,
    cc_ref,
    rs_ref,
    uu_ref,
    xx_ref,
    extra_ref,
    weight_ref,
    lanes_ref,
    p_in,
    s_in,
    p_ref,
    s_ref,
    edge_ref,
    plane_e,
    plane_o,
    wp_ref,
    ws_ref,
    shared_ref,
    table_ref,
    mu_ref,
    sums_out,
    send_o,
    rows_ref,
):
    ny, planes, groups = sizes.ny, sizes.planes, sizes.groups
    place = lax.axis_index("gx")
    even = place % 2 == 0
    x_o, _ = facing(sizes, even)

    @pl.loop(0, ny // SUB)
    def _(r):
        y0 = pl.multiple_of(r * SUB, SUB)
        at = pl.ds(y0, SUB)
        txl = jnp.where(even, from_o[at, :], from_e[at, :])
        ip = 1.0 / (ip_ref[at, :] + extra_ref[at, :] * txl)
        is_ = 1.0 / (extra_ref[pl.ds(y0 + 2 * ny, SUB), :] + extra_ref[pl.ds(y0 + ny, SUB), :] * txl)
        cc, uu = cc_ref[at, :] * ip, uu_ref[at, :] * is_
        rp, rs, xx = rp_ref[at, :] * ip, rs_ref[at, :] * is_, xx_ref[at, :] * is_
        for i, value in enumerate([ip, cc, rp, rs, uu, xx]):
            edge_ref[pl.ds(y0 + i * ny, SUB), :] = value
        end = pl.ds(y0 + (planes - 1) * ny, SUB)
        tx = tx_ref[end, :]
        low = [ip * txl, cc * txl, uu * txl, xx]
        high = [ip_ref[end, :] * tx, cc_ref[end, :] * tx, uu_ref[end, :] * tx, xx_ref[end, :]]
        for i in range(4):
            to = pl.ds(y0 + i * ny, SUB)
            plane_o[to, :] = jnp.where(even, low[i], high[i])
            plane_e[to, :] = jnp.where(even, high[i], low[i])
        rp_end = rp_ref[end, :]
        s0 = rs - xx * rp
        p_ref[pl.ds(y0 + SUB, SUB), :] = rp
        s_ref[pl.ds(y0 + SUB, SUB), :] = s0
        send_o[at, :] = jnp.where(even, rp, rp_end)
        send_o[pl.ds(y0 + ny, SUB), :] = jnp.where(
            even, s0, rs_ref[end, :] - xx_ref[end, :] * rp_end
        )

    sub = iota((SUB, LANES), 0)
    for g in range(groups):
        y = path_y(sizes, cell_ref, g)
        at = pl.ds(g * SUB, SUB)
        slab = pl.ds(y, planes, ny)
        ip = jnp.where(sub == 0, edge_ref[pl.ds(y, 1), :], ip_ref[slab, :])
        xx = jnp.where(sub == 0, edge_ref[pl.ds(y + 5 * ny, 1), :], xx_ref[slab, :])
        rp = jnp.where(sub == 0, edge_ref[pl.ds(y + 2 * ny, 1), :], rp_ref[slab, :])
        rows_ref[g : g + 1, :] = jnp.sum(weight_ref[at, :] * rp, axis=0, keepdims=True)
        wp = weight_ref[at, :] * ip
        wp_ref[at, :] = wp
        ws_ref[at, :] = wp * xx
    shared_cells(sizes, cell_ref, weight_ref, wp_ref, shared_ref)

    tile_e, tile_o = from_e[ny : ny + SUB, :], from_o[ny : ny + SUB, :]
    low = jnp.where(even, tile_o, tile_e)
    high = jnp.where(even, tile_e, tile_o)
    before = wells_ref[0:groups, :]
    mine = wells_ref[groups : 2 * groups, :]
    is_before = before > 0.5
    sum_own = mine * (1.0 - before) + column_of(high[1:2, :], groups)
    sum_before = mine * before + column_of(low[0:1, :], groups)
    rhs_own, rhs_before, slot_own, slot_before = [
        lanes_ref[i * groups : (i + 1) * groups, :] for i in range(4)
    ]
    inv_own = 1.0 / (1.5 * sum_own + 0.5)
    inv_before = 1.0 / (1.5 * sum_before + 0.5)
    rhs = jnp.where(is_before, rhs_before, rhs_own)
    inv = jnp.where(is_before, inv_before, inv_own)
    entries = {
        BEFORE: before,
        RHS_OWN: rhs_own,
        INV_OWN: inv_own,
        SUM_OWN: sum_own,
        RHS: rhs,
        INV: inv,
        SLOT_OWN: slot_own,
        SLOT_BEFORE: slot_before,
    }
    for i, entry in entries.items():
        table_ref[i * groups : (i + 1) * groups, :] = entry
    mu = rhs * inv
    mu_ref[...] = mu

    add_wells_to_plane(sizes, cell_ref, mu_ref, wp_ref, ws_ref, x_o, send_o)
    put_sums(sizes, even, before, rows_ref[...] + shared_ref[...] * row_of(mu, groups), sums_out, send_o)


def put_sums(sizes, to_before, before, by_lane, rows_out, send_ref):
    ny, groups = sizes.ny, sizes.groups
    rows_out[...] = by_lane
    shared = by_lane * jnp.where(to_before, before, 1.0 - before)
    parts = groups // SUB
    lane = iota((SUB, LANES), 1)
    tile = jnp.zeros((SUB, LANES), F32)
    for q in range(parts):
        part = shared[q * SUB : (q + 1) * SUB, :]
        width = LANES
        while width > LANES // parts:
            width //= 2
            part = part + pltpu.roll(part, width, 1)
        tile = jnp.where(lane // (LANES // parts) == q, part, tile)
    send_ref[2 * ny : 2 * ny + SUB, :] = tile


def rows_of(tile, groups):
    parts = groups // SUB
    lane = iota((SUB, LANES), 1)
    return jnp.concatenate(
        [jnp.where(lane // (LANES // parts) == q, tile, 0.0) for q in range(parts)], axis=0
    )


def finish_core_plane(sizes, cell_ref, p_ref, s_ref, mu_ref, wp_ref, ws_ref, halo, plane_e, send_e):
    even = lax.axis_index("gx") % 2 == 0
    _, x_e = facing(sizes, even)
    finish_plane(sizes, x_e, p_ref, s_ref, halo, plane_e, send_e)
    add_wells_to_plane(sizes, cell_ref, mu_ref, wp_ref, ws_ref, x_e, send_e)


def near_weights(sizes, cell_ref, weight_ref, plane_e, plane_o, near_ref):
    ny, groups = sizes.ny, sizes.groups
    even = lax.axis_index("gx") % 2 == 0
    x_o, x_e = facing(sizes, even)
    for g in range(groups):
        y = path_y(sizes, cell_ref, g)
        for i, (x, plane) in enumerate(((x_o, plane_o), (x_e, plane_e))):
            weight = weight_ref[pl.ds(x + g * SUB, 1), :]
            for j in range(2):
                to = (2 * i + j) * groups + g
                near_ref[to : to + 1, :] = weight * plane[pl.ds(y + j * ny, 1), :]


def put_planes(sizes, even, send_e, send_o, p_ref, s_ref, pad):
    ny = sizes.ny
    x_o, x_e = facing(sizes, even)
    for send, x in ((send_o, x_o), (send_e, x_e)):
        start = pl.multiple_of(x * ny + pad, SUB)
        for r in range(0, ny, SUB):
            p_ref[pl.ds(start + r, SUB), :] = send[r : r + SUB, :]
            s_ref[pl.ds(start + r, SUB), :] = send[ny + r : ny + r + SUB, :]


def inner_kernel(
    sizes,
    first,
    cell_ref,
    mu_ref,
    wp_ref,
    ws_ref,
    weight_ref,
    send_o,
    sums_in,
    table_ref,
    tx_ref,
    ty_ref,
    tyl_ref,
    tz_ref,
    tzl_ref,
    rp_ref,
    ip_ref,
    cc_ref,
    rs_ref,
    uu_ref,
    xx_ref,
    edge_ref,
    plane_e,
    *refs,
):
    ny, planes = sizes.ny, sizes.planes
    rows = planes * ny
    even = lax.axis_index("gx") % 2 == 0
    if first:
        plane_o, _, _, p_old, s_old, p_ref, s_ref, rows_ref, sums_out, send_e, near_ref = refs
        halo = None
        near_weights(sizes, cell_ref, weight_ref, plane_e, plane_o, near_ref)
    else:
        halo, _, _, p_old, s_old, p_ref, s_ref, rows_ref, sums_out, send_e = refs
    finish_core_plane(sizes, cell_ref, p_old, s_old, mu_ref, wp_ref, ws_ref, halo, plane_e, send_e)
    before = table_ref[BEFORE * sizes.groups : (BEFORE + 1) * sizes.groups, :]
    put_sums(sizes, jnp.logical_not(even), before, sums_in[...], sums_out, send_e)
    add_wells(sizes, cell_ref, mu_ref, wp_ref, ws_ref, p_old, s_old, SUB)
    put_planes(sizes, even, send_e, send_o, p_old, s_old, SUB)

    @pl.loop(0, ny // SUB)
    def _(r):
        y0 = pl.multiple_of(r * SUB, SUB)
        here = [pl.ds(y0 + (x * ny + SUB), SUB) for x in range(planes)]
        ps = [p_old[at, :] for at in here]
        ss = [s_old[at, :] for at in here]
        tx = None
        for x in range(planes):
            at = pl.ds(y0 + x * ny, SUB)
            up = pl.ds(y0 + (x * ny + SUB + 1), SUB)
            down = pl.ds(y0 + (x * ny + SUB - 1), SUB)
            txl = tx
            tx = tx_ref[at, :] if x < planes - 1 else None
            ty, tyl, tz, tzl = ty_ref[at, :], tyl_ref[at, :], tz_ref[at, :], tzl_ref[at, :]

            def neighbours(fields, old):
                mid = fields[x]
                total = tz * pltpu.roll(mid, LANES - 1, 1) + tzl * pltpu.roll(mid, 1, 1)
                total = total + (ty * old[up, :] + tyl * old[down, :])
                if x < planes - 1:
                    total = total + tx * fields[x + 1]
                if x > 0:
                    total = total + txl * fields[x - 1]
                return total

            sum_p = neighbours(ps, p_old)
            sum_s = neighbours(ss, s_old)
            if x == 0:
                ip, cc, rp, rs, uu, xx = [edge_ref[pl.ds(y0 + i * ny, SUB), :] for i in range(6)]
            else:
                ip, cc, rp, rs, uu, xx = [ref[at, :] for ref in (ip_ref, cc_ref, rp_ref, rs_ref, uu_ref, xx_ref)]
            p = rp + ip * sum_p + cc * sum_s
            p_ref[here[x], :] = p
            s_ref[here[x], :] = rs + uu * sum_s - xx * p

    clear_ends(rows, p_ref, s_ref)
    path_rows(sizes, cell_ref, weight_ref, p_ref, rows_ref)


def facing_kernel(sizes, cell_ref, from_o, p_ref, s_ref, plane_o, near_ref, send_o, sums_ref):
    even = lax.axis_index("gx") % 2 == 0
    x_o, _ = facing(sizes, even)
    finish_plane(sizes, x_o, p_ref, s_ref, from_o, plane_o, send_o)
    near_sums(sizes, cell_ref, from_o, near_ref, 0, sums_ref)


def near_sums(sizes, cell_ref, halo, near_ref, side, sums_ref):
    groups = sizes.groups
    for g in range(groups):
        y = path_y(sizes, cell_ref, g)
        row = jnp.zeros((1, LANES), F32)
        for j in range(2):
            at = (2 * side + j) * groups + g
            row = row + near_ref[at : at + 1, :] * halo[pl.ds(y + j * sizes.ny, 1), :]
        sums_ref[g : g + 1, :] = row


def outer_kernel(
    sizes,
    final,
    cell_ref,
    send_in,
    from_o,
    from_e,
    rows_ref,
    near_o,
    sums_in,
    table_ref,
    wp_ref,
    ws_ref,
    shared_ref,
    near_ref,
    send_o,
    mu_ref,
    *rest,
):
    ny, groups = sizes.ny, sizes.groups
    near_e = rest[-1]
    even = lax.axis_index("gx") % 2 == 0
    x_o, _ = facing(sizes, even)

    def table(i):
        return table_ref[i * groups : (i + 1) * groups, :]

    tail = slice(2 * ny, 2 * ny + SUB)
    come_e, come_o = from_e[tail, :], from_o[tail, :]
    low = rows_of(jnp.where(even, come_o, come_e), groups)
    high = rows_of(jnp.where(even, come_e, come_o), groups)
    before = table(BEFORE)
    total = spread(lane_sum(sums_in[...] + jnp.where(before > 0.5, low, high)), groups)
    mu = (table(RHS) + total) * table(INV)
    mu_ref[...] = mu
    near_sums(sizes, cell_ref, from_e, near_ref, 1, near_e)
    by_lane = rows_ref[...] + near_o[...] + near_e[...] + shared_ref[...] * row_of(mu, groups)
    add_wells_to_plane(sizes, cell_ref, mu_ref, wp_ref, ws_ref, x_o, send_o)
    if not final:
        put_sums(sizes, even, before, by_lane, rest[0], send_o)
        return
    total_own = spread(lane_sum(sums_in[...] * (1.0 - before) + high), groups)
    total = spread(lane_sum(by_lane), groups)
    part_own, part_before = total * (1.0 - before), total * before
    grads_ref = rest[0]
    mu_own = (table(RHS_OWN) + total_own) * table(INV_OWN)
    grad_own = mu_own * table(SUM_OWN) - part_own
    grad_before = -part_before
    lane = iota((SUB, LANES), 1).astype(F32)
    outside = lane >= groups
    values = []
    for slots, grad in ((table(SLOT_OWN), grad_own), (table(SLOT_BEFORE), grad_before)):
        for q in range(groups // SUB):
            part = slice(q * SUB, (q + 1) * SUB)
            values.append((jnp.where(outside, -1.0, slots[part, :] - lane), grad[part, :]))
    for d in range(sizes.devices):
        total = jnp.zeros((SUB, LANES), F32)
        for slot, grad in values:
            total = total + jnp.where(slot == float(d * groups), grad, 0.0)
        grads_ref[d] = jnp.sum(total, axis=0, keepdims=True)


def final_kernel(
    sizes,
    cell_ref,
    p_in,
    s_in,
    mu_ref,
    wp_ref,
    ws_ref,
    plane_e,
    send_o,
    from_e,
    p_old,
    s_old,
    p_out,
    s_out,
    send_e,
    sems,
):
    rows = sizes.planes * sizes.ny
    even = lax.axis_index("gx") % 2 == 0
    finish_core_plane(sizes, cell_ref, p_old, s_old, mu_ref, wp_ref, ws_ref, from_e, plane_e, send_e)
    add_wells(sizes, cell_ref, mu_ref, wp_ref, ws_ref, p_old, s_old, SUB)
    put_planes(sizes, even, send_e, send_o, p_old, s_old, SUB)
    copies = [
        pltpu.make_async_copy(field.at[pl.ds(SUB, rows)], out, sems.at[i])
        for i, (field, out) in enumerate(((p_old, p_out), (s_old, s_out)))
    ]
    for copy in copies:
        copy.start()
    for copy in copies:
        copy.wait()


class Sizes:
    def __init__(self, planes, ny, groups, run, devices):
        self.planes, self.ny, self.groups, self.run, self.devices = planes, ny, groups, run, devices


def body(
    rhs_pressure,
    rhs_saturation,
    trans_x,
    trans_y,
    trans_z,
    coupling,
    upwind,
    storage,
    cross,
    accel,
    perf_cell,
    perf_well,
    perf_index,
    well_rhs,
    well_slot,
):
    planes, ny, nz = trans_x.shape
    devices = lax.axis_size("gx")
    groups = well_rhs.shape[0] // devices
    run = perf_cell.shape[0] // groups
    sizes = Sizes(planes, ny, groups, run, devices)
    rows = planes * ny
    padded = rows + 2 * SUB
    SMEM, VMEM, HBM, DMA = pltpu.SMEM, pltpu.VMEM, pltpu.HBM, pltpu.SemaphoreType.DMA

    def flat(array):
        return array.reshape(rows, nz)

    def lines(array):
        return array.reshape(-1, LANES)

    def call(kernel, args, spaces, outs, scratch, name, micros, aliases=None):
        return pl.pallas_call(
            kernel,
            in_specs=[spec(space) for space in spaces],
            out_specs=[spec(out.memory_space) for out in outs],
            out_shape=outs,
            scratch_shapes=scratch,
            input_output_aliases=aliases or {},
            compiler_params=pltpu.CompilerParams(vmem_limit_bytes=16 * 1024 * 1024),
            cost_estimate=pl.CostEstimate(flops=int(micros * 4e6), bytes_accessed=int(micros * 3e6), transcendentals=0),
            name=name,
        )(*[placed(a, space) for a, space in zip(args, spaces)])

    def call_vmem(kernel, args, outs, scratch, name, micros, aliases=None):
        return call(
            functools.partial(kernel, sizes), [y] + args, [SMEM] + [VMEM] * len(args), outs, scratch,
            name, micros, aliases,
        )

    pairs_e = [(i, i ^ 1) for i in range(devices) if i ^ 1 < devices]
    pairs_o = []
    for i in range(1, devices - 1, 2):
        pairs_o += [(i, i + 1), (i + 1, i)]

    def to_core(block):
        return lax.ppermute(block, "gx", pairs_e)

    def to_chip(block):
        return lax.ppermute(block, "gx", pairs_o)

    index = lines(perf_index)
    send, wells = call(
        functools.partial(first_kernel, sizes),
        [flat(trans_x), lines(perf_well), index],
        [HBM, HBM, HBM],
        [vmem(ny + SUB), vmem(2 * groups)],
        [VMEM(index.shape, jnp.int32), VMEM(index.shape, F32), DMA((3,))],
        "first",
        1,
    )
    from_o = to_chip(send)
    from_e = to_core(send)
    big = [trans_x, trans_y, trans_z, accel, coupling, upwind, storage, rhs_pressure, rhs_saturation, cross]
    made = call(
        functools.partial(setup_kernel, sizes),
        [perf_cell, perf_index, lines(well_rhs), lines(well_slot)] + big,
        [HBM] * (4 + len(big)),
        [vmem(rows)] * 11 + [vmem(3 * ny), vmem(groups * SUB), SMEM((groups,), jnp.int32)]
        + [vmem(padded), vmem(padded), vmem(4 * groups)],
        [
            VMEM((planes, ny, LANES), F32),
            VMEM((planes, ny + SUB, LANES), F32),
        ]
        + [VMEM((planes, ny, LANES), F32)] * 8
        + [
            VMEM((rows, LANES), F32),
            SMEM(perf_cell.shape, jnp.int32),
            SMEM(perf_index.shape, F32),
            VMEM(lines(well_rhs).shape, F32),
            VMEM(lines(well_slot).shape, jnp.int32),
            DMA((CHUNKS, 10)),
            DMA((4,)),
        ],
        "setup",
        4,
    )
    coefficients, (extra, weight, y, p, s, lanes) = list(made[:11]), made[11:]
    group_row = VMEM((groups, LANES), F32)
    fields = [vmem(padded), vmem(padded)]
    block = vmem(2 * ny + SUB)
    slabs = vmem(groups * SUB)
    p, s, edge, plane_e, plane_o, wp, ws, shared, table, mu, sums, send_o = call(
        functools.partial(start_kernel, sizes),
        [y, from_o, from_e, wells, coefficients[0]] + coefficients[5:] + [extra, weight, lanes, p, s],
        [SMEM] + [VMEM] * 15,
        fields
        + [vmem(6 * ny), vmem(4 * ny), vmem(4 * ny), slabs, slabs, vmem(groups), vmem(TABLE * groups)]
        + [vmem(groups), vmem(groups), block],
        [group_row],
        "start",
        2,
        {14: 0, 15: 1},
    )
    near = None
    for sweep in range(1, SWEEPS):
        final = sweep == SWEEPS - 1
        next_o = to_chip(send_o)
        first = sweep == 1
        _, _, p, s, by_lane, sums, send_e, *rest = call_vmem(
            lambda sz, *refs: inner_kernel(sz, first, *refs),
            [mu, wp, ws, weight, send_o, sums, table]
            + coefficients
            + [edge, plane_e, plane_o if first else from_e, p, s],
            fields + fields + [vmem(groups), vmem(groups), block] + ([vmem(4 * groups)] if first else []),
            [],
            "inner",
            2,
            {22: 0, 23: 1},
        )
        if first:
            near = rest[0]
        next_e = to_core(send_e)
        from_e, from_o = next_e, next_o
        half_o, near_o = call_vmem(
            facing_kernel, [from_o, p, s, plane_o, near], [block, vmem(groups)], [], "facing", 0.5
        )
        send_o, mu, sums = call_vmem(
            lambda sz, *refs: outer_kernel(sz, final, *refs),
            [half_o, from_o, from_e, by_lane, near_o, sums, table, wp, ws, shared, near],
            [block, vmem(groups), pltpu.VMEM((devices, 1, LANES), F32) if final else vmem(groups)],
            [group_row],
            "outer",
            1,
            {1: 0},
        )
    grads = lax.all_to_all(sums, "gx", 0, 0)
    result = pltpu.HBM((rows, nz), F32)
    _, _, p, s = call_vmem(
        final_kernel,
        [p, s, mu, wp, ws, plane_e, send_o, from_e],
        fields + [result, result],
        [VMEM((2 * ny + SUB, LANES), F32), DMA((2,))],
        "final",
        2,
        {1: 0, 2: 1},
    )
    control = jnp.sum(grads, axis=(0, 1))[:groups]
    shape = trans_x.shape
    return p.reshape(shape), s.reshape(shape), control


def solution(mesh):
    grid = P(("ens", "gx"), None, None)
    line = P(("ens", "gx"))
    return jax.shard_map(
        body,
        mesh=mesh,
        in_specs=(grid,) * 10 + (line,) * 3 + (P("ens"), P("ens")),
        out_specs=(grid, grid, line),
        check_vma=False,
    )
```

```python
import functools

import jax
import jax.numpy as jnp
from jax import lax
from jax.experimental import pallas as pl
from jax.experimental.pallas import tpu as pltpu
from jax.sharding import PartitionSpec as P

SWEEPS = 6
SUB = 8
LANES = 128
F32 = jnp.float32
CHUNKS = 4


def vmem(rows):
    return pltpu.VMEM((rows, LANES), F32)


def placed(array, space):
    return array if space is pltpu.SMEM else pltpu.with_memory_space_constraint(array, space)


def spec(space):
    return pl.BlockSpec(memory_space=space)


def iota(shape, dim):
    return lax.broadcasted_iota(jnp.int32, shape, dim)


def lane_sum(block):
    return jnp.sum(block, axis=1, keepdims=True)


def spread(column, groups):
    return jnp.broadcast_to(column, (groups, LANES))


def row_of(column, groups):
    mine = iota((groups, LANES), 0) == iota((groups, LANES), 1)
    return jnp.sum(jnp.where(mine, column, 0.0), axis=0, keepdims=True)


def column_of(row, groups):
    mine = iota((groups, LANES), 0) == iota((groups, LANES), 1)
    return spread(lane_sum(jnp.where(mine, jnp.broadcast_to(row, (groups, LANES)), 0.0)), groups)


def well_block(part_own, part_before, groups):
    sub = iota((SUB, LANES), 0)
    own = jnp.broadcast_to(row_of(part_own, groups), (SUB, LANES))
    before = jnp.broadcast_to(row_of(part_before, groups), (SUB, LANES))
    return jnp.where(sub == 0, own, jnp.where(sub == 1, before, 0.0))


def group_rows(ref, groups, run):
    per_row = LANES // run
    return jnp.concatenate(
        [jnp.broadcast_to(ref[i : i + 1, :], (per_row, LANES)) for i in range(groups // per_row)], axis=0
    )


def first_kernel(
    sizes, tx_hbm, well_hbm, index_hbm, rhs_hbm, slot_hbm, send_ref, wells_ref, well_ref, index_ref, rhs_ref, slot_ref, sems
):
    ny, groups, run = sizes.ny, sizes.groups, sizes.run
    plane = pltpu.make_async_copy(
        tx_hbm.at[pl.ds((sizes.planes - 1) * ny, ny)], send_ref.at[pl.ds(0, ny)], sems.at[0]
    )
    get_well = pltpu.make_async_copy(well_hbm, well_ref, sems.at[1])
    get_index = pltpu.make_async_copy(index_hbm, index_ref, sems.at[2])
    get_rhs = pltpu.make_async_copy(rhs_hbm, rhs_ref, sems.at[3])
    get_slot = pltpu.make_async_copy(slot_hbm, slot_ref, sems.at[4])
    for copy in (get_well, get_index, plane, get_rhs, get_slot):
        copy.start()
    place = lax.axis_index("gx")
    shape = (groups, LANES)
    per_row = LANES // run
    local = iota(shape, 0) % per_row
    lane = iota(shape, 1)
    get_well.wait()
    get_index.wait()
    weights = jnp.where(lane // run == local, group_rows(index_ref, groups, run), 0.0)
    total = lane_sum(weights)
    first = jnp.where(lane == local * run, group_rows(well_ref, groups, run).astype(F32), 0.0)
    well = lane_sum(first)
    before = well < (place * groups).astype(F32)
    before = spread(jnp.where(before, 1.0, 0.0), groups)
    total = spread(total, groups)
    wells_ref[0:groups, :] = before
    wells_ref[groups : 2 * groups, :] = total
    send_ref[ny : ny + SUB, :] = well_block(total * (1.0 - before), total * before, groups)
    get_rhs.wait()
    get_slot.wait()
    behind = jnp.maximum(place - 1, 0)
    for i, (ref, whose) in enumerate(((rhs_ref, place), (rhs_ref, behind), (slot_ref, place), (slot_ref, behind))):
        wells_ref[(i + 2) * groups : (i + 3) * groups, :] = own_lanes(ref, whose, groups)
    plane.wait()


def split_cell(cell, ny):
    if ny & (ny - 1):
        row = lax.div(cell, LANES)
        return lax.div(row, ny), lax.rem(row, ny), lax.rem(cell, LANES)
    bits_z, bits_y = LANES.bit_length() - 1, ny.bit_length() - 1
    row = lax.shift_right_logical(cell, bits_z)
    return lax.shift_right_logical(row, bits_y), row & (ny - 1), cell & (LANES - 1)


def setup_kernel(
    sizes,
    cell_hbm,
    index_hbm,
    tx_hbm,
    ty_hbm,
    tz_hbm,
    accel_hbm,
    coupling_hbm,
    upwind_hbm,
    storage_hbm,
    rhs_p_hbm,
    rhs_s_hbm,
    cross_hbm,
    tx_ref,
    ty_ref,
    tyl_ref,
    tz_ref,
    tzl_ref,
    rp_ref,
    ip_ref,
    cc_ref,
    rs_ref,
    uu_ref,
    xx_ref,
    extra_ref,
    weight_ref,
    y_ref,
    raw_tx,
    raw_ty,
    raw_tz,
    raw_accel,
    raw_coupling,
    raw_upwind,
    raw_storage,
    raw_rhs_p,
    raw_rhs_s,
    raw_cross,
    cwi_ref,
    cell_ref,
    index_ref,
    sems,
    fetch_sems,
):
    ny, planes, groups, run = sizes.ny, sizes.planes, sizes.groups, sizes.run
    rows = planes * ny
    part = ny // CHUNKS
    moves = [
        (tx_hbm, raw_tx),
        (ty_hbm, raw_ty),
        (tz_hbm, raw_tz),
        (accel_hbm, raw_accel),
        (coupling_hbm, raw_coupling),
        (upwind_hbm, raw_upwind),
        (storage_hbm, raw_storage),
        (rhs_p_hbm, raw_rhs_p),
        (rhs_s_hbm, raw_rhs_s),
        (cross_hbm, raw_cross),
    ]

    def copies(c):
        found = []
        for i, (src, dst) in enumerate(moves):
            start = pl.multiple_of(c * part, SUB)
            to = pl.multiple_of(start + SUB, SUB) if dst is raw_ty else start
            found.append(
                pltpu.make_async_copy(src.at[:, pl.ds(start, part)], dst.at[:, pl.ds(to, part)], sems.at[c, i])
            )
        return found

    fetches = [
        pltpu.make_async_copy(src, dst, fetch_sems.at[i])
        for i, (src, dst) in enumerate(((cell_hbm, cell_ref), (index_hbm, index_ref)))
    ]
    for fetch in fetches:
        fetch.start()
    for c in range(CHUNKS):
        for copy in copies(c):
            copy.start()

    last = lax.axis_index("gx") == lax.axis_size("gx") - 1
    keep_last = jnp.where(last, 0.0, 1.0)
    zero = jnp.zeros((SUB, LANES), F32)

    @pl.loop(0, rows // SUB, unroll=8)
    def _(i):
        cwi_ref[pl.ds(pl.multiple_of(i * SUB, SUB), SUB), :] = zero

    for fetch in fetches:
        fetch.wait()
    spot = iota((SUB, LANES), 0) * LANES + iota((SUB, LANES), 1)
    for g in range(groups):
        _, y, _ = split_cell(cell_ref[g * run], ny)
        y_ref[g] = y
        weight = zero
        for k in range(g * run, (g + 1) * run):
            x, _, z = split_cell(cell_ref[k], ny)
            weight = weight + jnp.where(spot == x * LANES + z, index_ref[k], 0.0)
        weight_ref[g * SUB : (g + 1) * SUB, :] = weight
        slab = pl.ds(y, planes, ny)
        cwi_ref[slab, :] = cwi_ref[slab, :] + weight

    lane = iota((SUB, LANES), 1)
    sub = iota((SUB, LANES), 0)

    @pl.loop(0, CHUNKS)
    def _(c):
        for copy in copies(c):
            copy.wait()

        @pl.loop(0, part // SUB)
        def _(r):
            y0 = pl.multiple_of(c * part + r * SUB, SUB)
            ypos = sub + y0
            here = pl.ds(y0, SUB)
            txl = None
            for x in range(planes):
                at = pl.ds(y0 + x * ny, SUB)
                tx = raw_tx[x, here, :]
                if x == planes - 1:
                    tx = tx * keep_last
                tx_ref[at, :] = tx
                ty = jnp.where(ypos == ny - 1, 0.0, raw_ty[x, pl.ds(y0 + SUB, SUB), :])
                tyl = jnp.where(ypos == 0, 0.0, raw_ty[x, pl.ds(y0 + SUB - 1, SUB), :])
                tz = jnp.where(lane == LANES - 1, 0.0, raw_tz[x, here, :])
                tzl = pltpu.roll(tz, 1, 1)
                ty_ref[at, :] = ty
                tyl_ref[at, :] = tyl
                tz_ref[at, :] = tz
                tzl_ref[at, :] = tzl
                tsum = tx + ty + tyl + tz + tzl
                if x > 0:
                    tsum = tsum + txl
                accel = raw_accel[x, here, :]
                coupling = raw_coupling[x, here, :]
                upwind = raw_upwind[x, here, :]
                to_p = accel * (1.0 + jnp.abs(coupling))
                to_s = accel * jnp.abs(upwind)
                dp = to_p * tsum + accel * cwi_ref[at, :]
                ds = to_s * tsum + raw_storage[x, here, :]
                rhs_p, rhs_s, cross = raw_rhs_p[x, here, :], raw_rhs_s[x, here, :], raw_cross[x, here, :]
                if x == 0:
                    extra_ref[here, :] = to_p
                    extra_ref[pl.ds(y0 + ny, SUB), :] = to_s
                    extra_ref[pl.ds(y0 + 2 * ny, SUB), :] = ds
                    ip_ref[at, :] = dp
                    ip, is_ = 1.0, 1.0
                else:
                    ip = 1.0 / dp
                    is_ = 1.0 / ds
                    ip_ref[at, :] = ip
                cc_ref[at, :] = coupling * ip
                rp_ref[at, :] = rhs_p * ip
                rs_ref[at, :] = rhs_s * is_
                uu_ref[at, :] = upwind * is_
                xx_ref[at, :] = cross * is_
                txl = tx


def own_lanes(ref, place, groups):
    shape = (groups, LANES)
    start = place * groups
    row = jnp.broadcast_to(ref[pl.ds(start // LANES, 1), :].astype(F32), shape)
    mine = iota(shape, 1) == iota(shape, 0) + start % LANES
    return spread(lane_sum(jnp.where(mine, row, 0.0)), groups)


def clear_ends(rows, *refs):
    zero = jnp.zeros((SUB, LANES), F32)
    for ref in refs:
        ref[0:SUB, :] = zero
        ref[rows + SUB : rows + 2 * SUB, :] = zero


def path_y(sizes, cell_ref, g):
    return cell_ref[g]


def slab_of(sizes, cell_ref, g, pad):
    return pl.ds(path_y(sizes, cell_ref, g) + pad, sizes.planes, sizes.ny)


def add_wells(sizes, cell_ref, mu_ref, wp_ref, ws_ref, p_ref, s_ref, pad):
    for g in range(sizes.groups):
        slab = slab_of(sizes, cell_ref, g, pad)
        at = pl.ds(g * SUB, SUB)
        mu = mu_ref[g : g + 1, :]
        p_ref[slab, :] = p_ref[slab, :] + mu * wp_ref[at, :]
        s_ref[slab, :] = s_ref[slab, :] - mu * ws_ref[at, :]


def add_wells_to_plane(sizes, cell_ref, mu_ref, wp_ref, ws_ref, x, send_ref):
    for g in range(sizes.groups):
        y = path_y(sizes, cell_ref, g)
        in_p, in_s, at = pl.ds(y, 1), pl.ds(y + sizes.ny, 1), pl.ds(x + g * SUB, 1)
        mu = mu_ref[g : g + 1, :]
        send_ref[in_p, :] = send_ref[in_p, :] + mu * wp_ref[at, :]
        send_ref[in_s, :] = send_ref[in_s, :] - mu * ws_ref[at, :]


def path_rows(sizes, cell_ref, weight_ref, p_ref, rows_ref):
    for g in range(sizes.groups):
        slab = slab_of(sizes, cell_ref, g, SUB)
        at = pl.ds(g * SUB, SUB)
        rows_ref[g : g + 1, :] = jnp.sum(p_ref[slab, :] * weight_ref[at, :], axis=0, keepdims=True)


def facing(sizes, even):
    last = sizes.planes - 1
    return jnp.where(even, 0, last), jnp.where(even, last, 0)


def finish_plane(sizes, x, p_ref, s_ref, halo_ref, plane_ref, send_ref):
    ny = sizes.ny
    start = pl.multiple_of(x * ny + SUB, SUB)
    for r in range(0, ny, SUB):
        at = slice(r, r + SUB)
        at_s = slice(ny + r, ny + r + SUB)
        p, s = p_ref[pl.ds(start + r, SUB), :], s_ref[pl.ds(start + r, SUB), :]
        if halo_ref is not None:
            hp, hs = halo_ref[at, :], halo_ref[at_s, :]
            a, b, c, xx = [plane_ref[i * ny + r : i * ny + r + SUB, :] for i in range(4)]
            change = a * hp + b * hs
            p = p + change
            s = s + c * hs - xx * change
        send_ref[at, :] = p
        send_ref[at_s, :] = s


BEFORE, RHS_OWN, INV_OWN, SUM_OWN, RHS, INV, SLOT_OWN, SLOT_BEFORE, TABLE = range(9)


def shared_cells(sizes, cell_ref, weight_ref, wp_ref, out_ref):
    groups = sizes.groups
    shape = (groups, LANES)
    sub, lane = iota(shape, 0), iota(shape, 1)
    y_row = jnp.full(shape, -1, jnp.int32)
    y_col = y_row
    for g in range(groups):
        y = path_y(sizes, cell_ref, g)
        y_row = jnp.where(lane == g, y, y_row)
        y_col = jnp.where(sub == g, y, y_col)
    total = jnp.zeros(shape, F32)
    empty = jnp.zeros((LANES - groups, LANES), F32)
    for x in range(sizes.planes):
        at = pl.ds(x, groups, SUB)
        other = jnp.concatenate([wp_ref[at, :], empty], axis=0)
        total = total + lax.dot_general(
            weight_ref[at, :], other, (((1,), (1,)), ((), ())),
            precision=lax.Precision.HIGHEST, preferred_element_type=F32,
        )
    out_ref[...] = jnp.where(y_row == y_col, total, 0.0)


def start_kernel(
    sizes,
    cell_ref,
    from_o,
    from_e,
    wells_ref,
    tx_ref,
    rp_ref,
    ip_ref,
    cc_ref,
    rs_ref,
    uu_ref,
    xx_ref,
    extra_ref,
    weight_ref,
    edge_ref,
    plane_e,
    plane_o,
    wp_ref,
    ws_ref,
    shared_ref,
    table_ref,
    mu_ref,
    sums_out,
    send_o,
    rows_ref,
):
    ny, planes, groups = sizes.ny, sizes.planes, sizes.groups
    place = lax.axis_index("gx")
    even = place % 2 == 0
    x_o, _ = facing(sizes, even)

    @pl.loop(0, ny // SUB)
    def _(r):
        y0 = pl.multiple_of(r * SUB, SUB)
        at = pl.ds(y0, SUB)
        txl = jnp.where(even, from_o[at, :], from_e[at, :])
        ip = 1.0 / (ip_ref[at, :] + extra_ref[at, :] * txl)
        is_ = 1.0 / (extra_ref[pl.ds(y0 + 2 * ny, SUB), :] + extra_ref[pl.ds(y0 + ny, SUB), :] * txl)
        cc, uu = cc_ref[at, :] * ip, uu_ref[at, :] * is_
        rp, rs, xx = rp_ref[at, :] * ip, rs_ref[at, :] * is_, xx_ref[at, :] * is_
        for i, value in enumerate([ip, cc, rp, rs, uu, xx]):
            edge_ref[pl.ds(y0 + i * ny, SUB), :] = value
        end = pl.ds(y0 + (planes - 1) * ny, SUB)
        tx = tx_ref[end, :]
        low = [ip * txl, cc * txl, uu * txl, xx]
        high = [ip_ref[end, :] * tx, cc_ref[end, :] * tx, uu_ref[end, :] * tx, xx_ref[end, :]]
        for i in range(4):
            to = pl.ds(y0 + i * ny, SUB)
            plane_o[to, :] = jnp.where(even, low[i], high[i])
            plane_e[to, :] = jnp.where(even, high[i], low[i])
        rp_end = rp_ref[end, :]
        send_o[at, :] = jnp.where(even, rp, rp_end)
        send_o[pl.ds(y0 + ny, SUB), :] = jnp.where(
            even, rs - xx * rp, rs_ref[end, :] - xx_ref[end, :] * rp_end
        )

    sub = iota((SUB, LANES), 0)
    for g in range(groups):
        y = path_y(sizes, cell_ref, g)
        at = pl.ds(g * SUB, SUB)
        slab = pl.ds(y, planes, ny)
        ip = jnp.where(sub == 0, edge_ref[pl.ds(y, 1), :], ip_ref[slab, :])
        xx = jnp.where(sub == 0, edge_ref[pl.ds(y + 5 * ny, 1), :], xx_ref[slab, :])
        rp = jnp.where(sub == 0, edge_ref[pl.ds(y + 2 * ny, 1), :], rp_ref[slab, :])
        rows_ref[g : g + 1, :] = jnp.sum(weight_ref[at, :] * rp, axis=0, keepdims=True)
        wp = weight_ref[at, :] * ip
        wp_ref[at, :] = wp
        ws_ref[at, :] = wp * xx
    shared_cells(sizes, cell_ref, weight_ref, wp_ref, shared_ref)

    tile_e, tile_o = from_e[ny : ny + SUB, :], from_o[ny : ny + SUB, :]
    low = jnp.where(even, tile_o, tile_e)
    high = jnp.where(even, tile_e, tile_o)
    before = wells_ref[0:groups, :]
    mine = wells_ref[groups : 2 * groups, :]
    is_before = before > 0.5
    sum_own = mine * (1.0 - before) + column_of(high[1:2, :], groups)
    sum_before = mine * before + column_of(low[0:1, :], groups)
    rhs_own, rhs_before, slot_own, slot_before = [
        wells_ref[i * groups : (i + 1) * groups, :] for i in range(2, 6)
    ]
    inv_own = 1.0 / (1.5 * sum_own + 0.5)
    inv_before = 1.0 / (1.5 * sum_before + 0.5)
    rhs = jnp.where(is_before, rhs_before, rhs_own)
    inv = jnp.where(is_before, inv_before, inv_own)
    entries = {
        BEFORE: before,
        RHS_OWN: rhs_own,
        INV_OWN: inv_own,
        SUM_OWN: sum_own,
        RHS: rhs,
        INV: inv,
        SLOT_OWN: slot_own,
        SLOT_BEFORE: slot_before,
    }
    for i, entry in entries.items():
        table_ref[i * groups : (i + 1) * groups, :] = entry
    mu = rhs * inv
    mu_ref[...] = mu

    add_wells_to_plane(sizes, cell_ref, mu_ref, wp_ref, ws_ref, x_o, send_o)
    put_sums(sizes, even, before, rows_ref[...] + shared_ref[...] * row_of(mu, groups), sums_out, send_o)


def put_sums(sizes, to_before, before, by_lane, rows_out, send_ref):
    ny, groups = sizes.ny, sizes.groups
    rows_out[...] = by_lane
    shared = by_lane * jnp.where(to_before, before, 1.0 - before)
    parts = groups // SUB
    lane = iota((SUB, LANES), 1)
    tile = jnp.zeros((SUB, LANES), F32)
    for q in range(parts):
        part = shared[q * SUB : (q + 1) * SUB, :]
        width = LANES
        while width > LANES // parts:
            width //= 2
            part = part + pltpu.roll(part, width, 1)
        tile = jnp.where(lane // (LANES // parts) == q, part, tile)
    send_ref[2 * ny : 2 * ny + SUB, :] = tile


def rows_of(tile, groups):
    parts = groups // SUB
    lane = iota((SUB, LANES), 1)
    return jnp.concatenate(
        [jnp.where(lane // (LANES // parts) == q, tile, 0.0) for q in range(parts)], axis=0
    )


def finish_core_plane(sizes, cell_ref, p_ref, s_ref, mu_ref, wp_ref, ws_ref, halo, plane_e, send_e):
    even = lax.axis_index("gx") % 2 == 0
    _, x_e = facing(sizes, even)
    finish_plane(sizes, x_e, p_ref, s_ref, halo, plane_e, send_e)
    add_wells_to_plane(sizes, cell_ref, mu_ref, wp_ref, ws_ref, x_e, send_e)


def near_weights(sizes, cell_ref, weight_ref, plane_e, plane_o, near_ref):
    ny, groups = sizes.ny, sizes.groups
    even = lax.axis_index("gx") % 2 == 0
    x_o, x_e = facing(sizes, even)
    for g in range(groups):
        y = path_y(sizes, cell_ref, g)
        for i, (x, plane) in enumerate(((x_o, plane_o), (x_e, plane_e))):
            weight = weight_ref[pl.ds(x + g * SUB, 1), :]
            for j in range(2):
                to = (2 * i + j) * groups + g
                near_ref[to : to + 1, :] = weight * plane[pl.ds(y + j * ny, 1), :]


def put_planes(sizes, even, send_e, send_o, p_ref, s_ref, pad):
    ny = sizes.ny
    x_o, x_e = facing(sizes, even)
    for send, x in ((send_o, x_o), (send_e, x_e)):
        start = pl.multiple_of(x * ny + pad, SUB)
        for r in range(0, ny, SUB):
            p_ref[pl.ds(start + r, SUB), :] = send[r : r + SUB, :]
            s_ref[pl.ds(start + r, SUB), :] = send[ny + r : ny + r + SUB, :]


def inner_kernel(
    sizes,
    first,
    cell_ref,
    mu_ref,
    wp_ref,
    ws_ref,
    weight_ref,
    send_o,
    sums_in,
    table_ref,
    tx_ref,
    ty_ref,
    tyl_ref,
    tz_ref,
    tzl_ref,
    rp_ref,
    ip_ref,
    cc_ref,
    rs_ref,
    uu_ref,
    xx_ref,
    edge_ref,
    plane_e,
    *refs,
):
    ny, planes = sizes.ny, sizes.planes
    rows = planes * ny
    even = lax.axis_index("gx") % 2 == 0
    if first:
        plane_o, p_old, s_old, p_ref, s_ref, rows_ref, sums_out, send_e, near_ref = refs
        halo = None
        clear_ends(rows, p_old, s_old)

        @pl.loop(0, ny // SUB)
        def _(r):
            y0 = pl.multiple_of(r * SUB, SUB)
            for x in range(planes):
                at, to = pl.ds(y0 + x * ny, SUB), pl.ds(y0 + (x * ny + SUB), SUB)
                if x == 0:
                    rp, rs, xx = [edge_ref[pl.ds(y0 + i * ny, SUB), :] for i in (2, 3, 5)]
                else:
                    rp, rs, xx = rp_ref[at, :], rs_ref[at, :], xx_ref[at, :]
                p_old[to, :] = rp
                s_old[to, :] = rs - xx * rp

        near_weights(sizes, cell_ref, weight_ref, plane_e, plane_o, near_ref)
    else:
        halo, _, _, p_old, s_old, p_ref, s_ref, rows_ref, sums_out, send_e = refs
    finish_core_plane(sizes, cell_ref, p_old, s_old, mu_ref, wp_ref, ws_ref, halo, plane_e, send_e)
    before = table_ref[BEFORE * sizes.groups : (BEFORE + 1) * sizes.groups, :]
    put_sums(sizes, jnp.logical_not(even), before, sums_in[...], sums_out, send_e)
    add_wells(sizes, cell_ref, mu_ref, wp_ref, ws_ref, p_old, s_old, SUB)
    put_planes(sizes, even, send_e, send_o, p_old, s_old, SUB)

    @pl.loop(0, ny // SUB)
    def _(r):
        y0 = pl.multiple_of(r * SUB, SUB)
        here = [pl.ds(y0 + (x * ny + SUB), SUB) for x in range(planes)]
        ps = [p_old[at, :] for at in here]
        ss = [s_old[at, :] for at in here]
        tx = None
        for x in range(planes):
            at = pl.ds(y0 + x * ny, SUB)
            up = pl.ds(y0 + (x * ny + SUB + 1), SUB)
            down = pl.ds(y0 + (x * ny + SUB - 1), SUB)
            txl = tx
            tx = tx_ref[at, :] if x < planes - 1 else None
            ty, tyl, tz, tzl = ty_ref[at, :], tyl_ref[at, :], tz_ref[at, :], tzl_ref[at, :]

            def neighbours(fields, old):
                mid = fields[x]
                total = tz * pltpu.roll(mid, LANES - 1, 1) + tzl * pltpu.roll(mid, 1, 1)
                total = total + (ty * old[up, :] + tyl * old[down, :])
                if x < planes - 1:
                    total = total + tx * fields[x + 1]
                if x > 0:
                    total = total + txl * fields[x - 1]
                return total

            sum_p = neighbours(ps, p_old)
            sum_s = neighbours(ss, s_old)
            if x == 0:
                ip, cc, rp, rs, uu, xx = [edge_ref[pl.ds(y0 + i * ny, SUB), :] for i in range(6)]
            else:
                ip, cc, rp, rs, uu, xx = [ref[at, :] for ref in (ip_ref, cc_ref, rp_ref, rs_ref, uu_ref, xx_ref)]
            p = rp + ip * sum_p + cc * sum_s
            p_ref[here[x], :] = p
            s_ref[here[x], :] = rs + uu * sum_s - xx * p

    clear_ends(rows, p_ref, s_ref)
    path_rows(sizes, cell_ref, weight_ref, p_ref, rows_ref)


def facing_kernel(sizes, cell_ref, from_o, p_ref, s_ref, plane_o, near_ref, send_o, sums_ref):
    even = lax.axis_index("gx") % 2 == 0
    x_o, _ = facing(sizes, even)
    finish_plane(sizes, x_o, p_ref, s_ref, from_o, plane_o, send_o)
    near_sums(sizes, cell_ref, from_o, near_ref, 0, sums_ref)


def near_sums(sizes, cell_ref, halo, near_ref, side, sums_ref):
    groups = sizes.groups
    for g in range(groups):
        y = path_y(sizes, cell_ref, g)
        row = jnp.zeros((1, LANES), F32)
        for j in range(2):
            at = (2 * side + j) * groups + g
            row = row + near_ref[at : at + 1, :] * halo[pl.ds(y + j * sizes.ny, 1), :]
        sums_ref[g : g + 1, :] = row


def outer_kernel(
    sizes,
    final,
    cell_ref,
    send_in,
    from_o,
    from_e,
    rows_ref,
    near_o,
    sums_in,
    table_ref,
    wp_ref,
    ws_ref,
    shared_ref,
    near_ref,
    send_o,
    mu_ref,
    *rest,
):
    ny, groups = sizes.ny, sizes.groups
    near_e = rest[-1]
    even = lax.axis_index("gx") % 2 == 0
    x_o, _ = facing(sizes, even)

    def table(i):
        return table_ref[i * groups : (i + 1) * groups, :]

    tail = slice(2 * ny, 2 * ny + SUB)
    come_e, come_o = from_e[tail, :], from_o[tail, :]
    low = rows_of(jnp.where(even, come_o, come_e), groups)
    high = rows_of(jnp.where(even, come_e, come_o), groups)
    before = table(BEFORE)
    total = spread(lane_sum(sums_in[...] + jnp.where(before > 0.5, low, high)), groups)
    mu = (table(RHS) + total) * table(INV)
    mu_ref[...] = mu
    near_sums(sizes, cell_ref, from_e, near_ref, 1, near_e)
    by_lane = rows_ref[...] + near_o[...] + near_e[...] + shared_ref[...] * row_of(mu, groups)
    add_wells_to_plane(sizes, cell_ref, mu_ref, wp_ref, ws_ref, x_o, send_o)
    if not final:
        put_sums(sizes, even, before, by_lane, rest[0], send_o)
        return
    total_own = spread(lane_sum(sums_in[...] * (1.0 - before) + high), groups)
    total = spread(lane_sum(by_lane), groups)
    part_own, part_before = total * (1.0 - before), total * before
    grads_ref = rest[0]
    mu_own = (table(RHS_OWN) + total_own) * table(INV_OWN)
    grad_own = mu_own * table(SUM_OWN) - part_own
    grad_before = -part_before
    lane = iota((SUB, LANES), 1).astype(F32)
    outside = lane >= groups
    values = []
    for slots, grad in ((table(SLOT_OWN), grad_own), (table(SLOT_BEFORE), grad_before)):
        for q in range(groups // SUB):
            part = slice(q * SUB, (q + 1) * SUB)
            values.append((jnp.where(outside, -1.0, slots[part, :] - lane), grad[part, :]))
    for d in range(sizes.devices):
        total = jnp.zeros((SUB, LANES), F32)
        for slot, grad in values:
            total = total + jnp.where(slot == float(d * groups), grad, 0.0)
        grads_ref[d] = jnp.sum(total, axis=0, keepdims=True)


def final_kernel(
    sizes,
    cell_ref,
    p_in,
    s_in,
    mu_ref,
    wp_ref,
    ws_ref,
    plane_e,
    send_o,
    from_e,
    p_old,
    s_old,
    p_out,
    s_out,
    send_e,
    sems,
):
    rows = sizes.planes * sizes.ny
    even = lax.axis_index("gx") % 2 == 0
    finish_core_plane(sizes, cell_ref, p_old, s_old, mu_ref, wp_ref, ws_ref, from_e, plane_e, send_e)
    add_wells(sizes, cell_ref, mu_ref, wp_ref, ws_ref, p_old, s_old, SUB)
    put_planes(sizes, even, send_e, send_o, p_old, s_old, SUB)
    copies = [
        pltpu.make_async_copy(field.at[pl.ds(SUB, rows)], out, sems.at[i])
        for i, (field, out) in enumerate(((p_old, p_out), (s_old, s_out)))
    ]
    for copy in copies:
        copy.start()
    for copy in copies:
        copy.wait()


class Sizes:
    def __init__(self, planes, ny, groups, run, devices):
        self.planes, self.ny, self.groups, self.run, self.devices = planes, ny, groups, run, devices


def body(
    rhs_pressure,
    rhs_saturation,
    trans_x,
    trans_y,
    trans_z,
    coupling,
    upwind,
    storage,
    cross,
    accel,
    perf_cell,
    perf_well,
    perf_index,
    well_rhs,
    well_slot,
):
    planes, ny, nz = trans_x.shape
    devices = lax.axis_size("gx")
    groups = well_rhs.shape[0] // devices
    run = perf_cell.shape[0] // groups
    sizes = Sizes(planes, ny, groups, run, devices)
    rows = planes * ny
    padded = rows + 2 * SUB
    SMEM, VMEM, HBM, DMA = pltpu.SMEM, pltpu.VMEM, pltpu.HBM, pltpu.SemaphoreType.DMA

    def flat(array):
        return array.reshape(rows, nz)

    def lines(array):
        return array.reshape(-1, LANES)

    def call(kernel, args, spaces, outs, scratch, name, micros, aliases=None):
        return pl.pallas_call(
            kernel,
            in_specs=[spec(space) for space in spaces],
            out_specs=[spec(out.memory_space) for out in outs],
            out_shape=outs,
            scratch_shapes=scratch,
            input_output_aliases=aliases or {},
            compiler_params=pltpu.CompilerParams(vmem_limit_bytes=16 * 1024 * 1024),
            cost_estimate=pl.CostEstimate(flops=int(micros * 4e6), bytes_accessed=int(micros * 3e6), transcendentals=0),
            name=name,
        )(*[placed(a, space) for a, space in zip(args, spaces)])

    def call_vmem(kernel, args, outs, scratch, name, micros, aliases=None):
        return call(
            functools.partial(kernel, sizes), [y] + args, [SMEM] + [VMEM] * len(args), outs, scratch,
            name, micros, aliases,
        )

    pairs_e = [(i, i ^ 1) for i in range(devices) if i ^ 1 < devices]
    pairs_o = []
    for i in range(1, devices - 1, 2):
        pairs_o += [(i, i + 1), (i + 1, i)]

    def to_core(block):
        return lax.ppermute(block, "gx", pairs_e)

    def to_chip(block):
        return lax.ppermute(block, "gx", pairs_o)

    index = lines(perf_index)
    send, wells = call(
        functools.partial(first_kernel, sizes),
        [flat(trans_x), lines(perf_well), index, lines(well_rhs), lines(well_slot)],
        [HBM] * 5,
        [vmem(ny + SUB), vmem(6 * groups)],
        [
            VMEM(index.shape, jnp.int32),
            VMEM(index.shape, F32),
            VMEM(lines(well_rhs).shape, F32),
            VMEM(lines(well_slot).shape, jnp.int32),
            DMA((5,)),
        ],
        "first",
        1,
    )
    from_o = to_chip(send)
    from_e = to_core(send)
    big = [trans_x, trans_y, trans_z, accel, coupling, upwind, storage, rhs_pressure, rhs_saturation, cross]
    made = call(
        functools.partial(setup_kernel, sizes),
        [perf_cell, perf_index] + big,
        [HBM] * (2 + len(big)),
        [vmem(rows)] * 11 + [vmem(3 * ny), vmem(groups * SUB), SMEM((groups,), jnp.int32)],
        [
            VMEM((planes, ny, LANES), F32),
            VMEM((planes, ny + SUB, LANES), F32),
        ]
        + [VMEM((planes, ny, LANES), F32)] * 8
        + [
            VMEM((rows, LANES), F32),
            SMEM(perf_cell.shape, jnp.int32),
            SMEM(perf_index.shape, F32),
            DMA((CHUNKS, 10)),
            DMA((2,)),
        ],
        "setup",
        4,
    )
    coefficients, (extra, weight, y) = list(made[:11]), made[11:]
    group_row = VMEM((groups, LANES), F32)
    fields = [vmem(padded), vmem(padded)]
    block = vmem(2 * ny + SUB)
    slabs = vmem(groups * SUB)
    edge, plane_e, plane_o, wp, ws, shared, table, mu, sums, send_o = call(
        functools.partial(start_kernel, sizes),
        [y, from_o, from_e, wells, coefficients[0]] + coefficients[5:] + [extra, weight],
        [SMEM] + [VMEM] * 12,
        [vmem(6 * ny), vmem(4 * ny), vmem(4 * ny), slabs, slabs, vmem(groups), vmem(TABLE * groups)]
        + [vmem(groups), vmem(groups), block],
        [group_row],
        "start",
        2,
    )
    near = None
    for sweep in range(1, SWEEPS):
        final = sweep == SWEEPS - 1
        next_o = to_chip(send_o)
        first = sweep == 1
        _, _, p, s, by_lane, sums, send_e, *rest = call_vmem(
            lambda sz, *refs: inner_kernel(sz, first, *refs),
            [mu, wp, ws, weight, send_o, sums, table]
            + coefficients
            + ([edge, plane_e, plane_o] if first else [edge, plane_e, from_e, p, s]),
            fields + fields + [vmem(groups), vmem(groups), block] + ([vmem(4 * groups)] if first else []),
            [],
            "inner",
            2,
            {} if first else {22: 0, 23: 1},
        )
        if first:
            near = rest[0]
        next_e = to_core(send_e)
        from_e, from_o = next_e, next_o
        half_o, near_o = call_vmem(
            facing_kernel, [from_o, p, s, plane_o, near], [block, vmem(groups)], [], "facing", 0.5
        )
        send_o, mu, sums = call_vmem(
            lambda sz, *refs: outer_kernel(sz, final, *refs),
            [half_o, from_o, from_e, by_lane, near_o, sums, table, wp, ws, shared, near],
            [block, vmem(groups), pltpu.VMEM((devices, 1, LANES), F32) if final else vmem(groups)],
            [group_row],
            "outer",
            1,
            {1: 0},
        )
    grads = lax.all_to_all(sums, "gx", 0, 0)
    result = pltpu.HBM((rows, nz), F32)
    _, _, p, s = call_vmem(
        final_kernel,
        [p, s, mu, wp, ws, plane_e, send_o, from_e],
        fields + [result, result],
        [VMEM((2 * ny + SUB, LANES), F32), DMA((2,))],
        "final",
        2,
        {1: 0, 2: 1},
    )
    control = jnp.sum(grads, axis=(0, 1))[:groups]
    shape = trans_x.shape
    return p.reshape(shape), s.reshape(shape), control


def solution(mesh):
    grid = P(("ens", "gx"), None, None)
    line = P(("ens", "gx"))
    return jax.shard_map(
        body,
        mesh=mesh,
        in_specs=(grid,) * 10 + (line,) * 3 + (P("ens"), P("ens")),
        out_specs=(grid, grid, line),
        check_vma=False,
    )
```

```python
import functools

import jax
import jax.numpy as jnp
from jax import lax
from jax.experimental import pallas as pl
from jax.experimental.pallas import tpu as pltpu
from jax.sharding import PartitionSpec as P

SWEEPS = 6
SUB = 8
LANES = 128
F32 = jnp.float32
CHUNKS = 2


def vmem(rows):
    return pltpu.VMEM((rows, LANES), F32)


def placed(array, space):
    return array if space is pltpu.SMEM else pltpu.with_memory_space_constraint(array, space)


def spec(space):
    return pl.BlockSpec(memory_space=space)


def iota(shape, dim):
    return lax.broadcasted_iota(jnp.int32, shape, dim)


def lane_sum(block):
    return jnp.sum(block, axis=1, keepdims=True)


def spread(column, groups):
    return jnp.broadcast_to(column, (groups, LANES))


def row_of(column, groups):
    mine = iota((groups, LANES), 0) == iota((groups, LANES), 1)
    return jnp.sum(jnp.where(mine, column, 0.0), axis=0, keepdims=True)


def column_of(row, groups):
    mine = iota((groups, LANES), 0) == iota((groups, LANES), 1)
    return spread(lane_sum(jnp.where(mine, jnp.broadcast_to(row, (groups, LANES)), 0.0)), groups)


def well_block(part_own, part_before, groups):
    sub = iota((SUB, LANES), 0)
    own = jnp.broadcast_to(row_of(part_own, groups), (SUB, LANES))
    before = jnp.broadcast_to(row_of(part_before, groups), (SUB, LANES))
    return jnp.where(sub == 0, own, jnp.where(sub == 1, before, 0.0))


def group_rows(ref, groups, run):
    per_row = LANES // run
    return jnp.concatenate(
        [jnp.broadcast_to(ref[i : i + 1, :], (per_row, LANES)) for i in range(groups // per_row)], axis=0
    )


def first_kernel(
    sizes, tx_hbm, well_hbm, index_hbm, rhs_hbm, slot_hbm, send_ref, wells_ref, well_ref, index_ref, rhs_ref, slot_ref, sems
):
    ny, groups, run = sizes.ny, sizes.groups, sizes.run
    plane = pltpu.make_async_copy(
        tx_hbm.at[pl.ds((sizes.planes - 1) * ny, ny)], send_ref.at[pl.ds(0, ny)], sems.at[0]
    )
    get_well = pltpu.make_async_copy(well_hbm, well_ref, sems.at[1])
    get_index = pltpu.make_async_copy(index_hbm, index_ref, sems.at[2])
    get_rhs = pltpu.make_async_copy(rhs_hbm, rhs_ref, sems.at[3])
    get_slot = pltpu.make_async_copy(slot_hbm, slot_ref, sems.at[4])
    for copy in (get_well, get_index, plane, get_rhs, get_slot):
        copy.start()
    place = lax.axis_index("gx")
    shape = (groups, LANES)
    per_row = LANES // run
    local = iota(shape, 0) % per_row
    lane = iota(shape, 1)
    get_well.wait()
    get_index.wait()
    weights = jnp.where(lane // run == local, group_rows(index_ref, groups, run), 0.0)
    total = lane_sum(weights)
    first = jnp.where(lane == local * run, group_rows(well_ref, groups, run).astype(F32), 0.0)
    well = lane_sum(first)
    before = well < (place * groups).astype(F32)
    before = spread(jnp.where(before, 1.0, 0.0), groups)
    total = spread(total, groups)
    wells_ref[0:groups, :] = before
    wells_ref[groups : 2 * groups, :] = total
    send_ref[ny : ny + SUB, :] = well_block(total * (1.0 - before), total * before, groups)
    get_rhs.wait()
    get_slot.wait()
    behind = jnp.maximum(place - 1, 0)
    for i, (ref, whose) in enumerate(((rhs_ref, place), (rhs_ref, behind), (slot_ref, place), (slot_ref, behind))):
        wells_ref[(i + 2) * groups : (i + 3) * groups, :] = own_lanes(ref, whose, groups)
    plane.wait()


def split_cell(cell, ny):
    if ny & (ny - 1):
        row = lax.div(cell, LANES)
        return lax.div(row, ny), lax.rem(row, ny), lax.rem(cell, LANES)
    bits_z, bits_y = LANES.bit_length() - 1, ny.bit_length() - 1
    row = lax.shift_right_logical(cell, bits_z)
    return lax.shift_right_logical(row, bits_y), row & (ny - 1), cell & (LANES - 1)


def setup_kernel(
    sizes,
    cell_hbm,
    index_hbm,
    tx_hbm,
    ty_hbm,
    tz_hbm,
    accel_hbm,
    coupling_hbm,
    upwind_hbm,
    storage_hbm,
    rhs_p_hbm,
    rhs_s_hbm,
    cross_hbm,
    tx_ref,
    ty_ref,
    tyl_ref,
    tz_ref,
    tzl_ref,
    rp_ref,
    ip_ref,
    cc_ref,
    rs_ref,
    uu_ref,
    xx_ref,
    extra_ref,
    weight_ref,
    y_ref,
    raw_tx,
    raw_ty,
    raw_tz,
    raw_accel,
    raw_coupling,
    raw_upwind,
    raw_storage,
    raw_rhs_p,
    raw_rhs_s,
    raw_cross,
    cwi_ref,
    cell_ref,
    index_ref,
    sems,
    fetch_sems,
):
    ny, planes, groups, run = sizes.ny, sizes.planes, sizes.groups, sizes.run
    rows = planes * ny
    part = ny // CHUNKS
    moves = [
        (tx_hbm, raw_tx),
        (ty_hbm, raw_ty),
        (tz_hbm, raw_tz),
        (accel_hbm, raw_accel),
        (coupling_hbm, raw_coupling),
        (upwind_hbm, raw_upwind),
        (storage_hbm, raw_storage),
        (rhs_p_hbm, raw_rhs_p),
        (rhs_s_hbm, raw_rhs_s),
        (cross_hbm, raw_cross),
    ]

    def copies(c):
        found = []
        for i, (src, dst) in enumerate(moves):
            start = pl.multiple_of(c * part, SUB)
            to = pl.multiple_of(start + SUB, SUB) if dst is raw_ty else start
            found.append(
                pltpu.make_async_copy(src.at[:, pl.ds(start, part)], dst.at[:, pl.ds(to, part)], sems.at[c, i])
            )
        return found

    fetches = [
        pltpu.make_async_copy(src, dst, fetch_sems.at[i])
        for i, (src, dst) in enumerate(((cell_hbm, cell_ref), (index_hbm, index_ref)))
    ]
    for fetch in fetches:
        fetch.start()
    for c in range(CHUNKS):
        for copy in copies(c):
            copy.start()

    last = lax.axis_index("gx") == lax.axis_size("gx") - 1
    keep_last = jnp.where(last, 0.0, 1.0)
    zero = jnp.zeros((SUB, LANES), F32)

    @pl.loop(0, rows // SUB, unroll=8)
    def _(i):
        cwi_ref[pl.ds(pl.multiple_of(i * SUB, SUB), SUB), :] = zero

    for fetch in fetches:
        fetch.wait()
    spot = iota((SUB, LANES), 0) * LANES + iota((SUB, LANES), 1)
    for g in range(groups):
        _, y, _ = split_cell(cell_ref[g * run], ny)
        y_ref[g] = y
        weight = zero
        for k in range(g * run, (g + 1) * run):
            x, _, z = split_cell(cell_ref[k], ny)
            weight = weight + jnp.where(spot == x * LANES + z, index_ref[k], 0.0)
        weight_ref[g * SUB : (g + 1) * SUB, :] = weight
        slab = pl.ds(y, planes, ny)
        cwi_ref[slab, :] = cwi_ref[slab, :] + weight

    lane = iota((SUB, LANES), 1)
    sub = iota((SUB, LANES), 0)

    @pl.loop(0, CHUNKS)
    def _(c):
        for copy in copies(c):
            copy.wait()

        @pl.loop(0, part // SUB)
        def _(r):
            y0 = pl.multiple_of(c * part + r * SUB, SUB)
            ypos = sub + y0
            here = pl.ds(y0, SUB)
            txl = None
            for x in range(planes):
                at = pl.ds(y0 + x * ny, SUB)
                tx = raw_tx[x, here, :]
                if x == planes - 1:
                    tx = tx * keep_last
                tx_ref[at, :] = tx
                ty = jnp.where(ypos == ny - 1, 0.0, raw_ty[x, pl.ds(y0 + SUB, SUB), :])
                tyl = jnp.where(ypos == 0, 0.0, raw_ty[x, pl.ds(y0 + SUB - 1, SUB), :])
                tz = jnp.where(lane == LANES - 1, 0.0, raw_tz[x, here, :])
                tzl = pltpu.roll(tz, 1, 1)
                ty_ref[at, :] = ty
                tyl_ref[at, :] = tyl
                tz_ref[at, :] = tz
                tzl_ref[at, :] = tzl
                tsum = tx + ty + tyl + tz + tzl
                if x > 0:
                    tsum = tsum + txl
                accel = raw_accel[x, here, :]
                coupling = raw_coupling[x, here, :]
                upwind = raw_upwind[x, here, :]
                to_p = accel * (1.0 + jnp.abs(coupling))
                to_s = accel * jnp.abs(upwind)
                dp = to_p * tsum + accel * cwi_ref[at, :]
                ds = to_s * tsum + raw_storage[x, here, :]
                rhs_p, rhs_s, cross = raw_rhs_p[x, here, :], raw_rhs_s[x, here, :], raw_cross[x, here, :]
                if x == 0:
                    extra_ref[here, :] = to_p
                    extra_ref[pl.ds(y0 + ny, SUB), :] = to_s
                    extra_ref[pl.ds(y0 + 2 * ny, SUB), :] = ds
                    ip_ref[at, :] = dp
                    ip, is_ = 1.0, 1.0
                else:
                    ip = 1.0 / dp
                    is_ = 1.0 / ds
                    ip_ref[at, :] = ip
                cc_ref[at, :] = coupling * ip
                rp_ref[at, :] = rhs_p * ip
                rs_ref[at, :] = rhs_s * is_
                uu_ref[at, :] = upwind * is_
                xx_ref[at, :] = cross * is_
                txl = tx


def own_lanes(ref, place, groups):
    shape = (groups, LANES)
    start = place * groups
    row = jnp.broadcast_to(ref[pl.ds(start // LANES, 1), :].astype(F32), shape)
    mine = iota(shape, 1) == iota(shape, 0) + start % LANES
    return spread(lane_sum(jnp.where(mine, row, 0.0)), groups)


def clear_ends(rows, *refs):
    zero = jnp.zeros((SUB, LANES), F32)
    for ref in refs:
        ref[0:SUB, :] = zero
        ref[rows + SUB : rows + 2 * SUB, :] = zero


def path_y(sizes, cell_ref, g):
    return cell_ref[g]


def slab_of(sizes, cell_ref, g, pad):
    return pl.ds(path_y(sizes, cell_ref, g) + pad, sizes.planes, sizes.ny)


def add_wells(sizes, cell_ref, mu_ref, wp_ref, ws_ref, p_ref, s_ref, pad):
    for g in range(sizes.groups):
        slab = slab_of(sizes, cell_ref, g, pad)
        at = pl.ds(g * SUB, SUB)
        mu = mu_ref[g : g + 1, :]
        p_ref[slab, :] = p_ref[slab, :] + mu * wp_ref[at, :]
        s_ref[slab, :] = s_ref[slab, :] - mu * ws_ref[at, :]


def add_wells_to_plane(sizes, cell_ref, mu_ref, wp_ref, ws_ref, x, send_ref):
    for g in range(sizes.groups):
        y = path_y(sizes, cell_ref, g)
        in_p, in_s, at = pl.ds(y, 1), pl.ds(y + sizes.ny, 1), pl.ds(x + g * SUB, 1)
        mu = mu_ref[g : g + 1, :]
        send_ref[in_p, :] = send_ref[in_p, :] + mu * wp_ref[at, :]
        send_ref[in_s, :] = send_ref[in_s, :] - mu * ws_ref[at, :]


def path_rows(sizes, cell_ref, weight_ref, p_ref, rows_ref):
    for g in range(sizes.groups):
        slab = slab_of(sizes, cell_ref, g, SUB)
        at = pl.ds(g * SUB, SUB)
        rows_ref[g : g + 1, :] = jnp.sum(p_ref[slab, :] * weight_ref[at, :], axis=0, keepdims=True)


def facing(sizes, even):
    last = sizes.planes - 1
    return jnp.where(even, 0, last), jnp.where(even, last, 0)


def finish_plane(sizes, x, p_ref, s_ref, halo_ref, plane_ref, send_ref):
    ny = sizes.ny
    start = pl.multiple_of(x * ny + SUB, SUB)
    for r in range(0, ny, SUB):
        at = slice(r, r + SUB)
        at_s = slice(ny + r, ny + r + SUB)
        p, s = p_ref[pl.ds(start + r, SUB), :], s_ref[pl.ds(start + r, SUB), :]
        if halo_ref is not None:
            hp, hs = halo_ref[at, :], halo_ref[at_s, :]
            a, b, c, xx = [plane_ref[i * ny + r : i * ny + r + SUB, :] for i in range(4)]
            change = a * hp + b * hs
            p = p + change
            s = s + c * hs - xx * change
        send_ref[at, :] = p
        send_ref[at_s, :] = s


BEFORE, RHS_OWN, INV_OWN, SUM_OWN, RHS, INV, SLOT_OWN, SLOT_BEFORE, TABLE = range(9)


def shared_cells(sizes, cell_ref, weight_ref, wp_ref, out_ref):
    groups = sizes.groups
    shape = (groups, LANES)
    sub, lane = iota(shape, 0), iota(shape, 1)
    y_row = jnp.full(shape, -1, jnp.int32)
    y_col = y_row
    for g in range(groups):
        y = path_y(sizes, cell_ref, g)
        y_row = jnp.where(lane == g, y, y_row)
        y_col = jnp.where(sub == g, y, y_col)
    total = jnp.zeros(shape, F32)
    empty = jnp.zeros((LANES - groups, LANES), F32)
    for x in range(sizes.planes):
        at = pl.ds(x, groups, SUB)
        other = jnp.concatenate([wp_ref[at, :], empty], axis=0)
        total = total + lax.dot_general(
            weight_ref[at, :], other, (((1,), (1,)), ((), ())),
            precision=lax.Precision.HIGHEST, preferred_element_type=F32,
        )
    out_ref[...] = jnp.where(y_row == y_col, total, 0.0)


def start_kernel(
    sizes,
    cell_ref,
    from_o,
    from_e,
    wells_ref,
    tx_ref,
    rp_ref,
    ip_ref,
    cc_ref,
    rs_ref,
    uu_ref,
    xx_ref,
    extra_ref,
    weight_ref,
    edge_ref,
    plane_e,
    plane_o,
    wp_ref,
    ws_ref,
    shared_ref,
    table_ref,
    mu_ref,
    sums_out,
    send_o,
    rows_ref,
):
    ny, planes, groups = sizes.ny, sizes.planes, sizes.groups
    place = lax.axis_index("gx")
    even = place % 2 == 0
    x_o, _ = facing(sizes, even)

    @pl.loop(0, ny // SUB)
    def _(r):
        y0 = pl.multiple_of(r * SUB, SUB)
        at = pl.ds(y0, SUB)
        txl = jnp.where(even, from_o[at, :], from_e[at, :])
        ip = 1.0 / (ip_ref[at, :] + extra_ref[at, :] * txl)
        is_ = 1.0 / (extra_ref[pl.ds(y0 + 2 * ny, SUB), :] + extra_ref[pl.ds(y0 + ny, SUB), :] * txl)
        cc, uu = cc_ref[at, :] * ip, uu_ref[at, :] * is_
        rp, rs, xx = rp_ref[at, :] * ip, rs_ref[at, :] * is_, xx_ref[at, :] * is_
        for i, value in enumerate([ip, cc, rp, rs, uu, xx]):
            edge_ref[pl.ds(y0 + i * ny, SUB), :] = value
        end = pl.ds(y0 + (planes - 1) * ny, SUB)
        tx = tx_ref[end, :]
        low = [ip * txl, cc * txl, uu * txl, xx]
        high = [ip_ref[end, :] * tx, cc_ref[end, :] * tx, uu_ref[end, :] * tx, xx_ref[end, :]]
        for i in range(4):
            to = pl.ds(y0 + i * ny, SUB)
            plane_o[to, :] = jnp.where(even, low[i], high[i])
            plane_e[to, :] = jnp.where(even, high[i], low[i])
        rp_end = rp_ref[end, :]
        send_o[at, :] = jnp.where(even, rp, rp_end)
        send_o[pl.ds(y0 + ny, SUB), :] = jnp.where(
            even, rs - xx * rp, rs_ref[end, :] - xx_ref[end, :] * rp_end
        )

    sub = iota((SUB, LANES), 0)
    for g in range(groups):
        y = path_y(sizes, cell_ref, g)
        at = pl.ds(g * SUB, SUB)
        slab = pl.ds(y, planes, ny)
        ip = jnp.where(sub == 0, edge_ref[pl.ds(y, 1), :], ip_ref[slab, :])
        xx = jnp.where(sub == 0, edge_ref[pl.ds(y + 5 * ny, 1), :], xx_ref[slab, :])
        rp = jnp.where(sub == 0, edge_ref[pl.ds(y + 2 * ny, 1), :], rp_ref[slab, :])
        rows_ref[g : g + 1, :] = jnp.sum(weight_ref[at, :] * rp, axis=0, keepdims=True)
        wp = weight_ref[at, :] * ip
        wp_ref[at, :] = wp
        ws_ref[at, :] = wp * xx
    shared_cells(sizes, cell_ref, weight_ref, wp_ref, shared_ref)

    tile_e, tile_o = from_e[ny : ny + SUB, :], from_o[ny : ny + SUB, :]
    low = jnp.where(even, tile_o, tile_e)
    high = jnp.where(even, tile_e, tile_o)
    before = wells_ref[0:groups, :]
    mine = wells_ref[groups : 2 * groups, :]
    is_before = before > 0.5
    sum_own = mine * (1.0 - before) + column_of(high[1:2, :], groups)
    sum_before = mine * before + column_of(low[0:1, :], groups)
    rhs_own, rhs_before, slot_own, slot_before = [
        wells_ref[i * groups : (i + 1) * groups, :] for i in range(2, 6)
    ]
    inv_own = 1.0 / (1.5 * sum_own + 0.5)
    inv_before = 1.0 / (1.5 * sum_before + 0.5)
    rhs = jnp.where(is_before, rhs_before, rhs_own)
    inv = jnp.where(is_before, inv_before, inv_own)
    entries = {
        BEFORE: before,
        RHS_OWN: rhs_own,
        INV_OWN: inv_own,
        SUM_OWN: sum_own,
        RHS: rhs,
        INV: inv,
        SLOT_OWN: slot_own,
        SLOT_BEFORE: slot_before,
    }
    for i, entry in entries.items():
        table_ref[i * groups : (i + 1) * groups, :] = entry
    mu = rhs * inv
    mu_ref[...] = mu

    add_wells_to_plane(sizes, cell_ref, mu_ref, wp_ref, ws_ref, x_o, send_o)
    put_sums(sizes, even, before, rows_ref[...] + shared_ref[...] * row_of(mu, groups), sums_out, send_o)


def put_sums(sizes, to_before, before, by_lane, rows_out, send_ref):
    ny, groups = sizes.ny, sizes.groups
    rows_out[...] = by_lane
    shared = by_lane * jnp.where(to_before, before, 1.0 - before)
    parts = groups // SUB
    lane = iota((SUB, LANES), 1)
    tile = jnp.zeros((SUB, LANES), F32)
    for q in range(parts):
        part = shared[q * SUB : (q + 1) * SUB, :]
        width = LANES
        while width > LANES // parts:
            width //= 2
            part = part + pltpu.roll(part, width, 1)
        tile = jnp.where(lane // (LANES // parts) == q, part, tile)
    send_ref[2 * ny : 2 * ny + SUB, :] = tile


def rows_of(tile, groups):
    parts = groups // SUB
    lane = iota((SUB, LANES), 1)
    return jnp.concatenate(
        [jnp.where(lane // (LANES // parts) == q, tile, 0.0) for q in range(parts)], axis=0
    )


def finish_core_plane(sizes, cell_ref, p_ref, s_ref, mu_ref, wp_ref, ws_ref, halo, plane_e, send_e):
    even = lax.axis_index("gx") % 2 == 0
    _, x_e = facing(sizes, even)
    finish_plane(sizes, x_e, p_ref, s_ref, halo, plane_e, send_e)
    add_wells_to_plane(sizes, cell_ref, mu_ref, wp_ref, ws_ref, x_e, send_e)


def near_weights(sizes, cell_ref, weight_ref, plane_e, plane_o, near_ref):
    ny, groups = sizes.ny, sizes.groups
    even = lax.axis_index("gx") % 2 == 0
    x_o, x_e = facing(sizes, even)
    for g in range(groups):
        y = path_y(sizes, cell_ref, g)
        for i, (x, plane) in enumerate(((x_o, plane_o), (x_e, plane_e))):
            weight = weight_ref[pl.ds(x + g * SUB, 1), :]
            for j in range(2):
                to = (2 * i + j) * groups + g
                near_ref[to : to + 1, :] = weight * plane[pl.ds(y + j * ny, 1), :]


def put_planes(sizes, even, send_e, send_o, p_ref, s_ref, pad):
    ny = sizes.ny
    x_o, x_e = facing(sizes, even)
    for send, x in ((send_o, x_o), (send_e, x_e)):
        start = pl.multiple_of(x * ny + pad, SUB)
        for r in range(0, ny, SUB):
            p_ref[pl.ds(start + r, SUB), :] = send[r : r + SUB, :]
            s_ref[pl.ds(start + r, SUB), :] = send[ny + r : ny + r + SUB, :]


def inner_kernel(
    sizes,
    first,
    cell_ref,
    mu_ref,
    wp_ref,
    ws_ref,
    weight_ref,
    send_o,
    sums_in,
    table_ref,
    tx_ref,
    ty_ref,
    tyl_ref,
    tz_ref,
    tzl_ref,
    rp_ref,
    ip_ref,
    cc_ref,
    rs_ref,
    uu_ref,
    xx_ref,
    edge_ref,
    plane_e,
    *refs,
):
    ny, planes = sizes.ny, sizes.planes
    rows = planes * ny
    even = lax.axis_index("gx") % 2 == 0
    if first:
        plane_o, p_old, s_old, p_ref, s_ref, rows_ref, sums_out, send_e, near_ref = refs
        halo = None
        clear_ends(rows, p_old, s_old)

        @pl.loop(0, ny // SUB)
        def _(r):
            y0 = pl.multiple_of(r * SUB, SUB)
            for x in range(planes):
                at, to = pl.ds(y0 + x * ny, SUB), pl.ds(y0 + (x * ny + SUB), SUB)
                if x == 0:
                    rp, rs, xx = [edge_ref[pl.ds(y0 + i * ny, SUB), :] for i in (2, 3, 5)]
                else:
                    rp, rs, xx = rp_ref[at, :], rs_ref[at, :], xx_ref[at, :]
                p_old[to, :] = rp
                s_old[to, :] = rs - xx * rp

        near_weights(sizes, cell_ref, weight_ref, plane_e, plane_o, near_ref)
    else:
        halo, _, _, p_old, s_old, p_ref, s_ref, rows_ref, sums_out, send_e = refs
    finish_core_plane(sizes, cell_ref, p_old, s_old, mu_ref, wp_ref, ws_ref, halo, plane_e, send_e)
    before = table_ref[BEFORE * sizes.groups : (BEFORE + 1) * sizes.groups, :]
    put_sums(sizes, jnp.logical_not(even), before, sums_in[...], sums_out, send_e)
    add_wells(sizes, cell_ref, mu_ref, wp_ref, ws_ref, p_old, s_old, SUB)
    put_planes(sizes, even, send_e, send_o, p_old, s_old, SUB)

    @pl.loop(0, ny // SUB)
    def _(r):
        y0 = pl.multiple_of(r * SUB, SUB)
        here = [pl.ds(y0 + (x * ny + SUB), SUB) for x in range(planes)]
        ps = [p_old[at, :] for at in here]
        ss = [s_old[at, :] for at in here]
        tx = None
        for x in range(planes):
            at = pl.ds(y0 + x * ny, SUB)
            up = pl.ds(y0 + (x * ny + SUB + 1), SUB)
            down = pl.ds(y0 + (x * ny + SUB - 1), SUB)
            txl = tx
            tx = tx_ref[at, :] if x < planes - 1 else None
            ty, tyl, tz, tzl = ty_ref[at, :], tyl_ref[at, :], tz_ref[at, :], tzl_ref[at, :]

            def neighbours(fields, old):
                mid = fields[x]
                total = tz * pltpu.roll(mid, LANES - 1, 1) + tzl * pltpu.roll(mid, 1, 1)
                total = total + (ty * old[up, :] + tyl * old[down, :])
                if x < planes - 1:
                    total = total + tx * fields[x + 1]
                if x > 0:
                    total = total + txl * fields[x - 1]
                return total

            sum_p = neighbours(ps, p_old)
            sum_s = neighbours(ss, s_old)
            if x == 0:
                ip, cc, rp, rs, uu, xx = [edge_ref[pl.ds(y0 + i * ny, SUB), :] for i in range(6)]
            else:
                ip, cc, rp, rs, uu, xx = [ref[at, :] for ref in (ip_ref, cc_ref, rp_ref, rs_ref, uu_ref, xx_ref)]
            p = rp + ip * sum_p + cc * sum_s
            p_ref[here[x], :] = p
            s_ref[here[x], :] = rs + uu * sum_s - xx * p

    clear_ends(rows, p_ref, s_ref)
    path_rows(sizes, cell_ref, weight_ref, p_ref, rows_ref)


def facing_kernel(sizes, cell_ref, from_o, p_ref, s_ref, plane_o, near_ref, send_o, sums_ref):
    even = lax.axis_index("gx") % 2 == 0
    x_o, _ = facing(sizes, even)
    finish_plane(sizes, x_o, p_ref, s_ref, from_o, plane_o, send_o)
    near_sums(sizes, cell_ref, from_o, near_ref, 0, sums_ref)


def near_sums(sizes, cell_ref, halo, near_ref, side, sums_ref):
    groups = sizes.groups
    for g in range(groups):
        y = path_y(sizes, cell_ref, g)
        row = jnp.zeros((1, LANES), F32)
        for j in range(2):
            at = (2 * side + j) * groups + g
            row = row + near_ref[at : at + 1, :] * halo[pl.ds(y + j * sizes.ny, 1), :]
        sums_ref[g : g + 1, :] = row


def outer_kernel(
    sizes,
    final,
    cell_ref,
    send_in,
    from_o,
    from_e,
    rows_ref,
    near_o,
    sums_in,
    table_ref,
    wp_ref,
    ws_ref,
    shared_ref,
    near_ref,
    send_o,
    mu_ref,
    *rest,
):
    ny, groups = sizes.ny, sizes.groups
    near_e = rest[-1]
    even = lax.axis_index("gx") % 2 == 0
    x_o, _ = facing(sizes, even)

    def table(i):
        return table_ref[i * groups : (i + 1) * groups, :]

    tail = slice(2 * ny, 2 * ny + SUB)
    come_e, come_o = from_e[tail, :], from_o[tail, :]
    low = rows_of(jnp.where(even, come_o, come_e), groups)
    high = rows_of(jnp.where(even, come_e, come_o), groups)
    before = table(BEFORE)
    total = spread(lane_sum(sums_in[...] + jnp.where(before > 0.5, low, high)), groups)
    mu = (table(RHS) + total) * table(INV)
    mu_ref[...] = mu
    near_sums(sizes, cell_ref, from_e, near_ref, 1, near_e)
    by_lane = rows_ref[...] + near_o[...] + near_e[...] + shared_ref[...] * row_of(mu, groups)
    add_wells_to_plane(sizes, cell_ref, mu_ref, wp_ref, ws_ref, x_o, send_o)
    if not final:
        put_sums(sizes, even, before, by_lane, rest[0], send_o)
        return
    total_own = spread(lane_sum(sums_in[...] * (1.0 - before) + high), groups)
    total = spread(lane_sum(by_lane), groups)
    part_own, part_before = total * (1.0 - before), total * before
    grads_ref = rest[0]
    mu_own = (table(RHS_OWN) + total_own) * table(INV_OWN)
    grad_own = mu_own * table(SUM_OWN) - part_own
    grad_before = -part_before
    lane = iota((SUB, LANES), 1).astype(F32)
    outside = lane >= groups
    values = []
    for slots, grad in ((table(SLOT_OWN), grad_own), (table(SLOT_BEFORE), grad_before)):
        for q in range(groups // SUB):
            part = slice(q * SUB, (q + 1) * SUB)
            values.append((jnp.where(outside, -1.0, slots[part, :] - lane), grad[part, :]))
    for d in range(sizes.devices):
        total = jnp.zeros((SUB, LANES), F32)
        for slot, grad in values:
            total = total + jnp.where(slot == float(d * groups), grad, 0.0)
        grads_ref[d] = jnp.sum(total, axis=0, keepdims=True)


def final_kernel(
    sizes,
    cell_ref,
    p_in,
    s_in,
    mu_ref,
    wp_ref,
    ws_ref,
    plane_e,
    send_o,
    from_e,
    p_old,
    s_old,
    p_out,
    s_out,
    send_e,
    sems,
):
    rows = sizes.planes * sizes.ny
    even = lax.axis_index("gx") % 2 == 0
    finish_core_plane(sizes, cell_ref, p_old, s_old, mu_ref, wp_ref, ws_ref, from_e, plane_e, send_e)
    add_wells(sizes, cell_ref, mu_ref, wp_ref, ws_ref, p_old, s_old, SUB)
    put_planes(sizes, even, send_e, send_o, p_old, s_old, SUB)
    copies = [
        pltpu.make_async_copy(field.at[pl.ds(SUB, rows)], out, sems.at[i])
        for i, (field, out) in enumerate(((p_old, p_out), (s_old, s_out)))
    ]
    for copy in copies:
        copy.start()
    for copy in copies:
        copy.wait()


class Sizes:
    def __init__(self, planes, ny, groups, run, devices):
        self.planes, self.ny, self.groups, self.run, self.devices = planes, ny, groups, run, devices


def body(
    rhs_pressure,
    rhs_saturation,
    trans_x,
    trans_y,
    trans_z,
    coupling,
    upwind,
    storage,
    cross,
    accel,
    perf_cell,
    perf_well,
    perf_index,
    well_rhs,
    well_slot,
):
    planes, ny, nz = trans_x.shape
    devices = lax.axis_size("gx")
    groups = well_rhs.shape[0] // devices
    run = perf_cell.shape[0] // groups
    sizes = Sizes(planes, ny, groups, run, devices)
    rows = planes * ny
    padded = rows + 2 * SUB
    SMEM, VMEM, HBM, DMA = pltpu.SMEM, pltpu.VMEM, pltpu.HBM, pltpu.SemaphoreType.DMA

    def flat(array):
        return array.reshape(rows, nz)

    def lines(array):
        return array.reshape(-1, LANES)

    def call(kernel, args, spaces, outs, scratch, name, micros, aliases=None):
        return pl.pallas_call(
            kernel,
            in_specs=[spec(space) for space in spaces],
            out_specs=[spec(out.memory_space) for out in outs],
            out_shape=outs,
            scratch_shapes=scratch,
            input_output_aliases=aliases or {},
            compiler_params=pltpu.CompilerParams(vmem_limit_bytes=16 * 1024 * 1024),
            cost_estimate=pl.CostEstimate(flops=int(micros * 4e6), bytes_accessed=int(micros * 3e6), transcendentals=0),
            name=name,
        )(*[placed(a, space) for a, space in zip(args, spaces)])

    def call_vmem(kernel, args, outs, scratch, name, micros, aliases=None):
        return call(
            functools.partial(kernel, sizes), [y] + args, [SMEM] + [VMEM] * len(args), outs, scratch,
            name, micros, aliases,
        )

    pairs_e = [(i, i ^ 1) for i in range(devices) if i ^ 1 < devices]
    pairs_o = []
    for i in range(1, devices - 1, 2):
        pairs_o += [(i, i + 1), (i + 1, i)]

    def to_core(block):
        return lax.ppermute(block, "gx", pairs_e)

    def to_chip(block):
        return lax.ppermute(block, "gx", pairs_o)

    index = lines(perf_index)
    send, wells = call(
        functools.partial(first_kernel, sizes),
        [flat(trans_x), lines(perf_well), index, lines(well_rhs), lines(well_slot)],
        [HBM] * 5,
        [vmem(ny + SUB), vmem(6 * groups)],
        [
            VMEM(index.shape, jnp.int32),
            VMEM(index.shape, F32),
            VMEM(lines(well_rhs).shape, F32),
            VMEM(lines(well_slot).shape, jnp.int32),
            DMA((5,)),
        ],
        "first",
        1,
    )
    from_o = to_chip(send)
    from_e = to_core(send)
    big = [trans_x, trans_y, trans_z, accel, coupling, upwind, storage, rhs_pressure, rhs_saturation, cross]
    made = call(
        functools.partial(setup_kernel, sizes),
        [perf_cell, perf_index] + big,
        [HBM] * (2 + len(big)),
        [vmem(rows)] * 11 + [vmem(3 * ny), vmem(groups * SUB), SMEM((groups,), jnp.int32)],
        [
            VMEM((planes, ny, LANES), F32),
            VMEM((planes, ny + SUB, LANES), F32),
        ]
        + [VMEM((planes, ny, LANES), F32)] * 8
        + [
            VMEM((rows, LANES), F32),
            SMEM(perf_cell.shape, jnp.int32),
            SMEM(perf_index.shape, F32),
            DMA((CHUNKS, 10)),
            DMA((2,)),
        ],
        "setup",
        4,
    )
    coefficients, (extra, weight, y) = list(made[:11]), made[11:]
    group_row = VMEM((groups, LANES), F32)
    fields = [vmem(padded), vmem(padded)]
    block = vmem(2 * ny + SUB)
    slabs = vmem(groups * SUB)
    edge, plane_e, plane_o, wp, ws, shared, table, mu, sums, send_o = call(
        functools.partial(start_kernel, sizes),
        [y, from_o, from_e, wells, coefficients[0]] + coefficients[5:] + [extra, weight],
        [SMEM] + [VMEM] * 12,
        [vmem(6 * ny), vmem(4 * ny), vmem(4 * ny), slabs, slabs, vmem(groups), vmem(TABLE * groups)]
        + [vmem(groups), vmem(groups), block],
        [group_row],
        "start",
        2,
    )
    near = None
    for sweep in range(1, SWEEPS):
        final = sweep == SWEEPS - 1
        next_o = to_chip(send_o)
        first = sweep == 1
        _, _, p, s, by_lane, sums, send_e, *rest = call_vmem(
            lambda sz, *refs: inner_kernel(sz, first, *refs),
            [mu, wp, ws, weight, send_o, sums, table]
            + coefficients
            + ([edge, plane_e, plane_o] if first else [edge, plane_e, from_e, p, s]),
            fields + fields + [vmem(groups), vmem(groups), block] + ([vmem(4 * groups)] if first else []),
            [],
            "inner",
            2,
            {} if first else {22: 0, 23: 1},
        )
        if first:
            near = rest[0]
        next_e = to_core(send_e)
        from_e, from_o = next_e, next_o
        half_o, near_o = call_vmem(
            facing_kernel, [from_o, p, s, plane_o, near], [block, vmem(groups)], [], "facing", 0.5
        )
        send_o, mu, sums = call_vmem(
            lambda sz, *refs: outer_kernel(sz, final, *refs),
            [half_o, from_o, from_e, by_lane, near_o, sums, table, wp, ws, shared, near],
            [block, vmem(groups), pltpu.VMEM((devices, 1, LANES), F32) if final else vmem(groups)],
            [group_row],
            "outer",
            1,
            {1: 0},
        )
    grads = lax.all_to_all(sums, "gx", 0, 0)
    result = pltpu.HBM((rows, nz), F32)
    _, _, p, s = call_vmem(
        final_kernel,
        [p, s, mu, wp, ws, plane_e, send_o, from_e],
        fields + [result, result],
        [VMEM((2 * ny + SUB, LANES), F32), DMA((2,))],
        "final",
        2,
        {1: 0, 2: 1},
    )
    control = jnp.sum(grads, axis=(0, 1))[:groups]
    shape = trans_x.shape
    return p.reshape(shape), s.reshape(shape), control


def solution(mesh):
    grid = P(("ens", "gx"), None, None)
    line = P(("ens", "gx"))
    return jax.shard_map(
        body,
        mesh=mesh,
        in_specs=(grid,) * 10 + (line,) * 3 + (P("ens"), P("ens")),
        out_specs=(grid, grid, line),
        check_vma=False,
    )
```
